32 devices in a mesh: dp: 8 (over y, x, core), expert: 4 (over z).
Axes of the slice: x: 2, y: 2, z: 4, core: 2. Of those that a mesh axis runs over, the one named last changes fastest.
Arguments:
- frames: bfloat16 [16384, 512], P(('dp', 'expert')), may hold values from -8 to 8
- lengths: int32 [32, 4], replicated, may hold values from 1 to 380, as said below
- choice_first: int32 [16384, 1], P(('dp', 'expert')), may hold values from 0 to 3; in each aligned block of 512 rows (0 to 511, 512 to 1023, ...) at most 256 rows name the same one
- choice_second: int32 [16384, 1], P(('dp', 'expert')), may hold values from 0 to 3; in each aligned block of 512 rows (0 to 511, 512 to 1023, ...) at most 256 rows name the same one
- embed_weight: bfloat16 [512, 512], replicated, may hold values from -0.25 to 0.25
- routers: bfloat16 [2, 512, 4], P(None, ('dp', 'expert')), may hold values from -0.25 to 0.25
- norm_gains: bfloat16 [6, 512], P(None, ('dp', 'expert')), may hold values from 0.25 to 1.75
- attn_in: bfloat16 [512, 1536], P(('dp', 'expert')), may hold values from -0.25 to 0.25
- attn_out: bfloat16 [512, 512], P(('dp', 'expert')), may hold values from -1 to 1
- conv_in: bfloat16 [512, 1024], P(('dp', 'expert')), may hold values from -0.25 to 0.25
- conv_kernel: bfloat16 [15, 512], P(None, ('dp', 'expert')), may hold values from -1.5 to 1.5
- bn_shift: bfloat16 [512], P(('dp', 'expert')), may hold values from -3 to 3
- conv_out: bfloat16 [512, 512], P(('dp', 'expert')), may hold values from -0.375 to 0.375
- expert_in: bfloat16 [2, 4, 512, 2048], P(None, 'expert', 'dp'), may hold values from -0.25 to 0.25
- expert_out: bfloat16 [2, 4, 2048, 512], P(None, 'expert', 'dp'), may hold values from -2 to 2
- cotangent: bfloat16 [16384, 512], P(('dp', 'expert')), may hold values from -6 to 6
Outputs:
- block_out: bfloat16 [16384, 512], P(('dp', 'expert'))
- frames_grad: float32 [16384, 512], P(('dp', 'expert'))
- embed_grad: float32 [512, 512], replicated
- routers_grad: float32 [2, 512, 4], P(None, ('dp', 'expert'))
- norm_gains_grad: float32 [6, 512], P(None, ('dp', 'expert'))
- attn_in_grad: float32 [512, 1536], P(('dp', 'expert'))
- attn_out_grad: float32 [512, 512], P(('dp', 'expert'))
- conv_in_grad: float32 [512, 1024], P(('dp', 'expert'))
- conv_kernel_grad: float32 [15, 512], P(None, ('dp', 'expert'))
- bn_shift_grad: float32 [512], P(('dp', 'expert'))
- conv_out_grad: float32 [512, 512], P(('dp', 'expert'))
- expert_in_grad: float32 [2, 4, 512, 2048], P(None, 'expert', 'dp')
- expert_out_grad: float32 [2, 4, 2048, 512], P(None, 'expert', 'dp')
The draws below stay inside these ranges and needn't reach their ends.
Inputs may be any that keep to these rules, and one draw needn't show every extreme that they name: `lengths`: A row lists, in order, the frame counts of the 4 segments of one device's 512 frames and sums to 512; the last segment is padding of at most 32 frames, the others hold 50 frames or more, and each row's largest entry is 380. `choice_first`: among the frames of one device no expert is chosen more than 256 times, and in every draw some expert is chosen exactly 256 times by the frames of some device. `choice_second`: among the frames of one device no expert is chosen more than 256 times, and in every draw some expert is chosen exactly 256 times by the frames of some device.
All inputs are finite; a program needn't handle non-finite values.
Results may differ from the reference program's by a relative error of at most 0.018.
Values may be sent and summed in bfloat16 or wider, within the bound.
No kernel may reach another device: no remote copies, remote signals or barrier semaphores. Data moves between devices by JAX's collectives and lax.ppermute only.
A program may use at most 192 MiB of HBM per device.

```python
import math
import jax
import jax.numpy as jnp
import numpy as np
from jax import lax

D = 512
H = 8
DH = 64
FF = 2048
K = 15
E = 4
TOK_DEV = 512
UTT = 4
MINLEN = 50
PADMAX = 32
MAXLEN = 380
CAP = 256
SHARDS = 32
TOKENS = 16384


def draw_frames(key, part):
    key = jax.random.fold_in(key, 11)
    noise_key, offset_key = jax.random.split(key, 2)
    ramp = 0.35 + 0.7 * jnp.arange(SHARDS, dtype=jnp.float32) / max(SHARDS - 1, 1)
    noise = jax.random.normal(noise_key, (SHARDS, TOK_DEV, D), jnp.float32)
    offsets = jax.random.normal(offset_key, (SHARDS, 1, D), jnp.float32) * ramp[:, None, None]
    values = jnp.clip(noise + offsets, -8.0, 8.0)
    return values.reshape(SHARDS * TOK_DEV, D).astype(jnp.bfloat16)


def draw_lengths(key, part):
    key = jax.random.fold_in(key, 23)
    pad_key, split_key, order_key, pick_key = jax.random.split(key, 4)
    row_ids = jnp.arange(SHARDS, dtype=jnp.int32)
    picked = jax.random.randint(pick_key, (), 0, SHARDS, dtype=jnp.int32)
    padding = jax.random.randint(pad_key, (SHARDS,), 1, PADMAX + 1, dtype=jnp.int32)
    padding = jnp.where(row_ids == picked, PADMAX, padding).astype(jnp.int32)
    remainder = TOK_DEV - MAXLEN - padding
    lower = jnp.maximum(MINLEN, remainder - MAXLEN).astype(jnp.int32)
    upper = jnp.minimum(MAXLEN, remainder - MINLEN).astype(jnp.int32)
    middle = jax.random.randint(split_key, (SHARDS,), lower, upper + 1, dtype=jnp.int32)
    middle = jnp.where(row_ids == picked, lower, middle).astype(jnp.int32)
    real_parts = jnp.stack([jnp.full((SHARDS,), MAXLEN, jnp.int32), middle, remainder - middle], 1)
    orders = jax.vmap(lambda row_key: jax.random.permutation(row_key, 3))(jax.random.split(order_key, SHARDS))
    shuffled = jnp.take_along_axis(real_parts, orders.astype(jnp.int32), 1)
    return jnp.concatenate([shuffled, padding[:, None]], 1).astype(jnp.int32)


def steps_of(rng, shape, shards, least, high):
    loudness = 1.0
    for position, shards_of in shards:
        draws = jax.random.uniform(jax.random.fold_in(jax.random.fold_in(rng, 6), position), (shards_of,), jnp.float32, least / len(shards), high / len(shards))
        loudness = loudness * jnp.repeat(jnp.exp(draws), shape[position] // shards_of).reshape((-1,) + (1,) * (len(shape) - 1 - position))
    return loudness


def shared_out(key, own, number, rows, count, top, most, lean):
    sequence = jax.random.permutation(key, count)
    crowded, ordinary = portions_of(count, rows * top, most, lean, True), portions_of(count, rows * top, most, lean, False)
    places = jnp.arange(count)

    def named(sizes, turn):
        used = int((sizes > 0).sum())
        fixed = max(1, used // 4)
        passed = fixed + (places - fixed + turn * (used - fixed)) % max(1, count - fixed)
        return jnp.zeros((count,), jnp.int32).at[sequence[jnp.where(places < fixed, places, passed)]].set(jnp.asarray(sizes, jnp.int32))

    sizes = jnp.where(number % 4 == 0, named(crowded, number // 4), named(ordinary, number - number // 4 - 1))
    mixed = jax.random.permutation(jax.random.fold_in(own, 3), count)
    source_of, sink = mixed[0:count // 2 * 2:2], mixed[1:count // 2 * 2:2]
    slack = jnp.minimum(sizes[source_of] - 1, most - sizes[sink]) // 2
    slack = jnp.where((source_of == sequence[0]) | (sink == sequence[0]) | (sizes[sink] == 0), 0, jnp.maximum(slack, 0))
    passed = jax.random.randint(jax.random.fold_in(own, 4), (count // 2,), 0, 1 << 20) % (slack + 1)
    sizes = sizes.at[source_of].add(-passed).at[sink].add(passed)
    items = jnp.searchsorted(jnp.cumsum(sizes), jnp.arange(rows * top), side="right").astype(jnp.int32)
    table = items.reshape(top, rows).T
    table = table[jax.random.permutation(jax.random.fold_in(own, 1), rows)]
    turn = jax.random.randint(jax.random.fold_in(own, 2), (rows, 1), 0, top)
    return jnp.take_along_axis(table, (jnp.arange(top)[None, :] + turn) % top, axis=1)


def portions_of(count, total, bound, slope, full):
    portions = [(1 << 20) // math.isqrt(standing ** slope) + 1 for standing in range(1, count + 1)]
    largest = bound if full else min(bound, max(-(-total // count), total * portions[0] // sum(portions)))
    least = 1 if total - largest >= count - 1 else 0
    counts, rest = [largest] + [least] * (count - 1), total - largest - least * (count - 1)
    while rest > 0:
        movable = [i for i in range(1, count) if counts[i] < largest] or [i for i in range(1, count) if counts[i] < bound]
        pool, left = sum([portions[i] for i in movable]), rest
        for i in movable:
            extra = min(bound - counts[i], max(1, left * portions[i] // pool), rest)
            counts[i] = counts[i] + extra
            rest = rest - extra
    return np.array(counts)


def gaussian(own_key, extent, deviation, reach, pieces=(), held_as=jnp.bfloat16):
    factor_of = steps_of(own_key, extent, pieces, -0.22, 0.18) if pieces else 1.0
    entries = jax.random.normal(own_key, extent, jnp.float32) * deviation * factor_of
    return jnp.minimum(jnp.maximum(entries, -reach), reach).astype(held_as)


def setup_inputs(seed: int = 0) -> dict:
    keys = jax.random.split(jax.random.key(seed), 17)
    frames = draw_frames(jax.random.fold_in(keys[16], 71), 0)
    lengths = draw_lengths(jax.random.fold_in(keys[16], 71), 0)
    choice_first_keys = jax.random.split(jax.random.fold_in(keys[2], 1), TOKENS // TOK_DEV)
    choice_first_turns = jax.random.permutation(jax.random.fold_in(keys[2], 3), TOKENS // TOK_DEV)
    choice_first = jax.vmap(lambda own, number: shared_out(jax.random.fold_in(keys[2], 2), own, number, TOK_DEV, E, 1, CAP, 2))(choice_first_keys, choice_first_turns).reshape((TOKENS, 1))
    choice_second_keys = jax.random.split(jax.random.fold_in(keys[3], 1), TOKENS // TOK_DEV)
    choice_second_turns = jax.random.permutation(jax.random.fold_in(keys[3], 3), TOKENS // TOK_DEV)
    choice_second = jax.vmap(lambda own, number: shared_out(jax.random.fold_in(keys[3], 2), own, number, TOK_DEV, E, 1, CAP, 2))(choice_second_keys, choice_second_turns).reshape((TOKENS, 1))
    embed_weight = gaussian(keys[4], (D, D), D ** -0.5, 0.25)
    routers = gaussian(keys[5], (2, D, E), D ** -0.5, 0.25, ((1, 32),))
    norm_gains = jnp.clip(1.0 + 0.15 * jax.random.normal(keys[6], (6, D), jnp.float32), 0.25, 1.75).astype(jnp.bfloat16)
    attn_in = gaussian(keys[7], (D, 3 * D), D ** -0.5, 0.25, ((0, 32),))
    attn_out = gaussian(keys[8], (D, D), (D // 16) ** -0.5, 1.0, ((0, 32),))
    conv_in = gaussian(keys[9], (D, 2 * D), D ** -0.5, 0.25, ((0, 32),))
    conv_kernel = gaussian(keys[10], (K, D), K ** -0.5, 1.5, ((1, 32),))
    bn_shift = gaussian(keys[11], (D,), 0.5, 3.0, ((0, 32),))
    conv_out = gaussian(keys[12], (D, D), (D // 2) ** -0.5, 0.375, ((0, 32),))
    expert_in = gaussian(keys[13], (2, E, D, FF), D ** -0.5, 0.25, ((1, 4), (2, 8)))
    expert_out = gaussian(keys[14], (2, E, FF, D), (FF // 256) ** -0.5, 2.0, ((1, 4), (2, 8)))
    cotangent = gaussian(keys[15], (TOKENS, D), 1.0, 6.0, ((0, 32),))
    return dict(frames=frames, lengths=lengths, choice_first=choice_first, choice_second=choice_second, embed_weight=embed_weight, routers=routers, norm_gains=norm_gains, attn_in=attn_in, attn_out=attn_out, conv_in=conv_in, conv_kernel=conv_kernel, bn_shift=bn_shift, conv_out=conv_out, expert_in=expert_in, expert_out=expert_out, cotangent=cotangent)


EPSILON = 1e-05
MASK_FILL = 1000000000.0
HIGHEST = lax.Precision.HIGHEST

@jax.custom_vjp
def low(v):
    return lax.optimization_barrier(v.astype(jnp.bfloat16)).astype(jnp.float32)

@jax.custom_vjp
def low_back(v):
    return v

def low_keep(v):
    return (low(v), None)

def low_pass(kept, grad):
    return (grad,)

def back_keep(v):
    return (v, None)

def back_low(kept, grad):
    return (low(grad),)
low.defvjp(low_keep, low_pass)
low_back.defvjp(back_keep, back_low)

def product(left, right):
    return jnp.dot(left, right, precision=HIGHEST)

def layer_norm(rows_in, gain_row):
    centred = rows_in - lax.optimization_barrier(jnp.mean(rows_in, -1, keepdims=True))
    return centred * lax.rsqrt(lax.optimization_barrier(jnp.mean(centred * centred, -1, keepdims=True)) + EPSILON) * gain_row

def segments(lengths_row):
    seg_ends = jnp.cumsum(lengths_row, dtype=jnp.int32)
    seg_starts = seg_ends - lengths_row
    positions = jnp.arange(TOK_DEV, dtype=jnp.int32)
    segment = lax.optimization_barrier(jnp.sum((positions[:, None] >= seg_ends[None, :]).astype(jnp.int32), 1))
    member = segment[:, None] == jnp.arange(UTT, dtype=jnp.int32)[None, :]
    offsets = positions - lax.optimization_barrier(jnp.sum(jnp.where(member, seg_starts[None, :], 0), 1))
    validity = (segment < UTT - 1).astype(jnp.float32)
    return (segment, offsets, validity)

def rotation(offsets):
    half_dim = DH // 2
    frequency = 10000.0 ** (-jnp.arange(half_dim, dtype=jnp.float32) / half_dim)
    angles = offsets.astype(jnp.float32)[:, None] * frequency[None, :]
    return (jnp.cos(angles)[:, None, :], jnp.sin(angles)[:, None, :])

def rotate(values, cosine, sine_table):
    half_dim = values.shape[-1] // 2
    first_half = values[..., :half_dim]
    second_half = values[..., half_dim:]
    return jnp.concatenate([first_half * cosine - second_half * sine_table, first_half * sine_table + second_half * cosine], -1)

def depthwise(values, kernel, segment):
    reach_half = K // 2
    padded = jnp.pad(values, ((reach_half, reach_half), (0, 0)))
    seg_padded = jnp.pad(segment, (reach_half, reach_half), constant_values=-1)
    result = jnp.zeros(values.shape, jnp.float32)
    for tap_index in range(K):
        same_segment = (seg_padded[tap_index:tap_index + TOK_DEV] == segment).astype(jnp.float32)[:, None]
        result = result + kernel[tap_index] * padded[tap_index:tap_index + TOK_DEV] * same_segment
    return result

def gate_of(embedded, router, chosen):
    router_probs = jax.nn.softmax(product(embedded, router), -1)
    onehot = (chosen[:, None] == jnp.arange(E, dtype=jnp.int32)[None, :]).astype(jnp.float32)
    return lax.optimization_barrier(jnp.sum(router_probs * onehot, -1))

def expert_layer(rows_in, chosen, input_weight, output_weight):
    onehot = (chosen[:, None] == jnp.arange(E, dtype=jnp.int32)[None, :]).astype(jnp.int32)
    rank_within = lax.optimization_barrier(jnp.sum((jnp.cumsum(onehot, 0, dtype=jnp.int32) - onehot) * onehot, 1))
    slot_index = chosen * CAP + rank_within
    buffer = jnp.zeros((E * CAP, D), rows_in.dtype).at[slot_index].set(rows_in).reshape(E, CAP, D)
    preactivation = low_back(jnp.einsum('ecd,edf->ecf', buffer, input_weight, precision=HIGHEST))
    hidden = low(jax.nn.silu(preactivation))
    produced = low_back(low(jnp.einsum('ecf,efd->ecd', hidden, output_weight, precision=HIGHEST)))
    return produced.reshape(E * CAP, D)[slot_index]

def attention(normed_low, attn_in_matrix, attn_out_matrix, segment, offsets):
    projected = low_back(product(normed_low, attn_in_matrix))
    cosine, sine_table = rotation(offsets)
    query_rows = low(rotate(projected[:, :D].reshape(TOK_DEV, H, DH), cosine, sine_table))
    key_rows = low(rotate(projected[:, D:2 * D].reshape(TOK_DEV, H, DH), cosine, sine_table))
    value_rows = low(projected[:, 2 * D:].reshape(TOK_DEV, H, DH))
    block_rows = min(512, TOK_DEV)

    def one_block(inputs):
        query_block, segment_block = inputs
        scores = low_back(jnp.einsum('bhd,thd->hbt', query_block, key_rows, precision=HIGHEST) * DH ** (-0.5))
        allowed = (segment_block[:, None] == segment[None, :])[None]
        probabilities = low(jax.nn.softmax(jnp.where(allowed, scores, -MASK_FILL), -1))
        return jnp.einsum('hbt,thd->bhd', probabilities, value_rows, precision=HIGHEST)
    attended = lax.map(jax.checkpoint(one_block), (query_rows.reshape(-1, block_rows, H, DH), segment.reshape(-1, block_rows)))
    attended = low_back(low(attended.reshape(TOK_DEV, D)))
    return low_back(product(attended, attn_out_matrix))

def conv_front(normed_low, conv_in_matrix, kernel, segment):
    gates_in = low_back(product(normed_low, conv_in_matrix))
    glu_out = gates_in[:, :D] * jax.nn.sigmoid(gates_in[:, D:])
    return depthwise(glu_out, kernel, segment)

def reference(frames, lengths, choice_first, choice_second, embed_weight, routers, norm_gains, attn_in, attn_out, conv_in, conv_kernel, bn_shift, conv_out, expert_in, expert_out, cotangent):
    first_choices = choice_first[:, 0].reshape(SHARDS, TOK_DEV)
    second_choices = choice_second[:, 0].reshape(SHARDS, TOK_DEV)

    def forward(input_rows, embed_matrix, router_pair, gain_table, attn_in_matrix, attn_out_matrix, conv_in_matrix, kernel_table, shift_vector, conv_out_matrix, experts_in, experts_out):

        def front_part(shard_data):
            shard_rows, lengths_row, first_choice, second_choice = shard_data
            segment, offsets, validity = segments(lengths_row)
            embedded = jax.nn.silu(low_back(product(shard_rows, embed_matrix)))
            gate_first = gate_of(embedded, router_pair[0], first_choice)
            gate_second = gate_of(embedded, router_pair[1], second_choice)
            expert_input = low_back(low(layer_norm(shard_rows, gain_table[0])))
            after_first = shard_rows + 0.5 * gate_first[:, None] * expert_layer(expert_input, first_choice, experts_in[0], experts_out[0])
            attention_input = low(layer_norm(after_first, gain_table[1]))
            after_attention = after_first + attention(attention_input, attn_in_matrix, attn_out_matrix, segment, offsets)
            conv_input = low(layer_norm(after_attention, gain_table[2]))
            conv_depth = conv_front(conv_input, conv_in_matrix, kernel_table, segment)
            return (after_attention, conv_depth, gate_second, validity)
        after_attention, conv_depth, gate_second, validity = lax.map(jax.checkpoint(front_part), (input_rows.reshape(SHARDS, TOK_DEV, D), lengths, first_choices, second_choices))
        weighted = validity[..., None] * conv_depth
        frame_count = jnp.sum(validity)
        batch_mean = lax.optimization_barrier(jnp.sum(weighted, (0, 1))) / frame_count
        batch_var = lax.optimization_barrier(jnp.sum(weighted * conv_depth, (0, 1))) / frame_count - batch_mean * batch_mean
        batch_inverse = lax.rsqrt(batch_var + EPSILON)

        def rear_part(shard_data):
            attention_rows, depth_rows, gate_rows, validity_rows, second_choice = shard_data
            normalized = (depth_rows - batch_mean) * batch_inverse * gain_table[5] + shift_vector
            conv_rows = low_back(product(low(jax.nn.silu(normalized)), conv_out_matrix))
            after_conv = attention_rows + conv_rows
            expert_input = low_back(low(layer_norm(after_conv, gain_table[3])))
            after_second = after_conv + 0.5 * gate_rows[:, None] * expert_layer(expert_input, second_choice, experts_in[1], experts_out[1])
            return layer_norm(after_second, gain_table[4]) * validity_rows[:, None]
        result = lax.map(jax.checkpoint(rear_part), (after_attention, conv_depth, gate_second, validity, second_choices))
        return result.reshape(TOKENS, D)
    params = tuple((argument.astype(jnp.float32) for argument in (frames, embed_weight, routers, norm_gains, attn_in, attn_out, conv_in, conv_kernel, bn_shift, conv_out, expert_in, expert_out)))
    outputs, pullback = jax.vjp(forward, *params)
    gradients = pullback(cotangent.astype(jnp.float32))
    return (outputs.astype(jnp.bfloat16), gradients[0], gradients[1], gradients[2], gradients[3], gradients[4], gradients[5], gradients[6], gradients[7], gradients[8], gradients[9], gradients[10], gradients[11])
```

```python
import jax
import jax.numpy as jnp
from jax import lax
from jax.sharding import PartitionSpec as P

H = 8
DH = 64


EPSILON = 1e-05
MASK_FILL = 1000000000.0
HIGHEST = lax.Precision.HIGHEST


AXES = ("dp", "expert")


def position(axes):
    return lax.axis_index(axes)


def bit_count(axes):
    total = 1
    for name in axes:
        total *= lax.axis_size(name)
    return total.bit_length() - 1


def exchange(values, axes, mask):
    total = 1 << bit_count(axes)
    return lax.ppermute(values, axes, [(i, i ^ mask) for i in range(total)])


def spread_order(axes):
    expert_bits = bit_count(("expert",)) if "expert" in axes else 0
    dp_bits = bit_count(("dp",)) if "dp" in axes else 0
    dp_list = [expert_bits + i for i in range(dp_bits)]
    return dp_list + list(range(expert_bits))


def reduce_scatter_bits(values, axes, order):
    count = bit_count(axes)
    index = position(axes)
    left = list(range(count - 1, -1, -1))
    for bit in order:
        dim = left.index(bit)
        own_bit = (index >> bit) & 1
        sent = lax.dynamic_index_in_dim(values, 1 - own_bit, dim, False)
        kept = lax.dynamic_index_in_dim(values, own_bit, dim, False)
        arrived = exchange(sent, axes, 1 << bit)
        values = (kept.astype(jnp.float32) + arrived.astype(jnp.float32)).astype(values.dtype)
        left.remove(bit)
    return values


def all_gather_bits(values, axes, order):
    index = position(axes)
    held = []
    for bit in order:
        own_bit = (index >> bit) & 1
        arrived = exchange(values, axes, 1 << bit)
        dim = sum(1 for other in held if other > bit)
        values = jnp.stack(
            [jnp.where(own_bit == 0, values, arrived), jnp.where(own_bit == 0, arrived, values)],
            dim,
        )
        held.append(bit)
    return values


def sum_everywhere(values):
    order = spread_order(AXES)
    expert_bits = bit_count(("expert",))
    groups = [order[:1]]
    rest = [order[1 : len(order) - expert_bits], order[len(order) - expert_bits :]]
    for bits in rest:
        groups += [bits[i : i + 2] for i in range(0, len(bits), 2)]
    for bits in groups:
        if len(bits) == 1:
            values = values + exchange(values, AXES, 1 << bits[0])
        else:
            low, high = 1 << bits[0], 1 << bits[1]
            near = exchange(values, AXES, low)
            far = exchange(values, AXES, high)
            across = exchange(values, AXES, low | high)
            values = (values + near) + (far + across)
    return values


def silu_slope(preactivation):
    logistic = jax.nn.sigmoid(preactivation)
    return logistic * (1.0 + preactivation * (1.0 - logistic))


def segments(lengths_row, row_count):
    seg_ends = jnp.cumsum(lengths_row, dtype=jnp.int32)
    seg_starts = seg_ends - lengths_row
    positions = jnp.arange(row_count, dtype=jnp.int32)
    segment = jnp.sum((positions[:, None] >= seg_ends[None, :]).astype(jnp.int32), 1)
    member = segment[:, None] == jnp.arange(lengths_row.shape[0], dtype=jnp.int32)[None, :]
    offsets = positions - jnp.sum(jnp.where(member, seg_starts[None, :], 0), 1)
    validity = (segment < lengths_row.shape[0] - 1).astype(jnp.float32)
    return (segment, offsets, validity)


def rotation(offsets, head_dim):
    half_dim = head_dim // 2
    frequency = 10000.0 ** (-jnp.arange(half_dim, dtype=jnp.float32) / half_dim)
    angles = offsets.astype(jnp.float32)[:, None] * frequency[None, :]
    return (jnp.cos(angles)[:, None, :], jnp.sin(angles)[:, None, :])


def rotate(values, cosine, sine_table):
    half_dim = values.shape[-1] // 2
    first_half = values[..., :half_dim]
    second_half = values[..., half_dim:]
    return jnp.concatenate(
        [
            first_half * cosine - second_half * sine_table,
            first_half * sine_table + second_half * cosine,
        ],
        -1,
    )


def norm_forward(rows_in, gain_row):
    centred = rows_in - jnp.mean(rows_in, -1, keepdims=True)
    inverse = lax.rsqrt(jnp.mean(centred * centred, -1, keepdims=True) + EPSILON)
    normed = centred * inverse
    return (normed * gain_row, normed, inverse)


def norm_backward(grad_out, gain_row, normed, inverse):
    scaled = grad_out * gain_row
    gain_grad = jnp.sum(grad_out * normed, 0)
    rows_grad = inverse * (
        scaled
        - jnp.mean(scaled, -1, keepdims=True)
        - normed * jnp.mean(scaled * normed, -1, keepdims=True)
    )
    return (rows_grad, gain_grad)


def depthwise(values, kernel, segment):
    row_count = values.shape[0]
    reach_half = kernel.shape[0] // 2
    padded = jnp.pad(values, ((reach_half, reach_half), (0, 0)))
    seg_padded = jnp.pad(segment, (reach_half, reach_half), constant_values=-1)
    result = jnp.zeros(values.shape, jnp.float32)
    for tap_index in range(kernel.shape[0]):
        same_segment = (seg_padded[tap_index : tap_index + row_count] == segment).astype(
            jnp.float32
        )[:, None]
        result = (
            result + kernel[tap_index] * padded[tap_index : tap_index + row_count] * same_segment
        )
    return result


def depthwise_backward(grad_out, values, kernel, segment):
    row_count = values.shape[0]
    reach_half = kernel.shape[0] // 2
    padded = jnp.pad(values, ((reach_half, reach_half), (0, 0)))
    seg_padded = jnp.pad(segment, (reach_half, reach_half), constant_values=-1)
    values_grad = jnp.zeros(values.shape, jnp.float32)
    kernel_rows = []
    for tap_index in range(kernel.shape[0]):
        same_segment = (seg_padded[tap_index : tap_index + row_count] == segment).astype(
            jnp.float32
        )[:, None]
        masked = grad_out * same_segment
        kernel_rows.append(jnp.sum(masked * padded[tap_index : tap_index + row_count], 0))
        start_row = 2 * reach_half - tap_index
        shifted = jnp.pad(masked, ((reach_half, reach_half), (0, 0)))[
            start_row : start_row + row_count
        ]
        values_grad = values_grad + kernel[tap_index] * shifted
    return (values_grad, jnp.stack(kernel_rows))


def attend_forward(query_rows, key_rows, value_rows, segment, block_rows):
    row_count, head_count, head_dim = query_rows.shape
    block_count = row_count // block_rows
    score_scale = head_dim ** (-0.5)

    def one_block(inputs):
        query_block, segment_block = inputs
        scores = (
            jnp.einsum("bhd,thd->hbt", query_block, key_rows, preferred_element_type=jnp.float32)
            * score_scale
        )
        allowed = (segment_block[:, None] == segment[None, :])[None]
        scores = jnp.where(allowed, scores, -MASK_FILL)
        row_max = jnp.max(scores, -1, keepdims=True)
        weights = jnp.exp(scores - row_max)
        row_total = jnp.sum(weights, -1, keepdims=True)
        probabilities = (weights / row_total).astype(jnp.bfloat16)
        attended = jnp.einsum(
            "hbt,thd->bhd", probabilities, value_rows, preferred_element_type=jnp.float32
        )
        return (attended, (row_max + jnp.log(row_total))[..., 0])

    attended, logsum = lax.map(
        one_block,
        (
            query_rows.reshape(block_count, block_rows, head_count, head_dim),
            segment.reshape(block_count, block_rows),
        ),
    )
    return (attended.reshape(row_count, head_count, head_dim), logsum)


def attend_backward(query_rows, key_rows, value_rows, segment, logsum, attended_grad, block_rows):
    row_count, head_count, head_dim = query_rows.shape
    block_count = row_count // block_rows
    score_scale = head_dim ** (-0.5)

    def one_block(running, inputs):
        key_grad, value_grad = running
        query_block, segment_block, logsum_block, grad_block = inputs
        scores = (
            jnp.einsum("bhd,thd->hbt", query_block, key_rows, preferred_element_type=jnp.float32)
            * score_scale
        )
        allowed = (segment_block[:, None] == segment[None, :])[None]
        probabilities = jnp.where(allowed, jnp.exp(scores - logsum_block[:, :, None]), 0.0)
        prob_grad = jnp.einsum(
            "bhd,thd->hbt", grad_block, value_rows, preferred_element_type=jnp.float32
        )
        row_inner = jnp.sum(probabilities * prob_grad, -1, keepdims=True)
        score_grad = (probabilities * (prob_grad - row_inner)).astype(jnp.bfloat16)
        query_grad = (
            jnp.einsum("hbt,thd->bhd", score_grad, key_rows, preferred_element_type=jnp.float32)
            * score_scale
        )
        key_grad = (
            key_grad
            + jnp.einsum(
                "hbt,bhd->thd", score_grad, query_block, preferred_element_type=jnp.float32
            )
            * score_scale
        )
        value_grad = value_grad + jnp.einsum(
            "hbt,bhd->thd",
            probabilities.astype(jnp.bfloat16),
            grad_block,
            preferred_element_type=jnp.float32,
        )
        return ((key_grad, value_grad), query_grad)

    zero_grad = jnp.zeros(query_rows.shape, jnp.float32)
    (key_grad, value_grad), query_grad = lax.scan(
        one_block,
        (zero_grad, zero_grad),
        (
            query_rows.reshape(block_count, block_rows, head_count, head_dim),
            segment.reshape(block_count, block_rows),
            logsum,
            attended_grad.reshape(block_count, block_rows, head_count, head_dim),
        ),
    )
    return (query_grad.reshape(row_count, head_count, head_dim), key_grad, value_grad)


def expert_slots(choice_col, expert_total, capacity, local_experts, peer_count):
    chosen = choice_col[:, 0]
    onehot = (chosen[:, None] == jnp.arange(expert_total, dtype=jnp.int32)[None, :]).astype(
        jnp.int32
    )
    rank_within = jnp.sum((jnp.cumsum(onehot, 0, dtype=jnp.int32) - onehot) * onehot, 1)
    slot_index = (
        chosen % local_experts * (peer_count * capacity)
        + chosen // local_experts * capacity
        + rank_within
    )
    return (slot_index, onehot.astype(jnp.float32))


def scatter_rows(rows_low, slot_index, local_experts, peer_count, capacity):
    buffer = jnp.zeros((local_experts * peer_count * capacity, rows_low.shape[1]), jnp.bfloat16)
    buffer = buffer.at[slot_index].set(rows_low)
    return buffer.reshape(local_experts, peer_count, capacity, rows_low.shape[1])


def to_experts(sent_rows):
    return lax.all_to_all(sent_rows, "expert", split_axis=1, concat_axis=1, tiled=True)


def from_experts(back_rows):
    return lax.all_to_all(back_rows, "expert", split_axis=1, concat_axis=1, tiled=True)


def gates(embedded, router, onehot):
    router_probs = jax.nn.softmax(jnp.dot(embedded, router, precision=HIGHEST), -1)
    return (router_probs, jnp.sum(router_probs * onehot, 1))


def expert_forward(arrived_rows, input_weight, output_weight):
    preactivation = jnp.einsum(
        "zve,zeg->zvg", arrived_rows, input_weight, preferred_element_type=jnp.float32
    )
    hidden = jax.nn.silu(preactivation).astype(jnp.bfloat16)
    produced = jnp.einsum(
        "gzm,gmb->gzb", hidden, output_weight, preferred_element_type=jnp.float32
    ).astype(jnp.bfloat16)
    return (preactivation, hidden, produced)


def expert_backward(row_grads, arrived_rows, preactivation, hidden, input_weight, output_weight):
    hidden_grad = jnp.einsum(
        "ysi,yzi->ysz", row_grads, output_weight, preferred_element_type=jnp.float32
    )
    preactivation_grad = (hidden_grad * silu_slope(preactivation)).astype(jnp.bfloat16)
    input_grad = jnp.einsum(
        "wot,wqt->woq", preactivation_grad, input_weight, preferred_element_type=jnp.float32
    ).astype(jnp.bfloat16)
    out_weight_grad = jnp.einsum(
        "ymv,yml->yvl", hidden, row_grads, preferred_element_type=jnp.float32
    ).astype(jnp.bfloat16)
    in_weight_grad = jnp.einsum(
        "keo,keu->kou", arrived_rows, preactivation_grad, preferred_element_type=jnp.float32
    ).astype(jnp.bfloat16)
    return (input_grad, in_weight_grad, out_weight_grad)


def shards(
    frames,
    lengths,
    choice_first,
    choice_second,
    embed_weight,
    routers,
    norm_gains,
    attn_in,
    attn_out,
    conv_in,
    conv_kernel,
    bn_shift,
    conv_out,
    expert_in,
    expert_out,
    cotangent,
):
    row_count, model_width = frames.shape
    router_count, slice_width, expert_total = routers.shape
    tap_count = conv_kernel.shape[0]
    gain_count = norm_gains.shape[0]
    peer_count = lax.axis_size("expert")
    dp_count = lax.axis_size("dp")
    device_total = peer_count * dp_count
    local_experts = expert_in.shape[1]
    capacity = 2 * row_count // expert_total
    dp_bits = bit_count(("dp",))
    expert_bits = bit_count(("expert",))
    hidden_width = expert_in.shape[3]
    slots = peer_count * capacity

    def scattered(rows_low, slot_index):
        return scatter_rows(rows_low, slot_index, local_experts, peer_count, capacity)

    def arrived_of(sent):
        return to_experts(sent).reshape(local_experts, slots, model_width)

    def returned_of(back, slot_index):
        back = from_experts(back.reshape(local_experts, peer_count, capacity, model_width))
        return back.reshape(-1, model_width)[slot_index].astype(jnp.float32)

    slot_first, onehot_first = expert_slots(
        choice_first, expert_total, capacity, local_experts, peer_count
    )
    slot_second, onehot_second = expert_slots(
        choice_second, expert_total, capacity, local_experts, peer_count
    )
    arrived_frames = arrived_of(scattered(frames, slot_first))
    dp_order = list(range(dp_bits))
    outer_bits = dp_order[1:]
    first_in = all_gather_bits(expert_in[0], ("dp",), outer_bits + [0])
    first_out = all_gather_bits(expert_out[0], ("dp",), outer_bits[::-1] + [0])

    def whole_weight(pieces, depth):
        pieces = pieces.reshape((dp_count,) + pieces.shape[dp_bits:])
        return jnp.moveaxis(pieces, 0, 1).reshape(local_experts, depth, -1)

    first_in = whole_weight(first_in, model_width)
    first_out = whole_weight(first_out, hidden_width)
    small_width = router_count * expert_total + gain_count + tap_count + 1
    small = jnp.concatenate(
        [
            jnp.moveaxis(routers, 1, 0).reshape(slice_width, -1),
            norm_gains.T,
            conv_kernel.T,
            bn_shift[:, None],
            jnp.zeros((slice_width, -small_width % 128), jnp.bfloat16),
        ],
        1,
    )
    dense = lax.all_gather(
        jnp.concatenate([attn_in, attn_out, conv_in, conv_out, small], 1), AXES, axis=0, tiled=True
    )
    second_in = lax.all_gather(expert_in[1], "dp", axis=1, tiled=True)
    second_out = lax.all_gather(expert_out[1], "dp", axis=1, tiled=True)

    width = model_width
    attn_in_all = dense[:, : 3 * width]
    attn_out_all = dense[:, 3 * width : 4 * width]
    conv_in_all = dense[:, 4 * width : 6 * width]
    conv_out_all = dense[:, 6 * width : 7 * width]
    small_all = dense[:, 7 * width :].astype(jnp.float32)
    start = router_count * expert_total
    router_pair = jnp.moveaxis(small_all[:, :start].reshape(width, router_count, expert_total), 1, 0)
    gain_rows = small_all[:, start : start + gain_count].T
    kernel = small_all[:, start + gain_count : start + gain_count + tap_count].T
    shift_row = small_all[:, start + gain_count + tap_count]

    own_lengths = lax.dynamic_index_in_dim(lengths, lax.axis_index(AXES), 0, keepdims=False)
    segment, offsets, validity = segments(own_lengths, row_count)
    frame_count = jnp.sum(lengths[:, :-1]).astype(jnp.float32)
    block_rows = min(512, row_count)
    cosine, sine_table = rotation(offsets, DH)
    rows_in = frames.astype(jnp.float32)
    embed_pre = jnp.dot(frames, embed_weight, preferred_element_type=jnp.float32)
    embedded = jax.nn.silu(embed_pre)
    probs_first, gate_first = gates(embedded, router_pair[0], onehot_first)
    probs_second, gate_second = gates(embedded, router_pair[1], onehot_second)

    first_norm, first_hat_arrived, _ = norm_forward(
        arrived_frames.astype(jnp.float32), gain_rows[0]
    )
    first_arrived = first_norm.astype(jnp.bfloat16)
    first_pre, first_hidden, first_produced = expert_forward(first_arrived, first_in, first_out)
    first_expert = returned_of(first_produced, slot_first)
    after_first = rows_in + 0.5 * gate_first[:, None] * first_expert

    attn_norm, attn_hat, attn_inverse = norm_forward(after_first, gain_rows[1])
    attn_low = attn_norm.astype(jnp.bfloat16)
    projected = jnp.dot(attn_low, attn_in_all, preferred_element_type=jnp.float32)
    query_rows = rotate(
        projected[:, :model_width].reshape(row_count, H, DH), cosine, sine_table
    ).astype(jnp.bfloat16)
    key_rows = rotate(
        projected[:, model_width : 2 * model_width].reshape(row_count, H, DH), cosine, sine_table
    ).astype(jnp.bfloat16)
    value_rows = projected[:, 2 * model_width :].reshape(row_count, H, DH).astype(jnp.bfloat16)
    attended, logsum = attend_forward(query_rows, key_rows, value_rows, segment, block_rows)
    attended_low = attended.reshape(row_count, model_width).astype(jnp.bfloat16)
    after_attention = after_first + jnp.dot(
        attended_low, attn_out_all, preferred_element_type=jnp.float32
    )
    conv_norm, conv_hat, conv_inverse = norm_forward(after_attention, gain_rows[2])
    conv_low = conv_norm.astype(jnp.bfloat16)
    gates_in = jnp.dot(conv_low, conv_in_all, preferred_element_type=jnp.float32)
    logistic = jax.nn.sigmoid(gates_in[:, model_width:])
    glu_out = gates_in[:, :model_width] * logistic
    conv_depth = depthwise(glu_out, kernel, segment)
    weighted = validity[:, None] * conv_depth
    moments = sum_everywhere(jnp.stack([jnp.sum(weighted, 0), jnp.sum(weighted * conv_depth, 0)]))
    batch_mean = moments[0] / frame_count
    batch_var = moments[1] / frame_count - batch_mean * batch_mean
    batch_inverse = lax.rsqrt(batch_var + EPSILON)
    centred_depth = conv_depth - batch_mean
    batch_hat = centred_depth * batch_inverse
    batch_out = batch_hat * gain_rows[5] + shift_row
    swish_low = jax.nn.silu(batch_out).astype(jnp.bfloat16)
    after_conv = after_attention + jnp.dot(
        swish_low, conv_out_all, preferred_element_type=jnp.float32
    )

    second_norm, second_hat, second_inverse = norm_forward(after_conv, gain_rows[3])
    second_arrived = arrived_of(scattered(second_norm.astype(jnp.bfloat16), slot_second))
    second_pre, second_hidden, second_produced = expert_forward(
        second_arrived, second_in, second_out
    )
    second_expert = returned_of(second_produced, slot_second)
    after_second = after_conv + 0.5 * gate_second[:, None] * second_expert
    final_norm, final_hat, final_inverse = norm_forward(after_second, gain_rows[4])
    block_out = (final_norm * validity[:, None]).astype(jnp.bfloat16)

    grad_final = cotangent.astype(jnp.float32) * validity[:, None]
    grad_second, final_gain_grad = norm_backward(grad_final, gain_rows[4], final_hat, final_inverse)
    second_sent = (0.5 * gate_second[:, None] * grad_second).astype(jnp.bfloat16)
    second_row_grads = arrived_of(scattered(second_sent, slot_second))
    second_gate_grad = 0.5 * jnp.sum(second_expert * grad_second, 1)
    second_logit_grad = (second_gate_grad * gate_second)[:, None] * (onehot_second - probs_second)
    second_input_grad, second_in_grad, second_out_grad = expert_backward(
        second_row_grads, second_arrived, second_pre, second_hidden, second_in, second_out
    )
    second_norm_grad = returned_of(second_input_grad, slot_second)
    rows_grad, second_gain_grad = norm_backward(
        second_norm_grad, gain_rows[3], second_hat, second_inverse
    )
    grad_conv = grad_second + rows_grad
    second_in_grad = lax.psum_scatter(second_in_grad, "dp", scatter_dimension=1, tiled=True)
    second_out_grad = lax.psum_scatter(second_out_grad, "dp", scatter_dimension=1, tiled=True)

    conv_grad_low = grad_conv.astype(jnp.bfloat16)
    conv_out_grad = jnp.einsum(
        "td,te->de", swish_low, conv_grad_low, preferred_element_type=jnp.float32
    )
    swish_grad = jnp.einsum(
        "te,de->td", conv_grad_low, conv_out_all, preferred_element_type=jnp.float32
    )
    batch_grad = swish_grad * silu_slope(batch_out)
    shift_grad = jnp.sum(batch_grad, 0)
    bn_gain_grad = jnp.sum(batch_grad * batch_hat, 0)
    hat_grad = batch_grad * gain_rows[5]
    hat_sums = sum_everywhere(
        jnp.stack([jnp.sum(hat_grad, 0), jnp.sum(hat_grad * centred_depth, 0)])
    )
    hat_total, hat_moment = (hat_sums[0], hat_sums[1])
    var_grad = -0.5 * hat_moment * batch_inverse * batch_inverse * batch_inverse
    mean_grad = -batch_inverse * hat_total - 2.0 * batch_mean * var_grad
    depth_grad = (
        hat_grad * batch_inverse
        + validity[:, None] * (mean_grad + 2.0 * conv_depth * var_grad) / frame_count
    )
    glu_grad, kernel_grad = depthwise_backward(depth_grad, glu_out, kernel, segment)
    gates_grad = jnp.concatenate(
        [glu_grad * logistic, glu_grad * gates_in[:, :model_width] * logistic * (1.0 - logistic)], 1
    ).astype(jnp.bfloat16)
    conv_in_grad = jnp.einsum("td,te->de", conv_low, gates_grad, preferred_element_type=jnp.float32)
    conv_norm_grad = jnp.einsum(
        "te,de->td", gates_grad, conv_in_all, preferred_element_type=jnp.float32
    )
    rows_grad, conv_gain_grad = norm_backward(conv_norm_grad, gain_rows[2], conv_hat, conv_inverse)
    grad_attention = grad_conv + rows_grad
    attention_grad_low = grad_attention.astype(jnp.bfloat16)
    attn_out_grad = jnp.einsum(
        "td,te->de", attended_low, attention_grad_low, preferred_element_type=jnp.float32
    )
    attended_grad = (
        jnp.einsum(
            "te,de->td", attention_grad_low, attn_out_all, preferred_element_type=jnp.float32
        )
        .astype(jnp.bfloat16)
        .reshape(row_count, H, DH)
    )
    query_grad, key_grad, value_grad = attend_backward(
        query_rows, key_rows, value_rows, segment, logsum, attended_grad, block_rows
    )
    projected_grad = jnp.concatenate(
        [
            rotate(query_grad, cosine, -sine_table).reshape(row_count, model_width),
            rotate(key_grad, cosine, -sine_table).reshape(row_count, model_width),
            value_grad.reshape(row_count, model_width),
        ],
        1,
    ).astype(jnp.bfloat16)
    attn_in_grad = jnp.einsum(
        "td,te->de", attn_low, projected_grad, preferred_element_type=jnp.float32
    )
    attn_norm_grad = jnp.einsum(
        "te,de->td", projected_grad, attn_in_all, preferred_element_type=jnp.float32
    )
    rows_grad, attn_gain_grad = norm_backward(attn_norm_grad, gain_rows[1], attn_hat, attn_inverse)
    grad_first = grad_attention + rows_grad

    first_sent = (0.5 * gate_first[:, None] * grad_first).astype(jnp.bfloat16)
    first_row_grads = arrived_of(scattered(first_sent, slot_first))
    first_gate_grad = 0.5 * jnp.sum(first_expert * grad_first, 1)
    first_logit_grad = (first_gate_grad * gate_first)[:, None] * (onehot_first - probs_first)

    def to_owners(term):
        term = lax.psum_scatter(term.astype(jnp.bfloat16), "dp", scatter_dimension=0, tiled=True)
        return lax.psum_scatter(term, "expert", scatter_dimension=0, tiled=True).astype(jnp.float32)

    conv_terms = to_owners(jnp.concatenate([attn_out_grad, conv_in_grad, conv_out_grad], 1))
    attn_terms = to_owners(attn_in_grad)

    embed_rows_grad = jnp.dot(first_logit_grad, router_pair[0].T, precision=HIGHEST) + jnp.dot(
        second_logit_grad, router_pair[1].T, precision=HIGHEST
    )
    embed_pre_grad = (embed_rows_grad * silu_slope(embed_pre)).astype(jnp.bfloat16)
    embed_term = jnp.einsum("td,te->de", frames, embed_pre_grad, preferred_element_type=jnp.float32)
    all_bits = dp_bits + expert_bits
    order = spread_order(AXES)
    embed_own = reduce_scatter_bits(
        embed_term.astype(jnp.bfloat16).reshape((2,) * all_bits + (slice_width, width)), AXES, order
    )
    embed_total = (
        all_gather_bits(embed_own, AXES, order[::-1]).reshape(width, width).astype(jnp.float32)
    )
    embed_rows = jnp.einsum(
        "te,de->td", embed_pre_grad, embed_weight, preferred_element_type=jnp.float32
    )

    first_input_grad, first_in_grad, first_out_grad = expert_backward(
        first_row_grads, first_arrived, first_pre, first_hidden, first_in, first_out
    )
    first_gain_grad = jnp.sum(first_input_grad.astype(jnp.float32) * first_hat_arrived, (0, 1))

    def to_expert_owners(term, order):
        pieces = term.reshape(local_experts, dp_count, -1, term.shape[2])
        pieces = jnp.moveaxis(pieces, 1, 0)
        pieces = pieces.reshape((2,) * dp_bits + pieces.shape[1:])
        return reduce_scatter_bits(pieces, ("dp",), order)

    first_out_own = to_expert_owners(first_out_grad, [0] + outer_bits[::-1])
    first_in_own = to_expert_owners(first_in_grad, [0] + outer_bits)

    router_terms = jnp.concatenate(
        [
            jnp.dot(embedded.T, first_logit_grad, precision=HIGHEST),
            jnp.dot(embedded.T, second_logit_grad, precision=HIGHEST),
        ],
        1,
    ).T
    small_terms = jnp.concatenate(
        [
            router_terms,
            first_gain_grad[None],
            attn_gain_grad[None],
            conv_gain_grad[None],
            second_gain_grad[None],
            final_gain_grad[None],
            bn_gain_grad[None],
            kernel_grad,
            shift_grad[None],
        ],
        0,
    )
    small_sums = lax.dynamic_slice_in_dim(
        sum_everywhere(small_terms), lax.axis_index(AXES) * slice_width, slice_width, 1
    )
    routers_out = jnp.moveaxis(
        small_sums[:start].reshape(router_count, expert_total, slice_width), 1, 2
    )
    gains_out = small_sums[start : start + gain_count]
    kernel_out = small_sums[start + gain_count : start + gain_count + tap_count]
    shift_out = small_sums[start + gain_count + tap_count]

    first_norm_grad = returned_of(first_input_grad, slot_first)
    _, first_hat, first_inverse = norm_forward(rows_in, gain_rows[0])
    rows_grad, _ = norm_backward(first_norm_grad, gain_rows[0], first_hat, first_inverse)
    frames_grad = grad_first + rows_grad + embed_rows
    return (
        block_out,
        frames_grad,
        embed_total,
        routers_out,
        gains_out,
        attn_terms,
        conv_terms[:, :width],
        conv_terms[:, width : 3 * width],
        kernel_out,
        shift_out,
        conv_terms[:, 3 * width :],
        jnp.stack([first_in_own, second_in_grad]).astype(jnp.float32),
        jnp.stack([first_out_own, second_out_grad]).astype(jnp.float32),
    )


def solution(mesh):
    in_specs = (
        P(("dp", "expert"), None),
        P(),
        P(("dp", "expert"), None),
        P(("dp", "expert"), None),
        P(),
        P(None, ("dp", "expert"), None),
        P(None, ("dp", "expert")),
        P(("dp", "expert"), None),
        P(("dp", "expert"), None),
        P(("dp", "expert"), None),
        P(None, ("dp", "expert")),
        P(("dp", "expert")),
        P(("dp", "expert"), None),
        P(None, "expert", "dp", None),
        P(None, "expert", "dp", None),
        P(("dp", "expert"), None),
    )
    out_specs = (
        P(("dp", "expert"), None),
        P(("dp", "expert"), None),
        P(),
        P(None, ("dp", "expert"), None),
        P(None, ("dp", "expert")),
        P(("dp", "expert"), None),
        P(("dp", "expert"), None),
        P(("dp", "expert"), None),
        P(None, ("dp", "expert")),
        P(("dp", "expert")),
        P(("dp", "expert"), None),
        P(None, "expert", "dp", None),
        P(None, "expert", "dp", None),
    )
    return jax.shard_map(shards, mesh=mesh, in_specs=in_specs, out_specs=out_specs, check_vma=False)
```

```python
import functools

import jax
import jax.numpy as jnp
import numpy as np
from jax import lax
from jax.experimental import pallas as pl
from jax.experimental.pallas import tpu as pltpu
from jax.sharding import PartitionSpec as P

H = 8
DH = 64
LANES = 128

EPSILON = 1e-05
MASK_FILL = 1000000000.0
HIGHEST = lax.Precision.HIGHEST
AXES = ("dp", "expert")
BF16 = jnp.bfloat16
F32 = jnp.float32
I32 = jnp.int32
MIB = 1 << 20


def bit_count(axes):
    total = 1
    for name in axes:
        total *= lax.axis_size(name)
    return total.bit_length() - 1


def exchange(values, axes, mask):
    total = 1 << bit_count(axes)
    return lax.ppermute(values, axes, [(i, i ^ mask) for i in range(total)])


def device_groups():
    z_bits = bit_count(("expert",))
    dp_bits = bit_count(("dp",))
    chips = list(range(z_bits + 1, z_bits + dp_bits))
    rests = [chips, list(range(z_bits))]
    return [[z_bits]] + [bits[i : i + 2] for bits in rests for i in range(0, len(bits), 2)]


def masks_of(bits):
    if len(bits) == 1:
        return [1 << bits[0]]
    low, high = 1 << bits[0], 1 << bits[1]
    return [low, high, low | high]


def sum_everywhere(values):
    for bits in device_groups():
        arrived = [exchange(values, AXES, mask) for mask in masks_of(bits)]
        if len(arrived) == 1:
            values = values + arrived[0]
        else:
            values = (values + arrived[0]) + (arrived[1] + arrived[2])
    return values


def gather_everywhere(values):
    total = 1 << bit_count(AXES)
    sent = jnp.broadcast_to(values[None], (total,) + values.shape)
    return lax.all_to_all(sent, AXES, split_axis=0, concat_axis=0, tiled=True)


def sum_to_owners(values, axes):
    arrived = lax.all_to_all(values, axes, split_axis=0, concat_axis=0, tiled=True)
    return jnp.sum(arrived.astype(F32), 0)


def swap_blocks(blocks):
    total = lax.axis_size("expert")
    moved = [blocks[0]]
    for k in range(1, total):
        moved.append(lax.ppermute(blocks[k], "expert", [(i, i ^ k) for i in range(total)]))
    return moved


def chip_masks():
    return [core << 1 for core in range(lax.axis_size("dp") // 2)]


def call(body, outs, *args, specs=None, out_specs=None, scratch=(), vmem=60, **kw):
    vmem_spec = pl.BlockSpec(memory_space=pltpu.VMEM)
    if specs is None:
        specs = [None] * len(args)
    grid = kw.pop("grid", (1,))
    specs = [
        jax.tree.map(lambda _: vmem_spec, arg) if spec is None else spec
        for spec, arg in zip(specs, args)
    ]
    if out_specs is None:
        out_specs = jax.tree.map(lambda _: vmem_spec, outs)
    return pl.pallas_call(
        body,
        out_shape=outs,
        in_specs=specs,
        out_specs=out_specs,
        scratch_shapes=list(scratch),
        grid=grid,
        compiler_params=pltpu.CompilerParams(vmem_limit_bytes=vmem * MIB),
        cost_estimate=pl.CostEstimate(flops=0, bytes_accessed=0, transcendentals=0),
        **kw,
    )(*args)


def shaped(shape, dtype):
    return jax.ShapeDtypeStruct(shape, dtype)


SMEM = pl.BlockSpec(memory_space=pltpu.SMEM)
ANY = pl.BlockSpec(memory_space=pl.ANY)


def dot(left, right):
    return lax.dot_general(left, right, (((1,), (0,)), ((), ())), preferred_element_type=F32)


def dot_nt(left, right):
    return lax.dot_general(left, right, (((1,), (1,)), ((), ())), preferred_element_type=F32)


def dot_tn(left, right):
    return lax.dot_general(left, right, (((0,), (0,)), ((), ())), preferred_element_type=F32)


def iota(shape, dim):
    return lax.broadcasted_iota(I32, shape, dim)


def normalize(rows):
    centred = rows - jnp.mean(rows, -1, keepdims=True)
    inverse = lax.rsqrt(jnp.mean(centred * centred, -1, keepdims=True) + EPSILON)
    return centred * inverse, inverse


def norm_backward(grad, gain, hat, inverse):
    scaled = grad * gain
    return inverse * (
        scaled
        - jnp.mean(scaled, -1, keepdims=True)
        - hat * jnp.mean(scaled * hat, -1, keepdims=True)
    )


def sigmoid(values):
    return 1.0 / (1.0 + jnp.exp(-values))


def slope(values, logistic):
    return logistic * (1.0 + values * (1.0 - logistic))


def chunks(total, size):
    return [pl.ds(start, size) for start in range(0, total, size)]


def gathered(slot_col, blocks, rows):
    slot = slot_col[rows, :]
    total = None
    for k, block in enumerate(blocks):
        capacity = block.shape[0]
        pick = (slot == iota((slot.shape[0], capacity), 1) + k * capacity).astype(F32).astype(BF16)
        part = dot(pick, block[...])
        total = part if total is None else total + part
    return total


def scatter_to(slot_row, values, outs):
    for k, out in enumerate(outs):
        capacity = out.shape[0]
        pick = (slot_row[...] == iota((capacity, slot_row.shape[1]), 0) + k * capacity)
        out[...] = dot(pick.astype(F32).astype(BF16), values).astype(BF16)


def start_kernel(own, frames, col1, row1, col2, row2, sent, slot_col1, slot_row1, slot_col2, slot_row2):
    rows = frames.shape[0]
    capacity = sent[0].shape[0]
    below = (iota((rows, rows), 0) > iota((rows, rows), 1)).astype(F32).astype(BF16)
    above = (iota((rows, rows), 0) < iota((rows, rows), 1)).astype(F32).astype(BF16)
    for col, row, out_col, out_row in (
        (col1, row1, slot_col1, slot_row1),
        (col2, row2, slot_col2, slot_row2),
    ):
        hot = (col[...] == iota((rows, LANES), 1)).astype(F32)
        rank = jnp.sum(dot(below, hot.astype(BF16)) * hot, 1, keepdims=True)
        out_col[...] = (col[...] ^ own[0]) * capacity + rank.astype(I32)
        hot = (row[...] == iota((16, rows), 0)).astype(F32)
        rank = jnp.sum(dot(hot.astype(BF16), above) * hot, 0, keepdims=True)
        out_row[...] = (row[...] ^ own[0]) * capacity + rank.astype(I32)
    scatter_to(slot_row1, frames[...], sent)


def expert_specs(weights, hidden, tile):
    count, rows, width = weights.shape
    half = rows // 2
    in_rows = width // count
    first = pl.BlockSpec((count, in_rows, tile), lambda j: (0, half // in_rows + j, 0))
    second = pl.BlockSpec((tile // half, half, width), lambda j: (j, 0, 0))
    return first, second


def flat(ref):
    count, rows, width = ref.shape
    return ref[...].reshape(count * rows, width)


def expert_forward_kernel(with_norm, block, gain, w_in, w_out, out, total, inputs):
    step = pl.program_id(0)

    @pl.when(step == 0)
    def _():
        if with_norm:
            hat, _ = normalize(block[...].astype(F32))
            inputs[...] = (hat * gain[...]).astype(BF16)
        else:
            inputs[...] = block[...]
        total[...] = jnp.zeros_like(total)

    pre = dot(inputs[...], flat(w_in))
    hidden = (pre * sigmoid(pre)).astype(BF16)
    total[...] += dot(hidden, flat(w_out))

    @pl.when(step == pl.num_programs(0) - 1)
    def _():
        out[...] = total[...].astype(BF16)


def expert_forward(block, gain, weights, hidden, with_norm, tile=512):
    capacity, width = block.shape
    first, second = expert_specs(weights, hidden, tile)
    whole = pl.BlockSpec((capacity, width), lambda j: (0, 0))
    return call(
        functools.partial(expert_forward_kernel, with_norm),
        shaped((capacity, width), BF16),
        block,
        gain,
        weights,
        weights,
        specs=[whole, pl.BlockSpec((1, width), lambda j: (0, 0)), first, second],
        out_specs=whole,
        scratch=[pltpu.VMEM((capacity, width), F32), pltpu.VMEM((capacity, width), BF16)],
        grid=(hidden // tile,),
        vmem=12,
    )


def expert_backward_kernel(
    with_norm, block, grad, gain, w_in, w_out, out, hidden_out, pre_grad_out, input_out, gain_out, total, hats
):
    step = pl.program_id(0)

    @pl.when(step == 0)
    def _():
        if with_norm:
            hat, _ = normalize(block[...].astype(F32))
            hats[...] = hat
            input_out[...] = (hat * gain[...]).astype(BF16)
        else:
            input_out[...] = block[...]
        total[...] = jnp.zeros_like(total)

    first, second = flat(w_in), flat(w_out)
    pre = dot(input_out[...], first)
    logistic = sigmoid(pre)
    hidden_out[...] = (pre * logistic).astype(BF16)
    hidden_grad = dot_nt(grad[...], second)
    pre_grad = (hidden_grad * slope(pre, logistic)).astype(BF16)
    pre_grad_out[...] = pre_grad
    total[...] += dot_nt(pre_grad, first)

    @pl.when(step == pl.num_programs(0) - 1)
    def _():
        back = total[...].astype(BF16)
        out[...] = back
        if with_norm:
            gain_out[...] = jnp.sum(back.astype(F32) * hats[...], 0, keepdims=True)
        else:
            gain_out[...] = jnp.zeros_like(gain_out)


def expert_backward(block, grad, gain, weights, hidden, with_norm, tile=512):
    capacity, width = block.shape
    first, second = expert_specs(weights, hidden, tile)
    whole = pl.BlockSpec((capacity, width), lambda j: (0, 0))
    tiled = pl.BlockSpec((capacity, tile), lambda j: (0, j))
    one = pl.BlockSpec((1, width), lambda j: (0, 0))
    return call(
        functools.partial(expert_backward_kernel, with_norm),
        (
            shaped((capacity, width), BF16),
            shaped((capacity, hidden), BF16),
            shaped((capacity, hidden), BF16),
            shaped((capacity, width), BF16),
            shaped((1, width), F32),
        ),
        block,
        grad,
        gain,
        weights,
        weights,
        specs=[whole, whole, one, first, second],
        out_specs=(whole, tiled, tiled, whole, one),
        scratch=[pltpu.VMEM((capacity, width), F32), pltpu.VMEM((capacity, width), F32)],
        grid=(hidden // tile,),
        vmem=16,
    )


def weight_grad_kernel(relative, dp_index, inputs, grads, hidden, pre_grads, *refs):
    outs, (first, second) = refs[:-2], refs[-2:]
    step = pl.program_id(0)
    first_sum = second_sum = None
    for block, grad, hid, pre_grad in zip(inputs, grads, hidden, pre_grads):
        part = dot_tn(block[...], pre_grad[...])
        first_sum = part if first_sum is None else first_sum + part
        part = dot_tn(hid[...], grad[...])
        second_sum = part if second_sum is None else second_sum + part
    count = sum(out.shape[0] for out in outs)
    half = outs[0].shape[1] // 2
    in_rows = first_sum.shape[0] // count
    tile = second_sum.shape[0]
    owners = tile // half
    place = pl.ds(pl.multiple_of(half + step * in_rows, in_rows), in_rows)
    if not relative:
        for device in range(count):
            outs[0][device, place, :] = first_sum[device * in_rows : (device + 1) * in_rows].astype(BF16)
        for number in range(owners):
            outs[0][step * owners + number, pl.ds(0, half), :] = second_sum[
                number * half : (number + 1) * half
            ].astype(BF16)
    else:
        first[...] = first_sum.astype(BF16)
        for number in range(count):
            source = pl.multiple_of((dp_index[0] ^ number) * in_rows, in_rows)
            outs[number % 2][number // 2, place, :] = first[pl.ds(source, in_rows), :]
        second[...] = second_sum.astype(BF16)
        for number in range(owners):
            owner = (step * owners + number) ^ dp_index[0]

            @pl.when(owner % 2 == 0)
            def _():
                outs[0][owner // 2, pl.ds(0, half), :] = second[pl.ds(number * half, half), :]

            @pl.when(owner % 2 == 1)
            def _():
                outs[1][owner // 2, pl.ds(0, half), :] = second[pl.ds(number * half, half), :]


def weight_grads(dp_index, inputs, grads, hidden, pre_grads, count, relative, tile=512):
    capacity, width = inputs[0].shape
    units = hidden[0].shape[1]
    whole = pl.BlockSpec((capacity, width), lambda j: (0, 0))
    tiled = pl.BlockSpec((capacity, tile), lambda j: (0, j))
    rows = 2 * units // count
    if relative:
        outs = (shaped((count // 2, rows, width), BF16),) * 2
    else:
        outs = (shaped((count, rows, width), BF16),)
    peers = len(inputs)
    return call(
        functools.partial(weight_grad_kernel, relative),
        outs,
        dp_index,
        list(inputs),
        list(grads),
        list(hidden),
        list(pre_grads),
        specs=[SMEM, [whole] * peers, [whole] * peers, [tiled] * peers, [tiled] * peers],
        out_specs=tuple(pl.BlockSpec(o.shape, lambda j: (0, 0, 0)) for o in outs),
        scratch=[pltpu.VMEM((width, tile), BF16), pltpu.VMEM((tile, width), BF16)],
        grid=(units // tile,),
        vmem=28,
    )


def dense_grad_kernel(
    experts, ua, dproj, attended, dat, uc, dgin, swish, dco, gate_grad1, gate1, col1, gate_grad2, gate2, col2,
    probs, routers, pre, embedded, frames, out, dz, router_terms, logits,
):
    width = ua.shape[1]
    rows = frames.shape[0]
    for part in chunks(rows, 128):
        lane = iota((128, LANES), 1)
        grad = jnp.zeros((128, LANES), F32)
        for number, (gate_grad, gate, col) in enumerate(((gate_grad1, gate1, col1), (gate_grad2, gate2, col2))):
            inside = (lane >= number * experts) & (lane < (number + 1) * experts)
            hot = (lane == col[part, :] + number * experts).astype(F32)
            scale = gate_grad[part, :] * gate[part, :]
            grad = jnp.where(inside, scale * (hot - probs[part, :]), grad)
        logits[part, :] = grad
        demb = lax.dot_general(
            grad, routers[...], (((1,), (1,)), ((), ())), precision=HIGHEST, preferred_element_type=F32
        )
        held = pre[part, :]
        dz[part, :] = (demb * slope(held, sigmoid(held))).astype(BF16)
    router_terms[...] = lax.dot_general(
        logits[...], embedded[...], (((0,), (0,)), ((), ())), precision=HIGHEST, preferred_element_type=F32
    )
    start = 0
    for left, right in ((ua, dproj), (attended, dat), (uc, dgin), (swish, dco), (frames, dz)):
        for column in range(0, right.shape[1], width):
            out[:, pl.ds(start, width)] = dot_tn(left[...], right[:, pl.ds(column, width)]).astype(BF16)
            start += width


def embed_kernel(experts, ends, frames, weight, routers, col1, col2, pre_out, embedded_out, probs_out, gate1, gate2, seg_col, seg_row, taps_out, offset_out):
    rows = frames.shape[0]
    for part in chunks(rows, 128):
        pre = dot(frames[part, :], weight[...])
        pre_out[part, :] = pre
        embedded = pre * sigmoid(pre)
        embedded_out[part, :] = embedded
        logits = jnp.dot(embedded, routers[...], precision=HIGHEST, preferred_element_type=F32)
        lane = iota(logits.shape, 1)
        probs = jnp.zeros_like(logits)
        for number, (col, gate) in enumerate(((col1, gate1), (col2, gate2))):
            inside = (lane >= number * experts) & (lane < (number + 1) * experts)
            top = jnp.max(jnp.where(inside, logits, -MASK_FILL), 1, keepdims=True)
            weights = jnp.where(inside, jnp.exp(jnp.where(inside, logits - top, 0.0)), 0.0)
            own = weights / jnp.sum(weights, 1, keepdims=True)
            hot = lane == col[part, :] + number * experts
            gate[part, :] = jnp.sum(jnp.where(hot, own, 0.0), 1, keepdims=True)
            probs = probs + own
        probs_out[part, :] = probs

    def segment_of(place):
        found = jnp.zeros(place.shape, I32)
        for number in range(3):
            found += (place >= ends[number]).astype(I32)
        return found

    segment = segment_of(iota((rows, 1), 0))
    seg_col[...] = segment
    seg_row[...] = segment_of(iota((1, rows), 1))
    place = iota((rows, LANES), 0) + iota((rows, LANES), 1) - 7
    same = (segment_of(place) == segment) & (place >= 0) & (place < rows)
    taps_out[...] = same.astype(F32)
    first = jnp.zeros((rows, 1), I32)
    for number in range(3):
        first = jnp.where(segment > number, ends[number], first)
    offset_out[...] = (iota((rows, 1), 0) - first).astype(F32)


def partner(values):
    half = DH // 2
    lane = iota(values.shape, 1)
    return jnp.where(lane % DH < half, pltpu.roll(values, LANES - half, 1), pltpu.roll(values, half, 1))


def front_kernel(
    frames, blocks, slot_col, gate, table, attn_in, attn_out, conv_in, cosine, sine, seg_col, seg_row, taps,
    expert_out, x1_out, x2_out, ua_out, qkv_out, lse_out, attended_out, uc_out, gin_out, depth_out, moments,
    padded,
):
    rows, width = frames.shape
    gains = lambda n: table[pl.ds(n, 1), :]
    for part in chunks(rows, 128):
        found = gathered(slot_col, blocks, part)
        expert_out[part, :] = found.astype(BF16)
        x1 = frames[part, :].astype(F32) + 0.5 * gate[part, :] * found
        x1_out[part, :] = x1
        hat, _ = normalize(x1)
        ua = (hat * gains(1)).astype(BF16)
        ua_out[part, :] = ua
        for piece in range(3 * width // LANES):
            lanes = pl.ds(piece * LANES, LANES)
            if piece % 2 == 0:
                pair = dot(ua, attn_in[:, pl.ds(piece * LANES, 2 * LANES)])
            values = pair[:, :LANES] if piece % 2 == 0 else pair[:, LANES:]
            if piece < 2 * width // LANES:
                values = values * cosine[part, :] + partner(values) * sine[part, :]
            if piece < width // LANES:
                values = values * DH**-0.5
            qkv_out[part, lanes] = values.astype(BF16)

    lane = iota((1, LANES), 1)
    sides = ((lane < DH), (lane >= DH))
    zero = jnp.zeros((), BF16)

    def attend(part_index, carry):
        part = pl.ds(pl.multiple_of(part_index * 128, 128), 128)
        related = seg_col[part, :] == seg_row[...]
        lse = jnp.zeros((128, LANES), F32)
        for pair in range(width // LANES):
            q = qkv_out[part, pl.ds(pair * LANES, LANES)]
            k = qkv_out[:, pl.ds(width + pair * LANES, LANES)]
            v = qkv_out[:, pl.ds(2 * width + pair * LANES, LANES)]
            result = jnp.zeros((128, LANES), F32)
            for side in range(2):
                scores = dot_nt(jnp.where(sides[side], q, zero), k)
                scores = jnp.where(related, scores, -MASK_FILL)
                top = jnp.max(scores, 1, keepdims=True)
                weights = jnp.exp(scores - top)
                summed = jnp.sum(weights, 1, keepdims=True)
                probs = (weights * (1.0 / summed)).astype(BF16)
                result += dot(probs, jnp.where(sides[side], v, zero))
                lse = jnp.where(lane == 2 * pair + side, top + jnp.log(summed), lse)
            attended_out[part, pl.ds(pair * LANES, LANES)] = result.astype(BF16)
        lse_out[part, :] = lse
        return carry

    lax.fori_loop(0, rows // 128, attend, 0)

    edge = jnp.zeros((8, width), F32)
    padded[pl.ds(0, 8), :] = edge
    padded[pl.ds(rows + 8, 8), :] = edge
    for part in chunks(rows, 128):
        x2 = x1_out[part, :] + dot(attended_out[part, :], attn_out[...])
        x2_out[part, :] = x2
        hat, _ = normalize(x2)
        uc = (hat * gains(2)).astype(BF16)
        uc_out[part, :] = uc
        gin = dot(uc, conv_in[...])
        gin_out[part, :] = gin
        padded[pl.ds(part.start + 8, 128), :] = gin[:, :width] * sigmoid(gin[:, width:])

    sums = jnp.zeros((1, width), F32)
    squares = jnp.zeros((1, width), F32)
    for part in chunks(rows, 64):
        depth = jnp.zeros((64, width), F32)
        for tap in range(15):
            weight = table[pl.ds(6 + tap, 1), :]
            depth += weight * padded[pl.ds(part.start + tap + 1, 64), :] * taps[part, pl.ds(tap, 1)]
        depth_out[part, :] = depth
        weighted = jnp.where(seg_col[part, :] < 3, depth, 0.0)
        sums += jnp.sum(weighted, 0, keepdims=True)
        squares += jnp.sum(weighted * depth, 0, keepdims=True)
    moments[pl.ds(0, 1), :] = sums
    moments[pl.ds(1, 1), :] = squares
    moments[pl.ds(2, 6), :] = jnp.zeros((6, width), F32)


def batch_terms(moments, frame_count):
    mean = moments[pl.ds(0, 1), :] / frame_count[0]
    variance = moments[pl.ds(1, 1), :] / frame_count[0] - mean * mean
    return mean, lax.rsqrt(variance + EPSILON)


def middle_kernel(frame_count, depth, moments, x2, table, conv_out, slot_row, swish_out, x3_out, sent, normed):
    rows, width = depth.shape
    mean, scale = batch_terms(moments, frame_count)
    for part in chunks(rows, 128):
        bn = (depth[part, :] - mean) * scale * table[pl.ds(5, 1), :] + table[pl.ds(21, 1), :]
        swish = (bn * sigmoid(bn)).astype(BF16)
        swish_out[part, :] = swish
        x3 = x2[part, :] + dot(swish, conv_out[...])
        x3_out[part, :] = x3
        hat, _ = normalize(x3)
        normed[part, :] = (hat * table[pl.ds(3, 1), :]).astype(BF16)
    scatter_to(slot_row, normed[...], sent)


def turn_kernel(
    x3, blocks, slot_col, slot_row, gate, table, cotangent, seg_col,
    block_out, dx4_out, gate_grad, gain_out, sent, grads,
):
    rows, width = x3.shape
    gain = table[pl.ds(4, 1), :]
    gain_sum = jnp.zeros((1, width), F32)
    for part in chunks(rows, 128):
        found = gathered(slot_col, blocks, part)
        half = 0.5 * gate[part, :]
        x4 = x3[part, :] + half * found
        hat, inverse = normalize(x4)
        valid = seg_col[part, :] < 3
        block_out[part, :] = jnp.where(valid, hat * gain, 0.0).astype(BF16)
        grad = jnp.where(valid, cotangent[part, :].astype(F32), 0.0)
        gain_sum += jnp.sum(grad * hat, 0, keepdims=True)
        dx4 = norm_backward(grad, gain, hat, inverse)
        dx4_out[part, :] = dx4
        gate_grad[part, :] = 0.5 * jnp.sum(found * dx4, 1, keepdims=True)
        grads[part, :] = (half * dx4).astype(BF16)
    gain_out[...] = gain_sum
    scatter_to(slot_row, grads[...], sent)


def conv_back_kernel(
    frame_count, dx4, blocks, slot_col, x3, table, conv_out, depth, moments,
    dx3_out, dco_out, dh_out, sums,
):
    rows, width = x3.shape
    mean, scale = batch_terms(moments, frame_count)
    total = jnp.zeros((1, width), F32)
    moment = jnp.zeros((1, width), F32)
    shift = jnp.zeros((1, width), F32)
    gain5 = jnp.zeros((1, width), F32)
    gain3 = jnp.zeros((1, width), F32)
    for part in chunks(rows, 128):
        grad = gathered(slot_col, blocks, part)
        hat, inverse = normalize(x3[part, :])
        gain3 += jnp.sum(grad * hat, 0, keepdims=True)
        dx3 = dx4[part, :] + norm_backward(grad, table[pl.ds(3, 1), :], hat, inverse)
        dx3_out[part, :] = dx3
        dco = dx3.astype(BF16)
        dco_out[part, :] = dco
        centred = depth[part, :] - mean
        hat = centred * scale
        bn = hat * table[pl.ds(5, 1), :] + table[pl.ds(21, 1), :]
        dbn = dot_nt(dco, conv_out[...]) * slope(bn, sigmoid(bn))
        shift += jnp.sum(dbn, 0, keepdims=True)
        gain5 += jnp.sum(dbn * hat, 0, keepdims=True)
        dh = dbn * table[pl.ds(5, 1), :]
        dh_out[part, :] = dh
        total += jnp.sum(dh, 0, keepdims=True)
        moment += jnp.sum(dh * centred, 0, keepdims=True)
    for number, row in enumerate((total, moment, shift, gain5, gain3)):
        sums[pl.ds(number, 1), :] = row
    sums[pl.ds(5, 3), :] = jnp.zeros((3, width), F32)


def back_kernel(
    frame_count, dh, depth, moments, sums, dx3, gin, x2, x1, table, conv_in, attn_out, attn_in, qkv, lse,
    cosine, sine, seg_col, seg_row, taps, expert, gate, slot_row,
    dgin_out, dat_out, dproj_out, dx1_out, gate_grad, terms, sent,
    padded, glu, grad_rows, dk, dv, rows_sent,
):
    rows, width = dh.shape
    mean, scale = batch_terms(moments, frame_count)
    total, moment = sums[pl.ds(0, 1), :], sums[pl.ds(1, 1), :]
    var_grad = -0.5 * moment * scale * scale * scale
    mean_grad = -scale * total - 2.0 * mean * var_grad
    edge = jnp.zeros((8, width), F32)
    for ref in (padded, glu):
        ref[pl.ds(0, 8), :] = edge
        ref[pl.ds(rows + 8, 8), :] = edge
    for part in chunks(rows, 64):
        held = depth[part, :]
        grad = (mean_grad + 2.0 * held * var_grad) * (1.0 / frame_count[0])
        padded[pl.ds(part.start + 8, 64), :] = dh[part, :] * scale + jnp.where(seg_col[part, :] < 3, grad, 0.0)
        glu[pl.ds(part.start + 8, 64), :] = gin[part, :width] * sigmoid(gin[part, width:])
    kernel_sums = [jnp.zeros((1, width), F32) for _ in range(15)]
    gain2 = jnp.zeros((1, width), F32)
    for part in chunks(rows, 64):
        dglu = jnp.zeros((64, width), F32)
        own = padded[pl.ds(part.start + 8, 64), :]
        for tap in range(15):
            mask = taps[part, pl.ds(tap, 1)]
            dglu += table[pl.ds(20 - tap, 1), :] * padded[pl.ds(part.start + tap + 1, 64), :] * mask
            shifted = glu[pl.ds(part.start + tap + 1, 64), :]
            kernel_sums[tap] += jnp.sum(own * shifted * mask, 0, keepdims=True)
        logistic = sigmoid(gin[part, width:])
        dgin_out[part, :width] = (dglu * logistic).astype(BF16)
        dgin_out[part, width:] = (dglu * gin[part, :width] * logistic * (1.0 - logistic)).astype(BF16)
    for tap in range(15):
        terms[pl.ds(6 + tap, 1), :] = kernel_sums[tap]
    for part in chunks(rows, 128):
        grad = dot_nt(dgin_out[part, :], conv_in[...])
        hat, inverse = normalize(x2[part, :])
        gain2 += jnp.sum(grad * hat, 0, keepdims=True)
        dx2 = dx3[part, :] + norm_backward(grad, table[pl.ds(2, 1), :], hat, inverse)
        dx1_out[part, :] = dx2
        dat = dx2.astype(BF16)
        dat_out[part, :] = dat
        grad_rows[part, :] = dot_nt(dat, attn_out[...]).astype(BF16)
    terms[pl.ds(2, 1), :] = gain2

    lane = iota((1, LANES), 1)
    sides = ((lane < DH), (lane >= DH))
    zero = jnp.zeros((), BF16)
    dk[...] = jnp.zeros_like(dk)
    dv[...] = jnp.zeros_like(dv)

    def attend(part_index, carry):
        part = pl.ds(pl.multiple_of(part_index * 128, 128), 128)
        related = seg_col[part, :] == seg_row[...]
        for pair in range(width // LANES):
            own = pl.ds(pair * LANES, LANES)
            q = qkv[part, own]
            k = qkv[:, pl.ds(width + pair * LANES, LANES)]
            v = qkv[:, pl.ds(2 * width + pair * LANES, LANES)]
            da = grad_rows[part, own]
            dq = jnp.zeros((128, LANES), F32)
            for side in range(2):
                head = 2 * pair + side
                q_side = jnp.where(sides[side], q, zero)
                da_side = jnp.where(sides[side], da, zero)
                scores = dot_nt(q_side, k) - lse[part, pl.ds(head, 1)]
                probs = jnp.where(related, jnp.exp(jnp.where(related, scores, 0.0)), 0.0)
                dprobs = dot_nt(da_side, v)
                inner = jnp.sum(probs * dprobs, 1, keepdims=True)
                dscores = (probs * (dprobs - inner)).astype(BF16)
                dq += dot(dscores, jnp.where(sides[side], k, zero))
                dk[:, own] += dot_tn(dscores, q_side)
                dv[:, own] += dot_tn(probs.astype(BF16), da_side)
            dq = dq * DH**-0.5
            dproj_out[part, own] = (dq * cosine[part, :] - partner(dq) * sine[part, :]).astype(BF16)
        return carry

    lax.fori_loop(0, rows // 128, attend, 0)

    gain1 = jnp.zeros((1, width), F32)
    for part in chunks(rows, 128):
        for pair in range(width // LANES):
            own = pl.ds(pair * LANES, LANES)
            held = dk[part, own]
            dproj_out[part, pl.ds(width + pair * LANES, LANES)] = (
                held * cosine[part, :] - partner(held) * sine[part, :]
            ).astype(BF16)
            dproj_out[part, pl.ds(2 * width + pair * LANES, LANES)] = dv[part, own].astype(BF16)
        grad = dot_nt(dproj_out[part, :], attn_in[...])
        hat, inverse = normalize(x1[part, :])
        gain1 += jnp.sum(grad * hat, 0, keepdims=True)
        dx1 = dx1_out[part, :] + norm_backward(grad, table[pl.ds(1, 1), :], hat, inverse)
        dx1_out[part, :] = dx1
        gate_grad[part, :] = 0.5 * jnp.sum(expert[part, :].astype(F32) * dx1, 1, keepdims=True)
        rows_sent[part, :] = (0.5 * gate[part, :] * dx1).astype(BF16)
    terms[pl.ds(1, 1), :] = gain1
    scatter_to(slot_row, rows_sent[...], sent)


def final_kernel(frames, blocks, slot_col, table, dx1, dz, embed_weight, out):
    for part in chunks(frames.shape[0], 128):
        grad = gathered(slot_col, blocks, part)
        hat, inverse = normalize(frames[part, :].astype(F32))
        dx0 = dx1[part, :] + norm_backward(grad, table[pl.ds(0, 1), :], hat, inverse)
        out[part, :] = dx0 + dot_nt(dz[part, :], embed_weight[...])


def after(value, *others):
    return lax.optimization_barrier((value,) + others)[0]


def shards(
    frames,
    lengths,
    choice_first,
    choice_second,
    embed_weight,
    routers,
    norm_gains,
    attn_in,
    attn_out,
    conv_in,
    conv_kernel,
    bn_shift,
    conv_out,
    expert_in,
    expert_out,
    cotangent,
):
    rows, width = frames.shape
    layers, slice_width, experts = routers.shape
    taps = conv_kernel.shape[0]
    gains = norm_gains.shape[0]
    peers = lax.axis_size("expert")
    dp_count = lax.axis_size("dp")
    dp_bits = bit_count(("dp",))
    capacity = 2 * rows // experts
    hidden = expert_in.shape[3]
    device = lax.axis_index(AXES)
    block = shaped((capacity, width), BF16)
    wide = shaped((rows, width), F32)
    low = shaped((rows, width), BF16)
    column = shaped((rows, 1), F32)

    dp_index = lax.axis_index("dp")[None]

    def shard_of(layer):
        first = expert_in[layer, 0]
        tiles = [first[:, start : start + width] for start in range(0, hidden, width)]
        return jnp.concatenate([expert_out[layer, 0]] + tiles, 0)

    first_weights = lax.all_gather(shard_of(0), "dp", axis=0)
    sent, slot_col1, slot_row1, slot_col2, slot_row2 = call(
        start_kernel,
        ([block] * peers, shaped((rows, 1), I32), shaped((1, rows), I32), shaped((rows, 1), I32), shaped((1, rows), I32)),
        lax.axis_index("expert")[None],
        frames,
        choice_first,
        choice_first.reshape(1, rows),
        choice_second,
        choice_second.reshape(1, rows),
        specs=[SMEM] + [None] * 5,
    )
    first_blocks = swap_blocks(sent)

    small_width = gains + taps + 1 + layers * experts
    small = jnp.concatenate(
        [
            norm_gains.T,
            conv_kernel.T,
            bn_shift[:, None],
            jnp.moveaxis(routers, 1, 0).reshape(slice_width, -1),
            jnp.zeros((slice_width, -small_width % LANES), BF16),
        ],
        1,
    )
    small_all = gather_everywhere(small).reshape(width, LANES).astype(F32)
    table = small_all[:, : gains + taps + 3].T
    router_table = jnp.pad(
        small_all[:, gains + taps + 1 : small_width], ((0, 0), (0, LANES - layers * experts))
    )
    dense = after(jnp.concatenate([attn_in, attn_out, conv_in, conv_out], 1), small_all, *first_blocks)
    dense = lax.all_to_all(
        jnp.broadcast_to(dense[None], (peers,) + dense.shape), "expert", split_axis=0, concat_axis=0, tiled=True
    )
    dense = lax.all_gather(
        dense.reshape(peers * slice_width, 7 * width), "dp", axis=0, tiled=True
    )
    second_weights = lax.all_gather(shard_of(1), "dp", axis=0)

    own_lengths = lax.dynamic_index_in_dim(lengths, device, 0, keepdims=False)
    frame_count = jnp.sum(lengths[:, :-1]).astype(F32)[None]
    (embed_pre, embedded, probs, gate1, gate2, seg_col, seg_row, tap_masks, offsets) = call(
        functools.partial(embed_kernel, experts),
        [
            wide,
            wide,
            shaped((rows, LANES), F32),
            column,
            column,
            shaped((rows, 1), I32),
            shaped((1, rows), I32),
            shaped((rows, LANES), F32),
            column,
        ],
        jnp.cumsum(own_lengths, dtype=I32)[:-1],
        frames,
        embed_weight,
        router_table,
        choice_first,
        choice_second,
        specs=[SMEM] + [None] * 5,
    )
    half = DH // 2
    frequency = 10000.0 ** (-jnp.arange(half, dtype=F32) / half)
    angles = offsets * jnp.tile(frequency, LANES // half)[None, :]
    sign = jnp.asarray(np.where(np.arange(LANES) % DH < half, -1.0, 1.0), F32)
    cosine, sine = jnp.cos(angles), jnp.sin(angles) * sign[None, :]

    def gain(number):
        return table[number : number + 1]

    first_results = swap_blocks(
        [expert_forward(block, gain(0), first_weights, hidden, True) for block in first_blocks]
    )

    def dense_spec(columns, start):
        return pl.BlockSpec((width, columns), lambda i: (0, start // columns))

    attn_in_spec = dense_spec(3 * width, 0)
    attn_out_spec = dense_spec(width, 3 * width)
    conv_in_spec = dense_spec(2 * width, 4 * width)
    conv_out_spec = dense_spec(width, 6 * width)
    sums_shape = shaped((8, width), F32)
    padded = pltpu.VMEM((rows + 16, width), F32)

    first_expert, x1, x2, ua, qkv, lse, attended, uc, gin, depth, moments = call(
        front_kernel,
        [
            low,
            wide,
            wide,
            low,
            shaped((rows, 3 * width), BF16),
            shaped((rows, LANES), F32),
            low,
            low,
            shaped((rows, 2 * width), F32),
            wide,
            sums_shape,
        ],
        frames,
        first_results,
        slot_col1,
        gate1,
        table,
        dense,
        dense,
        dense,
        cosine,
        sine,
        seg_col,
        seg_row,
        tap_masks,
        specs=[None] * 5 + [attn_in_spec, attn_out_spec, conv_in_spec] + [None] * 5,
        scratch=[padded],
    )
    moments = sum_everywhere(moments)
    swish, x3, sent = call(
        middle_kernel,
        (low, wide, [block] * peers),
        frame_count,
        depth,
        moments,
        x2,
        table,
        dense,
        slot_row2,
        specs=[SMEM] + [None] * 4 + [conv_out_spec, None],
        scratch=[pltpu.VMEM((rows, width), BF16)],
    )

    second_blocks = swap_blocks(sent)
    second_results = swap_blocks(
        [expert_forward(block, gain(3), second_weights, hidden, False) for block in second_blocks]
    )
    block_out, dx4, gate_grad2, gain4, sent = call(
        turn_kernel,
        (low, wide, column, shaped((1, width), F32), [block] * peers),
        x3,
        second_results,
        slot_col2,
        slot_row2,
        gate2,
        table,
        cotangent,
        seg_col,
        scratch=[pltpu.VMEM((rows, width), BF16)],
    )
    second_grads = swap_blocks(sent)
    backs = [
        expert_backward(block, grad, gain(3), second_weights, hidden, False)
        for block, grad in zip(second_blocks, second_grads)
    ]
    back, hid, pre_grads, inputs, _ = zip(*backs)
    second_back = swap_blocks(back)
    (second_grad,) = weight_grads(
        dp_index, inputs, second_grads, hid, pre_grads, dp_count, False
    )
    second_back[1] = after(second_back[1], second_grad)
    second_own = lax.psum_scatter(second_grad, "dp", scatter_dimension=0, tiled=True)[0]

    dx3, dco, dh, sums = call(
        conv_back_kernel,
        [wide, low, wide, sums_shape],
        frame_count,
        dx4,
        second_back,
        slot_col2,
        x3,
        table,
        dense,
        depth,
        moments,
        specs=[SMEM] + [None] * 5 + [conv_out_spec] + [None] * 2,
    )
    all_sums = sum_everywhere(sums)
    dgin, dat, dproj, dx1, gate_grad1, terms, sent = call(
        back_kernel,
        (
            shaped((rows, 2 * width), BF16),
            low,
            shaped((rows, 3 * width), BF16),
            wide,
            column,
            shaped((24, width), F32),
            [block] * peers,
        ),
        frame_count,
        dh,
        depth,
        moments,
        all_sums,
        dx3,
        gin,
        x2,
        x1,
        table,
        dense,
        dense,
        dense,
        qkv,
        lse,
        cosine,
        sine,
        seg_col,
        seg_row,
        tap_masks,
        first_expert,
        gate1,
        slot_row1,
        specs=[SMEM] + [None] * 9 + [conv_in_spec, attn_out_spec, attn_in_spec] + [None] * 10,
        scratch=[padded, padded, pltpu.VMEM((rows, width), BF16), pltpu.VMEM((rows, width), F32), pltpu.VMEM((rows, width), F32), pltpu.VMEM((rows, width), BF16)],
    )
    first_grads = swap_blocks(sent)

    dense_terms, dz, router_terms = call(
        functools.partial(dense_grad_kernel, experts),
        (shaped((width, 8 * width), BF16), low, shaped((LANES, width), F32)),
        ua,
        dproj,
        attended,
        dat,
        uc,
        dgin,
        swish,
        dco,
        gate_grad1,
        gate1,
        choice_first,
        gate_grad2,
        gate2,
        choice_second,
        probs,
        router_table,
        embed_pre,
        embedded,
        frames,
        scratch=[pltpu.VMEM((rows, LANES), F32)],
    )
    dense_own = sum_to_owners(dense_terms.reshape(dp_count, -1, 8 * width), "dp").astype(BF16)
    dense_own = sum_to_owners(dense_own.reshape(peers, slice_width, 8 * width), "expert")
    embed_total = gather_everywhere(dense_own[:, 7 * width :].astype(BF16))
    embed_total = embed_total.reshape(width, width).astype(F32)

    first_grads[1] = after(first_grads[1], dense_terms)
    backs = [
        expert_backward(block, grad, gain(0), first_weights, hidden, True)
        for block, grad in zip(first_blocks, first_grads)
    ]
    back, hid, pre_grads, inputs, gain0 = zip(*backs)
    gain0 = sum(gain0)
    first_back = swap_blocks(back)
    kept, moved = weight_grads(dp_index, inputs, first_grads, hid, pre_grads, dp_count, True)
    moved = after(moved, *first_back[1:])

    def dp_exchange(values, mask):
        return lax.ppermute(values, "dp", [(i, i ^ mask) for i in range(dp_count)])

    pair_sum = (kept.astype(F32) + dp_exchange(moved, 1).astype(F32)).astype(BF16)
    first_own = pair_sum[0].astype(F32)
    for number, mask in enumerate(chip_masks()):
        if mask:
            first_own = first_own + dp_exchange(pair_sum[number], mask).astype(F32)

    small_terms = jnp.concatenate(
        [
            gain0,
            terms[1:3],
            sums[4:5],
            gain4,
            sums[3:4],
            terms[6 : 6 + taps],
            sums[2:3],
            router_terms[: layers * experts],
        ],
        0,
    )
    small_terms = jnp.pad(small_terms.T, ((0, 0), (0, LANES - small_width)))
    small_sums = sum_to_owners(small_terms.reshape(-1, slice_width, LANES), AXES).T
    frames_grad = call(
        final_kernel,
        wide,
        frames,
        first_back,
        slot_col1,
        table,
        dx1,
        dz,
        embed_weight,
    )
    def matrices(own):
        half = own.shape[0] // 2
        first = jnp.concatenate(jnp.split(own[half:], hidden // width, 0), 1)
        return first, own[:half]

    first_pair, second_pair = matrices(first_own), matrices(second_own.astype(F32))
    return (
        block_out,
        frames_grad,
        embed_total,
        jnp.moveaxis(
            small_sums[gains + taps + 1 : small_width].reshape(layers, experts, slice_width), 1, 2
        ),
        small_sums[:gains],
        dense_own[:, : 3 * width],
        dense_own[:, 3 * width : 4 * width],
        dense_own[:, 4 * width : 6 * width],
        small_sums[gains : gains + taps],
        small_sums[gains + taps],
        dense_own[:, 6 * width : 7 * width],
        jnp.stack([first_pair[0], second_pair[0]])[:, None],
        jnp.stack([first_pair[1], second_pair[1]])[:, None],
    )


def solution(mesh):
    in_specs = (
        P(("dp", "expert"), None),
        P(),
        P(("dp", "expert"), None),
        P(("dp", "expert"), None),
        P(),
        P(None, ("dp", "expert"), None),
        P(None, ("dp", "expert")),
        P(("dp", "expert"), None),
        P(("dp", "expert"), None),
        P(("dp", "expert"), None),
        P(None, ("dp", "expert")),
        P(("dp", "expert")),
        P(("dp", "expert"), None),
        P(None, "expert", "dp", None),
        P(None, "expert", "dp", None),
        P(("dp", "expert"), None),
    )
    out_specs = (
        P(("dp", "expert"), None),
        P(("dp", "expert"), None),
        P(),
        P(None, ("dp", "expert"), None),
        P(None, ("dp", "expert")),
        P(("dp", "expert"), None),
        P(("dp", "expert"), None),
        P(("dp", "expert"), None),
        P(None, ("dp", "expert")),
        P(("dp", "expert")),
        P(("dp", "expert"), None),
        P(None, "expert", "dp", None),
        P(None, "expert", "dp", None),
    )
    return jax.shard_map(shards, mesh=mesh, in_specs=in_specs, out_specs=out_specs, check_vma=False)
```

```python
import functools

import jax
import jax.numpy as jnp
import numpy as np
from jax import lax
from jax.experimental import pallas as pl
from jax.experimental.pallas import tpu as pltpu
from jax.sharding import PartitionSpec as P

H = 8
DH = 64
LANES = 128

EPSILON = 1e-05
MASK_FILL = 1000000000.0
HIGHEST = lax.Precision.HIGHEST
AXES = ("dp", "expert")
BF16 = jnp.bfloat16
F32 = jnp.float32
I32 = jnp.int32
MIB = 1 << 20


def bit_count(axes):
    total = 1
    for name in axes:
        total *= lax.axis_size(name)
    return total.bit_length() - 1


def exchange(values, axes, mask):
    total = 1 << bit_count(axes)
    return lax.ppermute(values, axes, [(i, i ^ mask) for i in range(total)])


def device_groups():
    z_bits = bit_count(("expert",))
    dp_bits = bit_count(("dp",))
    chips = list(range(z_bits + 1, z_bits + dp_bits))
    rests = [chips, list(range(z_bits))]
    return [[z_bits]] + [bits[i : i + 2] for bits in rests for i in range(0, len(bits), 2)]


def masks_of(bits):
    if len(bits) == 1:
        return [1 << bits[0]]
    low, high = 1 << bits[0], 1 << bits[1]
    return [low, high, low | high]


def sum_everywhere(values):
    for bits in device_groups():
        arrived = [exchange(values, AXES, mask) for mask in masks_of(bits)]
        if len(arrived) == 1:
            values = values + arrived[0]
        else:
            values = (values + arrived[0]) + (arrived[1] + arrived[2])
    return values


def gather_everywhere(values):
    total = 1 << bit_count(AXES)
    sent = jnp.broadcast_to(values[None], (total,) + values.shape)
    return lax.all_to_all(sent, AXES, split_axis=0, concat_axis=0, tiled=True)


def sum_to_owners(values, axes):
    arrived = lax.all_to_all(values, axes, split_axis=0, concat_axis=0, tiled=True)
    return jnp.sum(arrived.astype(F32), 0)


def swap_blocks(blocks):
    total = lax.axis_size("expert")
    moved = [blocks[0]]
    for k in range(1, total):
        moved.append(lax.ppermute(blocks[k], "expert", [(i, i ^ k) for i in range(total)]))
    return moved


def chip_masks():
    return [core << 1 for core in range(lax.axis_size("dp") // 2)]


class Columns:
    def __init__(self, array, start, count):
        self.array, self.start, self.count = array, start, count


class Stream:
    def __init__(self, arrivals, results):
        self.arrivals, self.results = arrivals, results
        self.waited, self.sent = set(), []
        self.begin(0)
        self.begin(1)

    def begin(self, stage):
        for copy in self.arrivals.get(stage, ()):
            copy.start()

    def ready(self, stage):
        for copy in self.arrivals.get(stage, ()):
            copy.wait()
        self.waited.add(stage)
        self.begin(stage + 2)

    def flush(self, *refs):
        for ref in refs:
            copy = self.results[id(ref)]
            copy.start()
            self.sent.append(copy)

    def finish(self):
        for copy in self.sent:
            copy.wait()


def call(body, outs, *args, specs=None, out_specs=None, scratch=(), stages=None, vmem=60, cost=5, **kw):
    vmem_spec = pl.BlockSpec(memory_space=pltpu.VMEM)
    any_spec = pl.BlockSpec(memory_space=pl.ANY)
    if specs is None:
        specs = [None] * len(args)
    columns = [arg if isinstance(arg, Columns) else None for arg in args]
    args = [arg.array if isinstance(arg, Columns) else arg for arg in args]
    grid = kw.pop("grid", (1,))
    scratch = list(scratch)
    if stages is None:
        specs = [
            jax.tree.map(lambda _: vmem_spec, arg) if spec is None else spec
            for spec, arg in zip(specs, args)
        ]
        if out_specs is None:
            out_specs = jax.tree.map(lambda _: vmem_spec, outs)
        wrapped = body
    else:
        specs = [
            spec if spec is not None else jax.tree.map(lambda _: vmem_spec if stage is None else any_spec, arg)
            for spec, arg, stage in zip(specs, args, stages)
        ]
        out_specs = jax.tree.map(lambda _: any_spec, outs)
        buffers = []
        for arg, part, stage in zip(args, columns, stages):
            if stage is not None:
                for leaf in jax.tree.leaves(arg):
                    shape = leaf.shape if part is None else (leaf.shape[0], part.count)
                    buffers.append(pltpu.VMEM(shape, leaf.dtype))
        out_leaves, out_tree = jax.tree.flatten(outs)
        buffers += [pltpu.VMEM(leaf.shape, leaf.dtype) for leaf in out_leaves]
        own_scratch, total = len(scratch), len(buffers)
        scratch = scratch + buffers + [pltpu.SemaphoreType.DMA((total,))]

        def wrapped(*refs):
            refs = list(refs)
            ins, out_refs, rest = refs[: len(args)], refs[len(args) : len(args) + out_count], refs[len(args) + out_count :]
            own, held, sems = rest[:own_scratch], rest[own_scratch:-1], rest[-1]
            arrivals, given, used = {}, [], 0
            for ref, part, stage in zip(ins, columns, stages):
                if stage is None:
                    given.append(ref)
                    continue
                leaves, tree = jax.tree.flatten(ref)
                landed = []
                for leaf in leaves:
                    source = leaf if part is None else leaf.at[:, pl.ds(part.start, part.count)]
                    arrivals.setdefault(stage, []).append(
                        pltpu.make_async_copy(source, held[used], sems.at[used])
                    )
                    landed.append(held[used])
                    used += 1
                given.append(jax.tree.unflatten(tree, landed))
            results, places = {}, []
            for ref in jax.tree.leaves(out_refs):
                results[id(held[used])] = pltpu.make_async_copy(held[used], ref, sems.at[used])
                places.append(held[used])
                used += 1
            stream = Stream(arrivals, results)
            given_outs = jax.tree.unflatten(out_tree, places)
            given_outs = list(given_outs) if isinstance(given_outs, (tuple, list)) else [given_outs]
            body(stream, *given, *given_outs, *own)
            stream.finish()

        out_count = len(outs) if isinstance(outs, (tuple, list)) else 1
    return pl.pallas_call(
        wrapped,
        out_shape=outs,
        in_specs=specs,
        out_specs=out_specs,
        scratch_shapes=scratch,
        grid=grid,
        compiler_params=pltpu.CompilerParams(vmem_limit_bytes=vmem * MIB),
        cost_estimate=pl.CostEstimate(flops=cost * 1153 * 10**6, bytes_accessed=0, transcendentals=0),
        **kw,
    )(*args)


def shaped(shape, dtype):
    return jax.ShapeDtypeStruct(shape, dtype)


SMEM = pl.BlockSpec(memory_space=pltpu.SMEM)
ANY = pl.BlockSpec(memory_space=pl.ANY)


def dot(left, right):
    return lax.dot_general(left, right, (((1,), (0,)), ((), ())), preferred_element_type=F32)


def dot_nt(left, right):
    return lax.dot_general(left, right, (((1,), (1,)), ((), ())), preferred_element_type=F32)


def dot_tn(left, right):
    return lax.dot_general(left, right, (((0,), (0,)), ((), ())), preferred_element_type=F32)


def iota(shape, dim):
    return lax.broadcasted_iota(I32, shape, dim)


def normalize(rows):
    centred = rows - jnp.mean(rows, -1, keepdims=True)
    inverse = lax.rsqrt(jnp.mean(centred * centred, -1, keepdims=True) + EPSILON)
    return centred * inverse, inverse


def norm_backward(grad, gain, hat, inverse):
    scaled = grad * gain
    return inverse * (
        scaled
        - jnp.mean(scaled, -1, keepdims=True)
        - hat * jnp.mean(scaled * hat, -1, keepdims=True)
    )


def sigmoid(values):
    return 1.0 / (1.0 + jnp.exp(-values))


def slope(values, logistic):
    return logistic * (1.0 + values * (1.0 - logistic))


def chunks(total, size):
    return [pl.ds(start, size) for start in range(0, total, size)]


def gathered(slot_col, blocks, rows):
    slot = slot_col[rows, :]
    total = None
    for k, block in enumerate(blocks):
        capacity = block.shape[0]
        pick = (slot == iota((slot.shape[0], capacity), 1) + k * capacity).astype(F32).astype(BF16)
        part = dot(pick, block[...])
        total = part if total is None else total + part
    return total


def scatter_to(slot_row, values, outs):
    for k, out in enumerate(outs):
        capacity = out.shape[0]
        pick = (slot_row[...] == iota((capacity, slot_row.shape[1]), 0) + k * capacity)
        out[...] = dot(pick.astype(F32).astype(BF16), values).astype(BF16)


def start_kernel(own, frames, col1, row1, col2, row2, sent, slot_col1, slot_row1, slot_col2, slot_row2):
    rows = frames.shape[0]
    capacity = sent[0].shape[0]
    below = (iota((rows, rows), 0) > iota((rows, rows), 1)).astype(F32).astype(BF16)
    above = (iota((rows, rows), 0) < iota((rows, rows), 1)).astype(F32).astype(BF16)
    for col, row, out_col, out_row in (
        (col1, row1, slot_col1, slot_row1),
        (col2, row2, slot_col2, slot_row2),
    ):
        hot = (col[...] == iota((rows, LANES), 1)).astype(F32)
        rank = jnp.sum(dot(below, hot.astype(BF16)) * hot, 1, keepdims=True)
        out_col[...] = (col[...] ^ own[0]) * capacity + rank.astype(I32)
        hot = (row[...] == iota((16, rows), 0)).astype(F32)
        rank = jnp.sum(dot(hot.astype(BF16), above) * hot, 0, keepdims=True)
        out_row[...] = (row[...] ^ own[0]) * capacity + rank.astype(I32)
    scatter_to(slot_row1, frames[...], sent)


def expert_specs(weights, hidden, tile):
    count, rows, width = weights.shape
    half = rows // 2
    in_rows = width // count
    first = pl.BlockSpec((count, in_rows, tile), lambda j: (0, half // in_rows + j, 0))
    second = pl.BlockSpec((tile // half, half, width), lambda j: (j, 0, 0))
    return first, second


def flat(ref):
    count, rows, width = ref.shape
    return ref[...].reshape(count * rows, width)


def expert_forward_kernel(with_norm, block, gain, w_in, w_out, out, total, inputs):
    step = pl.program_id(0)

    @pl.when(step == 0)
    def _():
        if with_norm:
            hat, _ = normalize(block[...].astype(F32))
            inputs[...] = (hat * gain[...]).astype(BF16)
        else:
            inputs[...] = block[...]
        total[...] = jnp.zeros_like(total)

    pre = dot(inputs[...], flat(w_in))
    hidden = (pre * sigmoid(pre)).astype(BF16)
    total[...] += dot(hidden, flat(w_out))

    @pl.when(step == pl.num_programs(0) - 1)
    def _():
        out[...] = total[...].astype(BF16)


def expert_forward(block, gain, weights, hidden, with_norm, tile=512):
    capacity, width = block.shape
    first, second = expert_specs(weights, hidden, tile)
    whole = pl.BlockSpec((capacity, width), lambda j: (0, 0))
    return call(
        functools.partial(expert_forward_kernel, with_norm),
        shaped((capacity, width), BF16),
        block,
        gain,
        weights,
        weights,
        specs=[whole, pl.BlockSpec((1, width), lambda j: (0, 0)), first, second],
        out_specs=whole,
        scratch=[pltpu.VMEM((capacity, width), F32), pltpu.VMEM((capacity, width), BF16)],
        grid=(hidden // tile,),
        vmem=12,
        cost=8,
    )


def expert_backward_kernel(
    with_norm, block, grad, gain, w_in, w_out, out, hidden_out, pre_grad_out, input_out, gain_out, total, hats
):
    step = pl.program_id(0)

    @pl.when(step == 0)
    def _():
        if with_norm:
            hat, _ = normalize(block[...].astype(F32))
            hats[...] = hat
            input_out[...] = (hat * gain[...]).astype(BF16)
        else:
            input_out[...] = block[...]
        total[...] = jnp.zeros_like(total)

    first, second = flat(w_in), flat(w_out)
    pre = dot(input_out[...], first)
    logistic = sigmoid(pre)
    hidden_out[...] = (pre * logistic).astype(BF16)
    hidden_grad = dot_nt(grad[...], second)
    pre_grad = (hidden_grad * slope(pre, logistic)).astype(BF16)
    pre_grad_out[...] = pre_grad
    total[...] += dot_nt(pre_grad, first)

    @pl.when(step == pl.num_programs(0) - 1)
    def _():
        back = total[...].astype(BF16)
        out[...] = back
        if with_norm:
            gain_out[...] = jnp.sum(back.astype(F32) * hats[...], 0, keepdims=True)
        else:
            gain_out[...] = jnp.zeros_like(gain_out)


def expert_backward(block, grad, gain, weights, hidden, with_norm, tile=512):
    capacity, width = block.shape
    first, second = expert_specs(weights, hidden, tile)
    whole = pl.BlockSpec((capacity, width), lambda j: (0, 0))
    tiled = pl.BlockSpec((capacity, tile), lambda j: (0, j))
    one = pl.BlockSpec((1, width), lambda j: (0, 0))
    return call(
        functools.partial(expert_backward_kernel, with_norm),
        (
            shaped((capacity, width), BF16),
            shaped((capacity, hidden), BF16),
            shaped((capacity, hidden), BF16),
            shaped((capacity, width), BF16),
            shaped((1, width), F32),
        ),
        block,
        grad,
        gain,
        weights,
        weights,
        specs=[whole, whole, one, first, second],
        out_specs=(whole, tiled, tiled, whole, one),
        scratch=[pltpu.VMEM((capacity, width), F32), pltpu.VMEM((capacity, width), F32)],
        grid=(hidden // tile,),
        vmem=16,
        cost=20,
    )


def weight_grad_kernel(relative, dp_index, inputs, grads, hidden, pre_grads, *refs):
    outs, (first, second) = refs[:-2], refs[-2:]
    step = pl.program_id(0)
    first_sum = second_sum = None
    for block, grad, hid, pre_grad in zip(inputs, grads, hidden, pre_grads):
        part = dot_tn(block[...], pre_grad[...])
        first_sum = part if first_sum is None else first_sum + part
        part = dot_tn(hid[...], grad[...])
        second_sum = part if second_sum is None else second_sum + part
    count = sum(out.shape[0] for out in outs)
    half = outs[0].shape[1] // 2
    in_rows = first_sum.shape[0] // count
    tile = second_sum.shape[0]
    owners = tile // half
    place = pl.ds(pl.multiple_of(half + step * in_rows, in_rows), in_rows)
    if not relative:
        for device in range(count):
            outs[0][device, place, :] = first_sum[device * in_rows : (device + 1) * in_rows].astype(BF16)
        for number in range(owners):
            outs[0][step * owners + number, pl.ds(0, half), :] = second_sum[
                number * half : (number + 1) * half
            ].astype(BF16)
    else:
        first[...] = first_sum.astype(BF16)
        for number in range(count):
            source = pl.multiple_of((dp_index[0] ^ number) * in_rows, in_rows)
            outs[number % 2][number // 2, place, :] = first[pl.ds(source, in_rows), :]
        second[...] = second_sum.astype(BF16)
        for number in range(owners):
            owner = (step * owners + number) ^ dp_index[0]

            @pl.when(owner % 2 == 0)
            def _():
                outs[0][owner // 2, pl.ds(0, half), :] = second[pl.ds(number * half, half), :]

            @pl.when(owner % 2 == 1)
            def _():
                outs[1][owner // 2, pl.ds(0, half), :] = second[pl.ds(number * half, half), :]


def weight_grads(dp_index, inputs, grads, hidden, pre_grads, count, relative, tile=512):
    capacity, width = inputs[0].shape
    units = hidden[0].shape[1]
    whole = pl.BlockSpec((capacity, width), lambda j: (0, 0))
    tiled = pl.BlockSpec((capacity, tile), lambda j: (0, j))
    rows = 2 * units // count
    if relative:
        outs = (shaped((count // 2, rows, width), BF16),) * 2
    else:
        outs = (shaped((count, rows, width), BF16),)
    peers = len(inputs)
    return call(
        functools.partial(weight_grad_kernel, relative),
        outs,
        dp_index,
        list(inputs),
        list(grads),
        list(hidden),
        list(pre_grads),
        specs=[SMEM, [whole] * peers, [whole] * peers, [tiled] * peers, [tiled] * peers],
        out_specs=tuple(pl.BlockSpec(o.shape, lambda j: (0, 0, 0)) for o in outs),
        scratch=[pltpu.VMEM((width, tile), BF16), pltpu.VMEM((tile, width), BF16)],
        grid=(units // tile,),
        vmem=28,
        cost=8,
    )


def dense_grad_kernel(
    experts, stream, ua, dproj, attended, dat, uc, dgin, swish, dco, gate_grad1, gate1, col1, gate_grad2, gate2, col2,
    probs, routers, pre, embedded, frames, out, dz, router_terms, logits,
):
    width = ua.shape[1]
    rows = frames.shape[0]
    stream.ready(0)
    stream.ready(1)
    start = 0
    for left, right in ((ua, dproj), (attended, dat)):
        for column in range(0, right.shape[1], width):
            out[:, pl.ds(start, width)] = dot_tn(left[...], right[:, pl.ds(column, width)]).astype(BF16)
            start += width
    stream.ready(2)
    for part in chunks(rows, 256):
        lane = iota((256, LANES), 1)
        grad = jnp.zeros((256, LANES), F32)
        for number, (gate_grad, gate, col) in enumerate(((gate_grad1, gate1, col1), (gate_grad2, gate2, col2))):
            inside = (lane >= number * experts) & (lane < (number + 1) * experts)
            hot = (lane == col[part, :] + number * experts).astype(F32)
            scale = gate_grad[part, :] * gate[part, :]
            grad = jnp.where(inside, scale * (hot - probs[part, :]), grad)
        logits[part, :] = grad
        demb = lax.dot_general(
            grad, routers[...], (((1,), (1,)), ((), ())), precision=HIGHEST, preferred_element_type=F32
        )
        held = pre[part, :]
        dz[part, :] = (demb * slope(held, sigmoid(held))).astype(BF16)
    router_terms[...] = lax.dot_general(
        logits[...], embedded[...], (((0,), (0,)), ((), ())), precision=HIGHEST, preferred_element_type=F32
    )
    stream.flush(dz, router_terms)
    for left, right in ((uc, dgin), (swish, dco), (frames, dz)):
        for column in range(0, right.shape[1], width):
            out[:, pl.ds(start, width)] = dot_tn(left[...], right[:, pl.ds(column, width)]).astype(BF16)
            start += width
    stream.flush(out)


def dense_out_kernel(arrived, *outs):
    start = 0
    for out in outs:
        lanes = pl.ds(start, out.shape[1])
        total = arrived[0, :, lanes].astype(F32)
        for number in range(1, arrived.shape[0]):
            total = total + arrived[number, :, lanes].astype(F32)
        out[...] = total.astype(out.dtype)
        start += out.shape[1]


def embed_kernel(experts, ends, frames, weight, routers, col1, col2, pre_out, embedded_out, probs_out, gate1, gate2, seg_col, seg_row, taps_out, offset_out):
    rows = frames.shape[0]
    for part in chunks(rows, 256):
        pre = dot(frames[part, :], weight[...])
        pre_out[part, :] = pre
        embedded = pre * sigmoid(pre)
        embedded_out[part, :] = embedded
        logits = jnp.dot(embedded, routers[...], precision=HIGHEST, preferred_element_type=F32)
        lane = iota(logits.shape, 1)
        probs = jnp.zeros_like(logits)
        for number, (col, gate) in enumerate(((col1, gate1), (col2, gate2))):
            inside = (lane >= number * experts) & (lane < (number + 1) * experts)
            top = jnp.max(jnp.where(inside, logits, -MASK_FILL), 1, keepdims=True)
            weights = jnp.where(inside, jnp.exp(jnp.where(inside, logits - top, 0.0)), 0.0)
            own = weights / jnp.sum(weights, 1, keepdims=True)
            hot = lane == col[part, :] + number * experts
            gate[part, :] = jnp.sum(jnp.where(hot, own, 0.0), 1, keepdims=True)
            probs = probs + own
        probs_out[part, :] = probs

    def segment_of(place):
        found = jnp.zeros(place.shape, I32)
        for number in range(3):
            found += (place >= ends[number]).astype(I32)
        return found

    segment = segment_of(iota((rows, 1), 0))
    seg_col[...] = segment
    seg_row[...] = segment_of(iota((1, rows), 1))
    place = iota((rows, LANES), 0) + iota((rows, LANES), 1) - 7
    same = (segment_of(place) == segment) & (place >= 0) & (place < rows)
    taps_out[...] = same.astype(F32)
    first = jnp.zeros((rows, 1), I32)
    for number in range(3):
        first = jnp.where(segment > number, ends[number], first)
    offset_out[...] = (iota((rows, 1), 0) - first).astype(F32)


def partner(values):
    half = DH // 2
    lane = iota(values.shape, 1)
    return jnp.where(lane % DH < half, pltpu.roll(values, LANES - half, 1), pltpu.roll(values, half, 1))


def shifts(padded, part):
    size = part.size
    for offset in range(8):
        held = padded[pl.ds(part.start + offset, size + 8), :]
        if offset:
            yield offset - 1, held[:size]
        yield offset + 7, held[8:]


def folded(values):
    return jnp.sum(values.reshape(-1, 8, values.shape[1]), 0)


def front_kernel(
    stream, frames, blocks, slot_col, gate, table, attn_in, attn_out, conv_in, cosine, sine, seg_col, seg_row, taps,
    expert_out, x1_out, x2_out, ua_out, qkv_out, lse_out, attended_out, uc_out, gin_out, depth_out, moments,
    padded, flipped,
):
    rows, width = frames.shape
    gains = lambda n: table[pl.ds(n, 1), :]
    stream.ready(0)
    for part in chunks(rows, 256):
        found = gathered(slot_col, blocks, part)
        expert_out[part, :] = found.astype(BF16)
        x1 = frames[part, :].astype(F32) + 0.5 * gate[part, :] * found
        x1_out[part, :] = x1
        hat, _ = normalize(x1)
        ua_out[part, :] = (hat * gains(1)).astype(BF16)
    stream.flush(expert_out, x1_out, ua_out)
    stream.ready(1)
    for part in chunks(rows, 256):
        ua = ua_out[part, :]
        for piece in range(3 * width // LANES):
            lanes = pl.ds(piece * LANES, LANES)
            if piece % 2 == 0:
                pair = dot(ua, attn_in[:, pl.ds(piece * LANES, 2 * LANES)])
            values = pair[:, :LANES] if piece % 2 == 0 else pair[:, LANES:]
            if piece < 2 * width // LANES:
                values = values * cosine[part, :] + partner(values) * sine[part, :]
            if piece < width // LANES:
                values = values * DH**-0.5
            qkv_out[part, lanes] = values.astype(BF16)

    stream.flush(qkv_out)
    zero = jnp.zeros((), BF16)
    sides = tuple((iota((1, LANES), 1) < DH) == (side == 0) for side in range(2))
    turned = tuple((iota((LANES, 1), 0) < DH) == (side == 0) for side in range(2))
    for pair in range(width // LANES):
        flipped[pl.ds(pair * LANES, LANES), :] = qkv_out[:, pl.ds(2 * width + pair * LANES, LANES)].T

    def attend(part_index, carry):
        part = pl.ds(pl.multiple_of(part_index * 512, 512), 512)
        related = seg_col[...] == seg_row[:, part]
        for pair in range(width // LANES):
            q = qkv_out[part, pl.ds(pair * LANES, LANES)]
            k = qkv_out[:, pl.ds(width + pair * LANES, LANES)]
            v = flipped[pl.ds(pair * LANES, LANES), :]
            result = jnp.zeros((LANES, 512), F32)
            for side in range(2):
                scores = dot_nt(k, jnp.where(sides[side], q, zero))
                scores = jnp.where(related, scores, -MASK_FILL)
                top = jnp.max(scores, 0, keepdims=True)
                weights = jnp.exp(scores - top)
                summed = jnp.sum(weights, 0, keepdims=True)
                probs = (weights * (1.0 / summed)).astype(BF16)
                result += dot(jnp.where(turned[side], v, zero), probs)
                lse_out[pl.ds(2 * pair + side, 1), part] = top + jnp.log(summed)
            attended_out[part, pl.ds(pair * LANES, LANES)] = result.T.astype(BF16)
        return carry

    lax.fori_loop(0, rows // 512, attend, 0)
    stream.flush(attended_out, lse_out)
    stream.ready(2)

    edge = jnp.zeros((8, width), F32)
    padded[pl.ds(0, 8), :] = edge
    padded[pl.ds(rows + 8, 8), :] = edge
    for part in chunks(rows, 256):
        x2 = x1_out[part, :] + dot(attended_out[part, :], attn_out[...])
        x2_out[part, :] = x2
        hat, _ = normalize(x2)
        uc = (hat * gains(2)).astype(BF16)
        uc_out[part, :] = uc
        gin = dot(uc, conv_in[...])
        gin_out[part, :] = gin
        padded[pl.ds(part.start + 8, 256), :] = gin[:, :width] * sigmoid(gin[:, width:])

    stream.flush(x2_out, uc_out, gin_out)
    sums = jnp.zeros((1, width), F32)
    squares = jnp.zeros((1, width), F32)
    for part in chunks(rows, 64):
        depth = jnp.zeros((64, width), F32)
        for tap, shifted in shifts(padded, part):
            depth += table[pl.ds(6 + tap, 1), :] * shifted * taps[part, pl.ds(tap, 1)]
        depth_out[part, :] = depth
        weighted = jnp.where(seg_col[part, :] < 3, depth, 0.0)
        sums += jnp.sum(weighted, 0, keepdims=True)
        squares += jnp.sum(weighted * depth, 0, keepdims=True)
    moments[pl.ds(0, 1), :] = sums
    moments[pl.ds(1, 1), :] = squares
    moments[pl.ds(2, 6), :] = jnp.zeros((6, width), F32)
    stream.flush(depth_out, moments)


def batch_terms(moments, frame_count):
    mean = moments[pl.ds(0, 1), :] / frame_count[0]
    variance = moments[pl.ds(1, 1), :] / frame_count[0] - mean * mean
    return mean, lax.rsqrt(variance + EPSILON)


def middle_kernel(stream, frame_count, depth, moments, x2, table, conv_out, slot_row, swish_out, x3_out, sent, normed):
    rows, width = depth.shape
    stream.ready(0)
    mean, scale = batch_terms(moments, frame_count)
    for part in chunks(rows, 256):
        bn = (depth[part, :] - mean) * scale * table[pl.ds(5, 1), :] + table[pl.ds(21, 1), :]
        swish = (bn * sigmoid(bn)).astype(BF16)
        swish_out[part, :] = swish
        x3 = x2[part, :] + dot(swish, conv_out[...])
        x3_out[part, :] = x3
        hat, _ = normalize(x3)
        normed[part, :] = (hat * table[pl.ds(3, 1), :]).astype(BF16)
    stream.flush(swish_out, x3_out)
    scatter_to(slot_row, normed[...], sent)
    stream.flush(*sent)


def turn_kernel(
    stream, x3, blocks, slot_col, slot_row, gate, table, cotangent, seg_col,
    block_out, dx4_out, gate_grad, gain_out, sent, grads,
):
    rows, width = x3.shape
    gain = table[pl.ds(4, 1), :]
    stream.ready(0)
    gain_sum = jnp.zeros((1, width), F32)
    for part in chunks(rows, 256):
        found = gathered(slot_col, blocks, part)
        half = 0.5 * gate[part, :]
        x4 = x3[part, :] + half * found
        hat, inverse = normalize(x4)
        valid = seg_col[part, :] < 3
        block_out[part, :] = jnp.where(valid, hat * gain, 0.0).astype(BF16)
        grad = jnp.where(valid, cotangent[part, :].astype(F32), 0.0)
        gain_sum += jnp.sum(grad * hat, 0, keepdims=True)
        dx4 = norm_backward(grad, gain, hat, inverse)
        dx4_out[part, :] = dx4
        gate_grad[part, :] = 0.5 * jnp.sum(found * dx4, 1, keepdims=True)
        grads[part, :] = (half * dx4).astype(BF16)
    gain_out[...] = gain_sum
    stream.flush(block_out, dx4_out, gate_grad, gain_out)
    scatter_to(slot_row, grads[...], sent)
    stream.flush(*sent)


def conv_back_kernel(
    stream, frame_count, dx4, blocks, slot_col, x3, table, conv_out, depth, moments,
    dx3_out, dco_out, dh_out, sums,
):
    rows, width = x3.shape
    mean, scale = batch_terms(moments, frame_count)
    stream.ready(0)
    total = jnp.zeros((1, width), F32)
    moment = jnp.zeros((1, width), F32)
    shift = jnp.zeros((1, width), F32)
    gain5 = jnp.zeros((1, width), F32)
    gain3 = jnp.zeros((1, width), F32)
    for part in chunks(rows, 256):
        grad = gathered(slot_col, blocks, part)
        hat, inverse = normalize(x3[part, :])
        gain3 += jnp.sum(grad * hat, 0, keepdims=True)
        dx3 = dx4[part, :] + norm_backward(grad, table[pl.ds(3, 1), :], hat, inverse)
        dx3_out[part, :] = dx3
        dco = dx3.astype(BF16)
        dco_out[part, :] = dco
        centred = depth[part, :] - mean
        hat = centred * scale
        bn = hat * table[pl.ds(5, 1), :] + table[pl.ds(21, 1), :]
        dbn = dot_nt(dco, conv_out[...]) * slope(bn, sigmoid(bn))
        shift += jnp.sum(dbn, 0, keepdims=True)
        gain5 += jnp.sum(dbn * hat, 0, keepdims=True)
        dh = dbn * table[pl.ds(5, 1), :]
        dh_out[part, :] = dh
        total += jnp.sum(dh, 0, keepdims=True)
        moment += jnp.sum(dh * centred, 0, keepdims=True)
    for number, row in enumerate((total, moment, shift, gain5, gain3)):
        sums[pl.ds(number, 1), :] = row
    sums[pl.ds(5, 3), :] = jnp.zeros((3, width), F32)
    stream.flush(dx3_out, dco_out, dh_out, sums)


def back_kernel(
    stream, frame_count, dh, depth, moments, sums, dx3, gin, x2, x1, table, conv_in, attn_out, attn_in, qkv, lse,
    cosine, sine, seg_col, seg_row, taps, expert, gate, slot_row,
    dgin_out, dat_out, dproj_out, dx1_out, gate_grad, terms, sent,
    padded, glu, grad_rows, dk, dv, rows_sent, flipped,
):
    rows, width = dh.shape
    mean, scale = batch_terms(moments, frame_count)
    total, moment = sums[pl.ds(0, 1), :], sums[pl.ds(1, 1), :]
    var_grad = -0.5 * moment * scale * scale * scale
    mean_grad = -scale * total - 2.0 * mean * var_grad
    edge = jnp.zeros((8, width), F32)
    for ref in (padded, glu):
        ref[pl.ds(0, 8), :] = edge
        ref[pl.ds(rows + 8, 8), :] = edge
    stream.ready(0)
    for part in chunks(rows, 64):
        held = depth[part, :]
        grad = (mean_grad + 2.0 * held * var_grad) * (1.0 / frame_count[0])
        padded[pl.ds(part.start + 8, 64), :] = dh[part, :] * scale + jnp.where(seg_col[part, :] < 3, grad, 0.0)
    stream.ready(1)
    for part in chunks(rows, 64):
        glu[pl.ds(part.start + 8, 64), :] = gin[part, :width] * sigmoid(gin[part, width:])
    kernel_sums = [jnp.zeros((8, width), F32) for _ in range(15)]
    gain2 = jnp.zeros((1, width), F32)
    for part in chunks(rows, 64):
        dglu = jnp.zeros((64, width), F32)
        own = padded[pl.ds(part.start + 8, 64), :]
        for (tap, grad), (_, value) in zip(shifts(padded, part), shifts(glu, part)):
            mask = taps[part, pl.ds(tap, 1)]
            dglu += table[pl.ds(20 - tap, 1), :] * grad * mask
            kernel_sums[tap] += folded(own * value * mask)
        logistic = sigmoid(gin[part, width:])
        dgin_out[part, :width] = (dglu * logistic).astype(BF16)
        dgin_out[part, width:] = (dglu * gin[part, :width] * logistic * (1.0 - logistic)).astype(BF16)
    for tap in range(15):
        terms[pl.ds(6 + tap, 1), :] = jnp.sum(kernel_sums[tap], 0, keepdims=True)
    stream.flush(dgin_out)
    stream.ready(2)
    for part in chunks(rows, 256):
        grad = dot_nt(dgin_out[part, :], conv_in[...])
        hat, inverse = normalize(x2[part, :])
        gain2 += jnp.sum(grad * hat, 0, keepdims=True)
        dx2 = dx3[part, :] + norm_backward(grad, table[pl.ds(2, 1), :], hat, inverse)
        dx1_out[part, :] = dx2
        dat = dx2.astype(BF16)
        dat_out[part, :] = dat
        grad_rows[part, :] = dot_nt(dat, attn_out[...]).astype(BF16)
    terms[pl.ds(2, 1), :] = gain2

    stream.flush(dat_out)
    stream.ready(3)
    zero = jnp.zeros((), BF16)
    sides = tuple((iota((1, LANES), 1) < DH) == (side == 0) for side in range(2))
    turned = tuple((iota((LANES, 1), 0) < DH) == (side == 0) for side in range(2))
    for pair in range(width // LANES):
        flipped[pl.ds(pair * LANES, LANES), :] = qkv[:, pl.ds(width + pair * LANES, LANES)].T
    dk[...] = jnp.zeros_like(dk)
    dv[...] = jnp.zeros_like(dv)

    def attend(part_index, carry):
        part = pl.ds(pl.multiple_of(part_index * 512, 512), 512)
        related = seg_col[...] == seg_row[:, part]
        for pair in range(width // LANES):
            own = pl.ds(pair * LANES, LANES)
            q = qkv[part, own]
            k = qkv[:, pl.ds(width + pair * LANES, LANES)]
            v = qkv[:, pl.ds(2 * width + pair * LANES, LANES)]
            da = grad_rows[part, own]
            dq = jnp.zeros((LANES, 512), F32)
            dk_sum = jnp.zeros((rows, LANES), F32)
            dv_sum = jnp.zeros((rows, LANES), F32)
            for side in range(2):
                head = 2 * pair + side
                q_side = jnp.where(sides[side], q, zero)
                da_side = jnp.where(sides[side], da, zero)
                scores = dot_nt(k, q_side) - lse[pl.ds(head, 1), part]
                probs = jnp.exp(jnp.where(related, scores, -MASK_FILL))
                dprobs = dot_nt(v, da_side)
                inner = jnp.sum(probs * dprobs, 0, keepdims=True)
                dscores = (probs * (dprobs - inner)).astype(BF16)
                dq += dot(jnp.where(turned[side], flipped[own, :], zero), dscores)
                dk_sum += dot(dscores, q_side)
                dv_sum += dot(probs.astype(BF16), da_side)
            dk[:, own] += dk_sum
            dv[:, own] += dv_sum
            dq = dq.T * DH**-0.5
            dproj_out[part, own] = (dq * cosine[part, :] - partner(dq) * sine[part, :]).astype(BF16)
        return carry

    lax.fori_loop(0, rows // 512, attend, 0)

    stream.ready(4)
    gain1 = jnp.zeros((1, width), F32)
    for part in chunks(rows, 256):
        for pair in range(width // LANES):
            own = pl.ds(pair * LANES, LANES)
            held = dk[part, own]
            dproj_out[part, pl.ds(width + pair * LANES, LANES)] = (
                held * cosine[part, :] - partner(held) * sine[part, :]
            ).astype(BF16)
            dproj_out[part, pl.ds(2 * width + pair * LANES, LANES)] = dv[part, own].astype(BF16)
        grad = dot_nt(dproj_out[part, :], attn_in[...])
        hat, inverse = normalize(x1[part, :])
        gain1 += jnp.sum(grad * hat, 0, keepdims=True)
        dx1 = dx1_out[part, :] + norm_backward(grad, table[pl.ds(1, 1), :], hat, inverse)
        dx1_out[part, :] = dx1
        gate_grad[part, :] = 0.5 * jnp.sum(expert[part, :].astype(F32) * dx1, 1, keepdims=True)
        rows_sent[part, :] = (0.5 * gate[part, :] * dx1).astype(BF16)
    terms[pl.ds(1, 1), :] = gain1
    stream.flush(dproj_out, dx1_out, gate_grad, terms)
    scatter_to(slot_row, rows_sent[...], sent)
    stream.flush(*sent)


def final_kernel(frames, blocks, slot_col, table, dx1, dz, embed_weight, _, out):
    for part in chunks(frames.shape[0], 128):
        grad = gathered(slot_col, blocks, part)
        hat, inverse = normalize(frames[part, :].astype(F32))
        dx0 = dx1[part, :] + norm_backward(grad, table[pl.ds(0, 1), :], hat, inverse)
        out[part, :] = dx0 + dot_nt(dz[part, :], embed_weight[...])


def after(value, *others):
    return lax.optimization_barrier((value,) + others)[0]


def shards(
    frames,
    lengths,
    choice_first,
    choice_second,
    embed_weight,
    routers,
    norm_gains,
    attn_in,
    attn_out,
    conv_in,
    conv_kernel,
    bn_shift,
    conv_out,
    expert_in,
    expert_out,
    cotangent,
):
    rows, width = frames.shape
    layers, slice_width, experts = routers.shape
    taps = conv_kernel.shape[0]
    gains = norm_gains.shape[0]
    peers = lax.axis_size("expert")
    dp_count = lax.axis_size("dp")
    dp_bits = bit_count(("dp",))
    capacity = 2 * rows // experts
    hidden = expert_in.shape[3]
    device = lax.axis_index(AXES)
    block = shaped((capacity, width), BF16)
    wide = shaped((rows, width), F32)
    low = shaped((rows, width), BF16)
    column = shaped((rows, 1), F32)

    dp_index = lax.axis_index("dp")[None]

    def shard_of(layer):
        first = expert_in[layer, 0]
        tiles = [first[:, start : start + width] for start in range(0, hidden, width)]
        return jnp.concatenate([expert_out[layer, 0]] + tiles, 0)

    first_weights = lax.all_gather(shard_of(0), "dp", axis=0)
    sent, slot_col1, slot_row1, slot_col2, slot_row2 = call(
        start_kernel,
        ([block] * peers, shaped((rows, 1), I32), shaped((1, rows), I32), shaped((rows, 1), I32), shaped((1, rows), I32)),
        lax.axis_index("expert")[None],
        frames,
        choice_first,
        choice_first.reshape(1, rows),
        choice_second,
        choice_second.reshape(1, rows),
        specs=[SMEM] + [None] * 5,
    )
    first_blocks = swap_blocks(sent)

    small_width = gains + taps + 1 + layers * experts
    small = jnp.concatenate(
        [
            norm_gains.T,
            conv_kernel.T,
            bn_shift[:, None],
            jnp.moveaxis(routers, 1, 0).reshape(slice_width, -1),
            jnp.zeros((slice_width, -small_width % LANES), BF16),
        ],
        1,
    )
    small = after(small, sent[0])
    small_all = gather_everywhere(small).reshape(width, LANES).astype(F32)
    table = small_all[:, : gains + taps + 3].T
    router_table = jnp.pad(
        small_all[:, gains + taps + 1 : small_width], ((0, 0), (0, LANES - layers * experts))
    )
    dense = jnp.concatenate([attn_in, attn_out, conv_in, conv_out], 1)
    dense = lax.all_to_all(
        jnp.broadcast_to(dense[None], (peers,) + dense.shape), "expert", split_axis=0, concat_axis=0, tiled=True
    )
    dense = lax.all_gather(
        dense.reshape(peers * slice_width, 7 * width), "dp", axis=0, tiled=True
    )
    second_weights = lax.all_gather(shard_of(1), "dp", axis=0)

    own_lengths = lax.dynamic_index_in_dim(lengths, device, 0, keepdims=False)
    frame_count = jnp.sum(lengths[:, :-1]).astype(F32)[None]
    (embed_pre, embedded, probs, gate1, gate2, seg_col, seg_row, tap_masks, offsets) = call(
        functools.partial(embed_kernel, experts),
        [
            wide,
            wide,
            shaped((rows, LANES), F32),
            column,
            column,
            shaped((rows, 1), I32),
            shaped((1, rows), I32),
            shaped((rows, LANES), F32),
            column,
        ],
        jnp.cumsum(own_lengths, dtype=I32)[:-1],
        frames,
        embed_weight,
        router_table,
        choice_first,
        choice_second,
        specs=[SMEM] + [None] * 5,
    )
    half = DH // 2
    frequency = 10000.0 ** (-jnp.arange(half, dtype=F32) / half)
    angles = offsets * jnp.tile(frequency, LANES // half)[None, :]
    sign = jnp.asarray(np.where(np.arange(LANES) % DH < half, -1.0, 1.0), F32)
    cosine, sine = jnp.cos(angles), jnp.sin(angles) * sign[None, :]

    def gain(number):
        return table[number : number + 1]

    first_results = swap_blocks(
        [expert_forward(block, gain(0), first_weights, hidden, True) for block in first_blocks]
    )

    def dense_spec(columns, start):
        return pl.BlockSpec((width, columns), lambda i: (0, start // columns))

    attn_in_spec = dense_spec(3 * width, 0)
    attn_out_spec = dense_spec(width, 3 * width)
    conv_in_spec = dense_spec(2 * width, 4 * width)
    conv_out_spec = dense_spec(width, 6 * width)
    sums_shape = shaped((8, width), F32)
    padded = pltpu.VMEM((rows + 16, width), F32)

    first_expert, x1, x2, ua, qkv, lse, attended, uc, gin, depth, moments = call(
        front_kernel,
        [
            low,
            wide,
            wide,
            low,
            shaped((rows, 3 * width), BF16),
            shaped((8, rows), F32),
            low,
            low,
            shaped((rows, 2 * width), F32),
            wide,
            sums_shape,
        ],
        frames,
        first_results,
        slot_col1,
        gate1,
        table,
        Columns(dense, 0, 3 * width),
        Columns(dense, 3 * width, width),
        Columns(dense, 4 * width, 2 * width),
        cosine,
        sine,
        seg_col,
        seg_row,
        tap_masks,
        stages=[0, 0, None, None, None, 1, 2, 2, 1, 1, None, None, 2],
        cost=20,
        scratch=[padded, pltpu.VMEM((width, rows), BF16)],
    )
    moments = sum_everywhere(moments)
    swish, x3, sent = call(
        middle_kernel,
        (low, wide, [block] * peers),
        frame_count,
        depth,
        moments,
        x2,
        table,
        Columns(dense, 6 * width, width),
        slot_row2,
        specs=[SMEM] + [None] * 6,
        stages=[None, 0, None, 0, None, 0, None],
        scratch=[pltpu.VMEM((rows, width), BF16)],
    )

    second_blocks = swap_blocks(sent)
    second_results = swap_blocks(
        [expert_forward(block, gain(3), second_weights, hidden, False) for block in second_blocks]
    )
    block_out, dx4, gate_grad2, gain4, sent = call(
        turn_kernel,
        (low, wide, column, shaped((1, width), F32), [block] * peers),
        x3,
        second_results,
        slot_col2,
        slot_row2,
        gate2,
        table,
        cotangent,
        seg_col,
        stages=[0, 0, None, None, None, None, 0, None],
        scratch=[pltpu.VMEM((rows, width), BF16)],
    )
    second_grads = swap_blocks(sent)
    backs = [
        expert_backward(block, grad, gain(3), second_weights, hidden, False)
        for block, grad in zip(second_blocks, second_grads)
    ]
    back, hid, pre_grads, inputs, _ = zip(*backs)
    second_back = swap_blocks(back)
    (second_grad,) = weight_grads(
        dp_index, inputs, second_grads, hid, pre_grads, dp_count, False
    )
    second_back[1] = after(second_back[1], second_grad)
    second_own = lax.psum_scatter(second_grad, "dp", scatter_dimension=0, tiled=True)[0]

    dx3, dco, dh, sums = call(
        conv_back_kernel,
        [wide, low, wide, sums_shape],
        frame_count,
        dx4,
        second_back,
        slot_col2,
        x3,
        table,
        Columns(dense, 6 * width, width),
        depth,
        moments,
        specs=[SMEM] + [None] * 8,
        stages=[None, 0, 0, None, 0, None, 0, 0, None],
    )
    all_sums = sum_everywhere(sums)
    dgin, dat, dproj, dx1, gate_grad1, terms, sent = call(
        back_kernel,
        (
            shaped((rows, 2 * width), BF16),
            low,
            shaped((rows, 3 * width), BF16),
            wide,
            column,
            shaped((24, width), F32),
            [block] * peers,
        ),
        frame_count,
        dh,
        depth,
        moments,
        all_sums,
        dx3,
        gin,
        x2,
        x1,
        table,
        Columns(dense, 4 * width, 2 * width),
        Columns(dense, 3 * width, width),
        Columns(dense, 0, 3 * width),
        qkv,
        lse,
        cosine,
        sine,
        seg_col,
        seg_row,
        tap_masks,
        first_expert,
        gate1,
        slot_row1,
        specs=[SMEM] + [None] * 22,
        stages=[None, 0, 0, None, None, 2, 1, 2, 4, None, 2, 2, 4, 3, 3, 3, 3, None, None, 1, 4, None, None],
        cost=30,
        scratch=[padded, padded, pltpu.VMEM((rows, width), BF16), pltpu.VMEM((rows, width), F32), pltpu.VMEM((rows, width), F32), pltpu.VMEM((rows, width), BF16), pltpu.VMEM((width, rows), BF16)],
    )
    first_grads = swap_blocks(sent)

    dense_terms, dz, router_terms = call(
        functools.partial(dense_grad_kernel, experts),
        (shaped((width, 8 * width), BF16), low, shaped((LANES, width), F32)),
        ua,
        dproj,
        attended,
        dat,
        uc,
        dgin,
        swish,
        dco,
        gate_grad1,
        gate1,
        choice_first,
        gate_grad2,
        gate2,
        choice_second,
        probs,
        router_table,
        embed_pre,
        embedded,
        frames,
        stages=[0, 0, 1, 1, 2, 2, 2, 2] + [None] * 7 + [None, 2, 2, 2],
        cost=1,
        scratch=[pltpu.VMEM((rows, LANES), F32)],
    )
    dense_own = sum_to_owners(dense_terms.reshape(dp_count, -1, 8 * width), "dp").astype(BF16)
    dense_own = lax.all_to_all(
        dense_own.reshape(peers, slice_width, 8 * width), "expert", split_axis=0, concat_axis=0, tiled=True
    )
    owned = [shaped((slice_width, count * width), F32) for count in (3, 1, 2, 1)]
    *dense_own, embed_own = call(
        dense_out_kernel,
        (*owned, shaped((slice_width, width), BF16)),
        dense_own,
        cost=10,
    )
    embed_total = gather_everywhere(embed_own)
    embed_total = embed_total.reshape(width, width).astype(F32)

    backs = [
        expert_backward(block, grad, gain(0), first_weights, hidden, True)
        for block, grad in zip(first_blocks, first_grads)
    ]
    back, hid, pre_grads, inputs, gain0 = zip(*backs)
    gain0 = sum(gain0)
    first_back = swap_blocks(back)
    kept, moved = weight_grads(dp_index, inputs, first_grads, hid, pre_grads, dp_count, True)
    moved = after(moved, *first_back[1:])

    def dp_exchange(values, mask):
        return lax.ppermute(values, "dp", [(i, i ^ mask) for i in range(dp_count)])

    pair_sum = (kept.astype(F32) + dp_exchange(moved, 1).astype(F32)).astype(BF16)
    first_own = pair_sum[0].astype(F32)
    for number, mask in enumerate(chip_masks()):
        if mask:
            first_own = first_own + dp_exchange(pair_sum[number], mask).astype(F32)

    small_terms = jnp.concatenate(
        [
            gain0,
            terms[1:3],
            sums[4:5],
            gain4,
            sums[3:4],
            terms[6 : 6 + taps],
            sums[2:3],
            router_terms[: layers * experts],
        ],
        0,
    )
    small_terms = jnp.pad(small_terms.T, ((0, 0), (0, LANES - small_width)))
    small_sums = sum_to_owners(small_terms.reshape(-1, slice_width, LANES), AXES).T
    frames_grad = call(
        final_kernel,
        wide,
        frames,
        first_back,
        slot_col1,
        table,
        dx1,
        dz,
        embed_weight,
        second_own,
        specs=[None] * 7 + [ANY],
        cost=40,
    )
    def matrices(own):
        half = own.shape[0] // 2
        first = jnp.concatenate(jnp.split(own[half:], hidden // width, 0), 1)
        return first, own[:half]

    first_pair, second_pair = matrices(first_own), matrices(second_own.astype(F32))
    return (
        block_out,
        frames_grad,
        embed_total,
        jnp.moveaxis(
            small_sums[gains + taps + 1 : small_width].reshape(layers, experts, slice_width), 1, 2
        ),
        small_sums[:gains],
        *dense_own[:3],
        small_sums[gains : gains + taps],
        small_sums[gains + taps],
        dense_own[3],
        jnp.stack([first_pair[0], second_pair[0]])[:, None],
        jnp.stack([first_pair[1], second_pair[1]])[:, None],
    )


def solution(mesh):
    in_specs = (
        P(("dp", "expert"), None),
        P(),
        P(("dp", "expert"), None),
        P(("dp", "expert"), None),
        P(),
        P(None, ("dp", "expert"), None),
        P(None, ("dp", "expert")),
        P(("dp", "expert"), None),
        P(("dp", "expert"), None),
        P(("dp", "expert"), None),
        P(None, ("dp", "expert")),
        P(("dp", "expert")),
        P(("dp", "expert"), None),
        P(None, "expert", "dp", None),
        P(None, "expert", "dp", None),
        P(("dp", "expert"), None),
    )
    out_specs = (
        P(("dp", "expert"), None),
        P(("dp", "expert"), None),
        P(),
        P(None, ("dp", "expert"), None),
        P(None, ("dp", "expert")),
        P(("dp", "expert"), None),
        P(("dp", "expert"), None),
        P(("dp", "expert"), None),
        P(None, ("dp", "expert")),
        P(("dp", "expert")),
        P(("dp", "expert"), None),
        P(None, "expert", "dp", None),
        P(None, "expert", "dp", None),
    )
    return jax.shard_map(shards, mesh=mesh, in_specs=in_specs, out_specs=out_specs, check_vma=False)
```

```python
import functools

import jax
import jax.numpy as jnp
import numpy as np
from jax import lax
from jax.experimental import pallas as pl
from jax.experimental.pallas import tpu as pltpu
from jax.sharding import PartitionSpec as P

H = 8
DH = 64
LANES = 128

EPSILON = 1e-05
MASK_FILL = 1000000000.0
HIGHEST = lax.Precision.HIGHEST
AXES = ("dp", "expert")
BF16 = jnp.bfloat16
F32 = jnp.float32
I32 = jnp.int32
MIB = 1 << 20


def bit_count(axes):
    total = 1
    for name in axes:
        total *= lax.axis_size(name)
    return total.bit_length() - 1


def exchange(values, axes, mask):
    total = 1 << bit_count(axes)
    return lax.ppermute(values, axes, [(i, i ^ mask) for i in range(total)])


def device_groups():
    z_bits = bit_count(("expert",))
    dp_bits = bit_count(("dp",))
    chips = list(range(z_bits + 1, z_bits + dp_bits))
    rests = [chips, list(range(z_bits))]
    return [[z_bits]] + [bits[i : i + 2] for bits in rests for i in range(0, len(bits), 2)]


def masks_of(bits):
    if len(bits) == 1:
        return [1 << bits[0]]
    low, high = 1 << bits[0], 1 << bits[1]
    return [low, high, low | high]


def sum_everywhere(values):
    for bits in device_groups():
        arrived = [exchange(values, AXES, mask) for mask in masks_of(bits)]
        if len(arrived) == 1:
            values = values + arrived[0]
        else:
            values = (values + arrived[0]) + (arrived[1] + arrived[2])
    return values


def gather_everywhere(values):
    total = 1 << bit_count(AXES)
    sent = jnp.broadcast_to(values[None], (total,) + values.shape)
    return lax.all_to_all(sent, AXES, split_axis=0, concat_axis=0, tiled=True)


def sum_to_owners(values, axes):
    arrived = lax.all_to_all(values, axes, split_axis=0, concat_axis=0, tiled=True)
    return jnp.sum(arrived.astype(F32), 0)


def swap_blocks(blocks):
    total = lax.axis_size("expert")
    moved = [blocks[0]]
    for k in range(1, total):
        moved.append(lax.ppermute(blocks[k], "expert", [(i, i ^ k) for i in range(total)]))
    return moved


def chip_masks():
    return [core << 1 for core in range(lax.axis_size("dp") // 2)]


class Columns:
    def __init__(self, array, start, count):
        self.array, self.start, self.count = array, start, count


class Stream:
    def __init__(self, arrivals, results):
        self.arrivals, self.results = arrivals, results
        self.waited, self.sent = set(), []
        self.begin(0)
        self.begin(1)

    def begin(self, stage):
        for copy in self.arrivals.get(stage, ()):
            copy.start()

    def ready(self, stage):
        for copy in self.arrivals.get(stage, ()):
            copy.wait()
        self.waited.add(stage)
        self.begin(stage + 2)

    def flush(self, *refs):
        for ref in refs:
            copy = self.results[id(ref)]
            copy.start()
            self.sent.append(copy)

    def finish(self):
        for copy in self.sent:
            copy.wait()


def call(body, outs, *args, specs=None, out_specs=None, scratch=(), stages=None, vmem=60, cost=5, **kw):
    vmem_spec = pl.BlockSpec(memory_space=pltpu.VMEM)
    any_spec = pl.BlockSpec(memory_space=pl.ANY)
    if specs is None:
        specs = [None] * len(args)
    columns = [arg if isinstance(arg, Columns) else None for arg in args]
    args = [arg.array if isinstance(arg, Columns) else arg for arg in args]
    grid = kw.pop("grid", (1,))
    scratch = list(scratch)
    if stages is None:
        specs = [
            jax.tree.map(lambda _: vmem_spec, arg) if spec is None else spec
            for spec, arg in zip(specs, args)
        ]
        if out_specs is None:
            out_specs = jax.tree.map(lambda _: vmem_spec, outs)
        wrapped = body
    else:
        specs = [
            spec if spec is not None else jax.tree.map(lambda _: vmem_spec if stage is None else any_spec, arg)
            for spec, arg, stage in zip(specs, args, stages)
        ]
        out_specs = jax.tree.map(lambda _: any_spec, outs)
        buffers = []
        for arg, part, stage in zip(args, columns, stages):
            if stage is not None:
                for leaf in jax.tree.leaves(arg):
                    shape = leaf.shape if part is None else (leaf.shape[0], part.count)
                    buffers.append(pltpu.VMEM(shape, leaf.dtype))
        out_leaves, out_tree = jax.tree.flatten(outs)
        buffers += [pltpu.VMEM(leaf.shape, leaf.dtype) for leaf in out_leaves]
        own_scratch, total = len(scratch), len(buffers)
        scratch = scratch + buffers + [pltpu.SemaphoreType.DMA((total,))]

        def wrapped(*refs):
            refs = list(refs)
            ins, out_refs, rest = refs[: len(args)], refs[len(args) : len(args) + out_count], refs[len(args) + out_count :]
            own, held, sems = rest[:own_scratch], rest[own_scratch:-1], rest[-1]
            arrivals, given, used = {}, [], 0
            for ref, part, stage in zip(ins, columns, stages):
                if stage is None:
                    given.append(ref)
                    continue
                leaves, tree = jax.tree.flatten(ref)
                landed = []
                for leaf in leaves:
                    source = leaf if part is None else leaf.at[:, pl.ds(part.start, part.count)]
                    arrivals.setdefault(stage, []).append(
                        pltpu.make_async_copy(source, held[used], sems.at[used])
                    )
                    landed.append(held[used])
                    used += 1
                given.append(jax.tree.unflatten(tree, landed))
            results, places = {}, []
            for ref in jax.tree.leaves(out_refs):
                results[id(held[used])] = pltpu.make_async_copy(held[used], ref, sems.at[used])
                places.append(held[used])
                used += 1
            stream = Stream(arrivals, results)
            given_outs = jax.tree.unflatten(out_tree, places)
            given_outs = list(given_outs) if isinstance(given_outs, (tuple, list)) else [given_outs]
            body(stream, *given, *given_outs, *own)
            stream.finish()

        out_count = len(outs) if isinstance(outs, (tuple, list)) else 1
    return pl.pallas_call(
        wrapped,
        out_shape=outs,
        in_specs=specs,
        out_specs=out_specs,
        scratch_shapes=scratch,
        grid=grid,
        compiler_params=pltpu.CompilerParams(vmem_limit_bytes=vmem * MIB),
        cost_estimate=pl.CostEstimate(flops=cost * 1153 * 10**6, bytes_accessed=0, transcendentals=0),
        **kw,
    )(*args)


def shaped(shape, dtype):
    return jax.ShapeDtypeStruct(shape, dtype)


SMEM = pl.BlockSpec(memory_space=pltpu.SMEM)
ANY = pl.BlockSpec(memory_space=pl.ANY)


def dot(left, right):
    return lax.dot_general(left, right, (((1,), (0,)), ((), ())), preferred_element_type=F32)


def dot_nt(left, right):
    return lax.dot_general(left, right, (((1,), (1,)), ((), ())), preferred_element_type=F32)


def dot_tn(left, right):
    return lax.dot_general(left, right, (((0,), (0,)), ((), ())), preferred_element_type=F32)


def iota(shape, dim):
    return lax.broadcasted_iota(I32, shape, dim)


def normalize(rows):
    centred = rows - jnp.mean(rows, -1, keepdims=True)
    inverse = lax.rsqrt(jnp.mean(centred * centred, -1, keepdims=True) + EPSILON)
    return centred * inverse, inverse


def norm_backward(grad, gain, hat, inverse):
    scaled = grad * gain
    return inverse * (
        scaled
        - jnp.mean(scaled, -1, keepdims=True)
        - hat * jnp.mean(scaled * hat, -1, keepdims=True)
    )


def sigmoid(values):
    return 1.0 / (1.0 + jnp.exp(-values))


def slope(values, logistic):
    return logistic * (1.0 + values * (1.0 - logistic))


def chunks(total, size):
    return [pl.ds(start, size) for start in range(0, total, size)]


def gathered(slot_col, blocks, rows):
    slot = slot_col[rows, :]
    total = None
    for k, block in enumerate(blocks):
        capacity = block.shape[0]
        pick = (slot == iota((slot.shape[0], capacity), 1) + k * capacity).astype(F32).astype(BF16)
        part = dot(pick, block[...])
        total = part if total is None else total + part
    return total


def scatter_to(slot_row, values, outs):
    for k, out in enumerate(outs):
        capacity = out.shape[0]
        pick = (slot_row[...] == iota((capacity, slot_row.shape[1]), 0) + k * capacity)
        out[...] = dot(pick.astype(F32).astype(BF16), values).astype(BF16)


def start_kernel(own, frames, col1, row1, col2, row2, sent, slot_col1, slot_row1, slot_col2, slot_row2):
    rows = frames.shape[0]
    capacity = sent[0].shape[0]
    below = (iota((rows, rows), 0) > iota((rows, rows), 1)).astype(F32).astype(BF16)
    above = (iota((rows, rows), 0) < iota((rows, rows), 1)).astype(F32).astype(BF16)
    for col, row, out_col, out_row in (
        (col1, row1, slot_col1, slot_row1),
        (col2, row2, slot_col2, slot_row2),
    ):
        hot = (col[...] == iota((rows, LANES), 1)).astype(F32)
        rank = jnp.sum(dot(below, hot.astype(BF16)) * hot, 1, keepdims=True)
        out_col[...] = (col[...] ^ own[0]) * capacity + rank.astype(I32)
        hot = (row[...] == iota((16, rows), 0)).astype(F32)
        rank = jnp.sum(dot(hot.astype(BF16), above) * hot, 0, keepdims=True)
        out_row[...] = (row[...] ^ own[0]) * capacity + rank.astype(I32)
    scatter_to(slot_row1, frames[...], sent)


def expert_specs(weights, hidden, tile):
    count, rows, width = weights.shape
    half = rows // 2
    in_rows = width // count
    first = pl.BlockSpec((count, in_rows, tile), lambda j: (0, half // in_rows + j, 0))
    second = pl.BlockSpec((tile // half, half, width), lambda j: (j, 0, 0))
    return first, second


def flat(ref):
    count, rows, width = ref.shape
    return ref[...].reshape(count * rows, width)


def expert_forward_kernel(with_norm, block, gain, w_in, w_out, out, total, inputs):
    step = pl.program_id(0)

    @pl.when(step == 0)
    def _():
        if with_norm:
            hat, _ = normalize(block[...].astype(F32))
            inputs[...] = (hat * gain[...]).astype(BF16)
        else:
            inputs[...] = block[...]
        total[...] = jnp.zeros_like(total)

    pre = dot(inputs[...], flat(w_in))
    hidden = (pre * sigmoid(pre)).astype(BF16)
    total[...] += dot(hidden, flat(w_out))

    @pl.when(step == pl.num_programs(0) - 1)
    def _():
        out[...] = total[...].astype(BF16)


def expert_forward(block, gain, weights, hidden, with_norm, tile=512):
    capacity, width = block.shape
    first, second = expert_specs(weights, hidden, tile)
    whole = pl.BlockSpec((capacity, width), lambda j: (0, 0))
    return call(
        functools.partial(expert_forward_kernel, with_norm),
        shaped((capacity, width), BF16),
        block,
        gain,
        weights,
        weights,
        specs=[whole, pl.BlockSpec((1, width), lambda j: (0, 0)), first, second],
        out_specs=whole,
        scratch=[pltpu.VMEM((capacity, width), F32), pltpu.VMEM((capacity, width), BF16)],
        grid=(hidden // tile,),
        vmem=12,
        cost=8,
    )


def expert_backward_kernel(
    with_norm, block, grad, gain, w_in, w_out, out, hidden_out, pre_grad_out, input_out, gain_out, total, hats
):
    step = pl.program_id(0)

    @pl.when(step == 0)
    def _():
        if with_norm:
            hat, _ = normalize(block[...].astype(F32))
            hats[...] = hat
            input_out[...] = (hat * gain[...]).astype(BF16)
        else:
            input_out[...] = block[...]
        total[...] = jnp.zeros_like(total)

    first, second = flat(w_in), flat(w_out)
    pre = dot(input_out[...], first)
    logistic = sigmoid(pre)
    hidden_out[...] = (pre * logistic).astype(BF16)
    hidden_grad = dot_nt(grad[...], second)
    pre_grad = (hidden_grad * slope(pre, logistic)).astype(BF16)
    pre_grad_out[...] = pre_grad
    total[...] += dot_nt(pre_grad, first)

    @pl.when(step == pl.num_programs(0) - 1)
    def _():
        back = total[...].astype(BF16)
        out[...] = back
        if with_norm:
            gain_out[...] = jnp.sum(back.astype(F32) * hats[...], 0, keepdims=True)
        else:
            gain_out[...] = jnp.zeros_like(gain_out)


def expert_backward(block, grad, gain, weights, hidden, with_norm, tile=512):
    capacity, width = block.shape
    first, second = expert_specs(weights, hidden, tile)
    whole = pl.BlockSpec((capacity, width), lambda j: (0, 0))
    tiled = pl.BlockSpec((capacity, tile), lambda j: (0, j))
    one = pl.BlockSpec((1, width), lambda j: (0, 0))
    return call(
        functools.partial(expert_backward_kernel, with_norm),
        (
            shaped((capacity, width), BF16),
            shaped((capacity, hidden), BF16),
            shaped((capacity, hidden), BF16),
            shaped((capacity, width), BF16),
            shaped((1, width), F32),
        ),
        block,
        grad,
        gain,
        weights,
        weights,
        specs=[whole, whole, one, first, second],
        out_specs=(whole, tiled, tiled, whole, one),
        scratch=[pltpu.VMEM((capacity, width), F32), pltpu.VMEM((capacity, width), F32)],
        grid=(hidden // tile,),
        vmem=16,
        cost=20,
    )


def weight_grad_kernel(relative, dp_index, inputs, grads, hidden, pre_grads, *refs):
    outs, (first, second) = refs[:-2], refs[-2:]
    step = pl.program_id(0)
    first_sum = second_sum = None
    for block, grad, hid, pre_grad in zip(inputs, grads, hidden, pre_grads):
        part = dot_tn(block[...], pre_grad[...])
        first_sum = part if first_sum is None else first_sum + part
        part = dot_tn(hid[...], grad[...])
        second_sum = part if second_sum is None else second_sum + part
    count = sum(out.shape[0] for out in outs)
    half = outs[0].shape[1] // 2
    in_rows = first_sum.shape[0] // count
    tile = second_sum.shape[0]
    owners = tile // half
    place = pl.ds(pl.multiple_of(half + step * in_rows, in_rows), in_rows)
    if not relative:
        for device in range(count):
            outs[0][device, place, :] = first_sum[device * in_rows : (device + 1) * in_rows].astype(BF16)
        for number in range(owners):
            outs[0][step * owners + number, pl.ds(0, half), :] = second_sum[
                number * half : (number + 1) * half
            ].astype(BF16)
    else:
        first[...] = first_sum.astype(BF16)
        for number in range(count):
            source = pl.multiple_of((dp_index[0] ^ number) * in_rows, in_rows)
            outs[number % 2][number // 2, place, :] = first[pl.ds(source, in_rows), :]
        second[...] = second_sum.astype(BF16)
        for number in range(owners):
            owner = (step * owners + number) ^ dp_index[0]

            @pl.when(owner % 2 == 0)
            def _():
                outs[0][owner // 2, pl.ds(0, half), :] = second[pl.ds(number * half, half), :]

            @pl.when(owner % 2 == 1)
            def _():
                outs[1][owner // 2, pl.ds(0, half), :] = second[pl.ds(number * half, half), :]


def weight_grads(dp_index, inputs, grads, hidden, pre_grads, count, relative, tile=512):
    capacity, width = inputs[0].shape
    units = hidden[0].shape[1]
    whole = pl.BlockSpec((capacity, width), lambda j: (0, 0))
    tiled = pl.BlockSpec((capacity, tile), lambda j: (0, j))
    rows = 2 * units // count
    if relative:
        outs = (shaped((count // 2, rows, width), BF16),) * 2
    else:
        outs = (shaped((count, rows, width), BF16),)
    peers = len(inputs)
    return call(
        functools.partial(weight_grad_kernel, relative),
        outs,
        dp_index,
        list(inputs),
        list(grads),
        list(hidden),
        list(pre_grads),
        specs=[SMEM, [whole] * peers, [whole] * peers, [tiled] * peers, [tiled] * peers],
        out_specs=tuple(pl.BlockSpec(o.shape, lambda j: (0, 0, 0)) for o in outs),
        scratch=[pltpu.VMEM((width, tile), BF16), pltpu.VMEM((tile, width), BF16)],
        grid=(units // tile,),
        vmem=28,
        cost=8,
    )


def dense_grad_kernel(
    experts, stream, ua, dproj, attended, dat, uc, dgin, swish, dco, gate_grad1, gate1, col1, gate_grad2, gate2, col2,
    dp_index, probs, routers, pre, embedded, frames, kept, moved, dz, router_terms, logits, term,
):
    width = ua.shape[1]
    count = 2 * kept.shape[0]
    part_rows = width // count

    def place(left, right, tile):
        for column in range(right.shape[1] // width):
            term[...] = dot_tn(left[...], right[:, pl.ds(column * width, width)]).astype(BF16)
            for number in range(count):
                source = pl.multiple_of((dp_index[0] ^ number) * part_rows, part_rows)
                target = moved if number % 2 else kept
                target[number // 2, pl.ds((tile + column) * part_rows, part_rows), :] = term[pl.ds(source, part_rows), :]

    rows = frames.shape[0]
    stream.ready(0)
    stream.ready(1)
    place(ua, dproj, 0)
    place(attended, dat, 3)
    stream.ready(2)
    for part in chunks(rows, 256):
        lane = iota((256, LANES), 1)
        grad = jnp.zeros((256, LANES), F32)
        for number, (gate_grad, gate, col) in enumerate(((gate_grad1, gate1, col1), (gate_grad2, gate2, col2))):
            inside = (lane >= number * experts) & (lane < (number + 1) * experts)
            hot = (lane == col[part, :] + number * experts).astype(F32)
            scale = gate_grad[part, :] * gate[part, :]
            grad = jnp.where(inside, scale * (hot - probs[part, :]), grad)
        logits[part, :] = grad
        demb = lax.dot_general(
            grad, routers[...], (((1,), (1,)), ((), ())), precision=HIGHEST, preferred_element_type=F32
        )
        held = pre[part, :]
        dz[part, :] = (demb * slope(held, sigmoid(held))).astype(BF16)
    router_terms[...] = lax.dot_general(
        logits[...], embedded[...], (((0,), (0,)), ((), ())), precision=HIGHEST, preferred_element_type=F32
    )
    stream.flush(dz, router_terms)
    place(uc, dgin, 4)
    place(swish, dco, 6)
    place(frames, dz, 7)
    stream.flush(kept, moved)


def pair_kernel(kept, moved, *outs):
    for number, out in enumerate(outs):
        out[...] = (kept[number].astype(F32) + moved[number].astype(F32)).astype(BF16)


def experts_out_kernel(parts, second, in_out, out_out):
    _, _, in_rows, hidden = in_out.shape
    width = out_out.shape[3]
    half = out_out.shape[2]

    first = parts[0][...].astype(F32)
    for part in parts[1:]:
        first = first + part[...].astype(F32)
    for layer, values in ((0, first), (1, second[...].astype(F32))):
        out_out[layer, 0] = values[:half]
        for tile in range(hidden // width):
            rows = values[half + tile * in_rows : half + (tile + 1) * in_rows]
            in_out[layer, 0, :, tile * width : (tile + 1) * width] = rows


def dense_out_kernel(arrived, *outs):
    start = 0
    for out in outs:
        lanes = pl.ds(start, out.shape[1])
        total = arrived[0, :, lanes].astype(F32)
        for number in range(1, arrived.shape[0]):
            total = total + arrived[number, :, lanes].astype(F32)
        out[...] = total.astype(out.dtype)
        start += out.shape[1]


def embed_kernel(experts, ends, frames, weight, routers, col1, col2, pre_out, embedded_out, probs_out, gate1, gate2, seg_col, seg_row, taps_out, offset_out):
    rows = frames.shape[0]
    for part in chunks(rows, 256):
        pre = dot(frames[part, :], weight[...])
        pre_out[part, :] = pre
        embedded = pre * sigmoid(pre)
        embedded_out[part, :] = embedded
        logits = jnp.dot(embedded, routers[...], precision=HIGHEST, preferred_element_type=F32)
        lane = iota(logits.shape, 1)
        probs = jnp.zeros_like(logits)
        for number, (col, gate) in enumerate(((col1, gate1), (col2, gate2))):
            inside = (lane >= number * experts) & (lane < (number + 1) * experts)
            top = jnp.max(jnp.where(inside, logits, -MASK_FILL), 1, keepdims=True)
            weights = jnp.where(inside, jnp.exp(jnp.where(inside, logits - top, 0.0)), 0.0)
            own = weights / jnp.sum(weights, 1, keepdims=True)
            hot = lane == col[part, :] + number * experts
            gate[part, :] = jnp.sum(jnp.where(hot, own, 0.0), 1, keepdims=True)
            probs = probs + own
        probs_out[part, :] = probs

    def segment_of(place):
        found = jnp.zeros(place.shape, I32)
        for number in range(3):
            found += (place >= ends[number]).astype(I32)
        return found

    segment = segment_of(iota((rows, 1), 0))
    seg_col[...] = segment
    seg_row[...] = segment_of(iota((1, rows), 1))
    place = iota((rows, LANES), 0) + iota((rows, LANES), 1) - 7
    same = (segment_of(place) == segment) & (place >= 0) & (place < rows)
    taps_out[...] = same.astype(F32)
    first = jnp.zeros((rows, 1), I32)
    for number in range(3):
        first = jnp.where(segment > number, ends[number], first)
    offset_out[...] = (iota((rows, 1), 0) - first).astype(F32)


def partner(values):
    half = DH // 2
    lane = iota(values.shape, 1)
    return jnp.where(lane % DH < half, pltpu.roll(values, LANES - half, 1), pltpu.roll(values, half, 1))


def shifts(padded, part):
    size = part.size
    for offset in range(8):
        held = padded[pl.ds(part.start + offset, size + 8), :]
        if offset:
            yield offset - 1, held[:size]
        yield offset + 7, held[8:]


def folded(values):
    return jnp.sum(values.reshape(-1, 8, values.shape[1]), 0)


def front_kernel(
    stream, frames, blocks, slot_col, gate, table, attn_in, attn_out, conv_in, cosine, sine, seg_col, seg_row, taps,
    expert_out, x1_out, x2_out, ua_out, qkv_out, lse_out, attended_out, uc_out, gin_out, depth_out, moments,
    padded, flipped,
):
    rows, width = frames.shape
    gains = lambda n: table[pl.ds(n, 1), :]
    stream.ready(0)
    for part in chunks(rows, 256):
        found = gathered(slot_col, blocks, part)
        expert_out[part, :] = found.astype(BF16)
        x1 = frames[part, :].astype(F32) + 0.5 * gate[part, :] * found
        x1_out[part, :] = x1
        hat, _ = normalize(x1)
        ua_out[part, :] = (hat * gains(1)).astype(BF16)
    stream.flush(expert_out, x1_out, ua_out)
    stream.ready(1)
    for part in chunks(rows, 256):
        ua = ua_out[part, :]
        for piece in range(3 * width // LANES):
            lanes = pl.ds(piece * LANES, LANES)
            if piece % 2 == 0:
                pair = dot(ua, attn_in[:, pl.ds(piece * LANES, 2 * LANES)])
            values = pair[:, :LANES] if piece % 2 == 0 else pair[:, LANES:]
            if piece < 2 * width // LANES:
                values = values * cosine[part, :] + partner(values) * sine[part, :]
            if piece < width // LANES:
                values = values * DH**-0.5
            qkv_out[part, lanes] = values.astype(BF16)

    stream.flush(qkv_out)
    zero = jnp.zeros((), BF16)
    sides = tuple((iota((1, LANES), 1) < DH) == (side == 0) for side in range(2))
    turned = tuple((iota((LANES, 1), 0) < DH) == (side == 0) for side in range(2))
    for pair in range(width // LANES):
        flipped[pl.ds(pair * LANES, LANES), :] = qkv_out[:, pl.ds(2 * width + pair * LANES, LANES)].T

    def attend(part_index, carry):
        part = pl.ds(pl.multiple_of(part_index * 512, 512), 512)
        related = seg_col[...] == seg_row[:, part]
        for pair in range(width // LANES):
            q = qkv_out[part, pl.ds(pair * LANES, LANES)]
            k = qkv_out[:, pl.ds(width + pair * LANES, LANES)]
            v = flipped[pl.ds(pair * LANES, LANES), :]
            result = jnp.zeros((LANES, 512), F32)
            for side in range(2):
                scores = dot_nt(k, jnp.where(sides[side], q, zero))
                scores = jnp.where(related, scores, -MASK_FILL)
                top = jnp.max(scores, 0, keepdims=True)
                weights = jnp.exp(scores - top)
                summed = jnp.sum(weights, 0, keepdims=True)
                probs = (weights * (1.0 / summed)).astype(BF16)
                result += dot(jnp.where(turned[side], v, zero), probs)
                lse_out[pl.ds(2 * pair + side, 1), part] = top + jnp.log(summed)
            attended_out[part, pl.ds(pair * LANES, LANES)] = result.T.astype(BF16)
        return carry

    lax.fori_loop(0, rows // 512, attend, 0)
    stream.flush(attended_out, lse_out)
    stream.ready(2)

    edge = jnp.zeros((8, width), F32)
    padded[pl.ds(0, 8), :] = edge
    padded[pl.ds(rows + 8, 8), :] = edge
    for part in chunks(rows, 256):
        x2 = x1_out[part, :] + dot(attended_out[part, :], attn_out[...])
        x2_out[part, :] = x2
        hat, _ = normalize(x2)
        uc = (hat * gains(2)).astype(BF16)
        uc_out[part, :] = uc
        gin = dot(uc, conv_in[...])
        gin_out[part, :] = gin
        padded[pl.ds(part.start + 8, 256), :] = gin[:, :width] * sigmoid(gin[:, width:])

    stream.flush(x2_out, uc_out, gin_out)
    sums = jnp.zeros((1, width), F32)
    squares = jnp.zeros((1, width), F32)
    for part in chunks(rows, 64):
        depth = jnp.zeros((64, width), F32)
        for tap, shifted in shifts(padded, part):
            depth += table[pl.ds(6 + tap, 1), :] * shifted * taps[part, pl.ds(tap, 1)]
        depth_out[part, :] = depth
        weighted = jnp.where(seg_col[part, :] < 3, depth, 0.0)
        sums += jnp.sum(weighted, 0, keepdims=True)
        squares += jnp.sum(weighted * depth, 0, keepdims=True)
    moments[pl.ds(0, 1), :] = sums
    moments[pl.ds(1, 1), :] = squares
    moments[pl.ds(2, 6), :] = jnp.zeros((6, width), F32)
    stream.flush(depth_out, moments)


def batch_terms(moments, frame_count):
    mean = moments[pl.ds(0, 1), :] / frame_count[0]
    variance = moments[pl.ds(1, 1), :] / frame_count[0] - mean * mean
    return mean, lax.rsqrt(variance + EPSILON)


def middle_kernel(stream, frame_count, depth, moments, x2, table, conv_out, slot_row, swish_out, x3_out, sent, normed):
    rows, width = depth.shape
    stream.ready(0)
    mean, scale = batch_terms(moments, frame_count)
    for part in chunks(rows, 256):
        bn = (depth[part, :] - mean) * scale * table[pl.ds(5, 1), :] + table[pl.ds(21, 1), :]
        swish = (bn * sigmoid(bn)).astype(BF16)
        swish_out[part, :] = swish
        x3 = x2[part, :] + dot(swish, conv_out[...])
        x3_out[part, :] = x3
        hat, _ = normalize(x3)
        normed[part, :] = (hat * table[pl.ds(3, 1), :]).astype(BF16)
    stream.flush(swish_out, x3_out)
    scatter_to(slot_row, normed[...], sent)
    stream.flush(*sent)


def turn_kernel(
    stream, x3, blocks, slot_col, slot_row, gate, table, cotangent, seg_col,
    block_out, dx4_out, gate_grad, gain_out, sent, grads,
):
    rows, width = x3.shape
    gain = table[pl.ds(4, 1), :]
    stream.ready(0)
    gain_sum = jnp.zeros((1, width), F32)
    for part in chunks(rows, 256):
        found = gathered(slot_col, blocks, part)
        half = 0.5 * gate[part, :]
        x4 = x3[part, :] + half * found
        hat, inverse = normalize(x4)
        valid = seg_col[part, :] < 3
        block_out[part, :] = jnp.where(valid, hat * gain, 0.0).astype(BF16)
        grad = jnp.where(valid, cotangent[part, :].astype(F32), 0.0)
        gain_sum += jnp.sum(grad * hat, 0, keepdims=True)
        dx4 = norm_backward(grad, gain, hat, inverse)
        dx4_out[part, :] = dx4
        gate_grad[part, :] = 0.5 * jnp.sum(found * dx4, 1, keepdims=True)
        grads[part, :] = (half * dx4).astype(BF16)
    gain_out[...] = gain_sum
    stream.flush(block_out, dx4_out, gate_grad, gain_out)
    scatter_to(slot_row, grads[...], sent)
    stream.flush(*sent)


def conv_back_kernel(
    stream, frame_count, dx4, blocks, slot_col, x3, table, conv_out, depth, moments,
    dx3_out, dco_out, dh_out, sums,
):
    rows, width = x3.shape
    mean, scale = batch_terms(moments, frame_count)
    stream.ready(0)
    total = jnp.zeros((1, width), F32)
    moment = jnp.zeros((1, width), F32)
    shift = jnp.zeros((1, width), F32)
    gain5 = jnp.zeros((1, width), F32)
    gain3 = jnp.zeros((1, width), F32)
    for part in chunks(rows, 256):
        grad = gathered(slot_col, blocks, part)
        hat, inverse = normalize(x3[part, :])
        gain3 += jnp.sum(grad * hat, 0, keepdims=True)
        dx3 = dx4[part, :] + norm_backward(grad, table[pl.ds(3, 1), :], hat, inverse)
        dx3_out[part, :] = dx3
        dco = dx3.astype(BF16)
        dco_out[part, :] = dco
        centred = depth[part, :] - mean
        hat = centred * scale
        bn = hat * table[pl.ds(5, 1), :] + table[pl.ds(21, 1), :]
        dbn = dot_nt(dco, conv_out[...]) * slope(bn, sigmoid(bn))
        shift += jnp.sum(dbn, 0, keepdims=True)
        gain5 += jnp.sum(dbn * hat, 0, keepdims=True)
        dh = dbn * table[pl.ds(5, 1), :]
        dh_out[part, :] = dh
        total += jnp.sum(dh, 0, keepdims=True)
        moment += jnp.sum(dh * centred, 0, keepdims=True)
    for number, row in enumerate((total, moment, shift, gain5, gain3)):
        sums[pl.ds(number, 1), :] = row
    sums[pl.ds(5, 3), :] = jnp.zeros((3, width), F32)
    stream.flush(dx3_out, dco_out, dh_out, sums)


def back_kernel(
    stream, frame_count, dh, depth, moments, sums, dx3, gin, x2, x1, table, conv_in, attn_out, attn_in, qkv, lse,
    cosine, sine, seg_col, seg_row, taps, expert, gate, slot_row,
    dgin_out, dat_out, dproj_out, dx1_out, gate_grad, terms, sent,
    padded, glu, grad_rows, dk, dv, rows_sent, flipped,
):
    rows, width = dh.shape
    mean, scale = batch_terms(moments, frame_count)
    total, moment = sums[pl.ds(0, 1), :], sums[pl.ds(1, 1), :]
    var_grad = -0.5 * moment * scale * scale * scale
    mean_grad = -scale * total - 2.0 * mean * var_grad
    edge = jnp.zeros((8, width), F32)
    for ref in (padded, glu):
        ref[pl.ds(0, 8), :] = edge
        ref[pl.ds(rows + 8, 8), :] = edge
    stream.ready(0)
    for part in chunks(rows, 64):
        held = depth[part, :]
        grad = (mean_grad + 2.0 * held * var_grad) * (1.0 / frame_count[0])
        padded[pl.ds(part.start + 8, 64), :] = dh[part, :] * scale + jnp.where(seg_col[part, :] < 3, grad, 0.0)
    stream.ready(1)
    for part in chunks(rows, 64):
        glu[pl.ds(part.start + 8, 64), :] = gin[part, :width] * sigmoid(gin[part, width:])
    kernel_sums = [jnp.zeros((8, width), F32) for _ in range(15)]
    gain2 = jnp.zeros((1, width), F32)
    for part in chunks(rows, 64):
        dglu = jnp.zeros((64, width), F32)
        own = padded[pl.ds(part.start + 8, 64), :]
        for (tap, grad), (_, value) in zip(shifts(padded, part), shifts(glu, part)):
            mask = taps[part, pl.ds(tap, 1)]
            dglu += table[pl.ds(20 - tap, 1), :] * grad * mask
            kernel_sums[tap] += folded(own * value * mask)
        logistic = sigmoid(gin[part, width:])
        dgin_out[part, :width] = (dglu * logistic).astype(BF16)
        dgin_out[part, width:] = (dglu * gin[part, :width] * logistic * (1.0 - logistic)).astype(BF16)
    for tap in range(15):
        terms[pl.ds(6 + tap, 1), :] = jnp.sum(kernel_sums[tap], 0, keepdims=True)
    stream.flush(dgin_out)
    stream.ready(2)
    for part in chunks(rows, 256):
        grad = dot_nt(dgin_out[part, :], conv_in[...])
        hat, inverse = normalize(x2[part, :])
        gain2 += jnp.sum(grad * hat, 0, keepdims=True)
        dx2 = dx3[part, :] + norm_backward(grad, table[pl.ds(2, 1), :], hat, inverse)
        dx1_out[part, :] = dx2
        dat = dx2.astype(BF16)
        dat_out[part, :] = dat
        grad_rows[part, :] = dot_nt(dat, attn_out[...]).astype(BF16)
    terms[pl.ds(2, 1), :] = gain2

    stream.flush(dat_out)
    stream.ready(3)
    zero = jnp.zeros((), BF16)
    sides = tuple((iota((1, LANES), 1) < DH) == (side == 0) for side in range(2))
    turned = tuple((iota((LANES, 1), 0) < DH) == (side == 0) for side in range(2))
    for pair in range(width // LANES):
        flipped[pl.ds(pair * LANES, LANES), :] = qkv[:, pl.ds(width + pair * LANES, LANES)].T
    dk[...] = jnp.zeros_like(dk)
    dv[...] = jnp.zeros_like(dv)

    def attend(part_index, carry):
        part = pl.ds(pl.multiple_of(part_index * 512, 512), 512)
        related = seg_col[...] == seg_row[:, part]
        for pair in range(width // LANES):
            own = pl.ds(pair * LANES, LANES)
            q = qkv[part, own]
            k = qkv[:, pl.ds(width + pair * LANES, LANES)]
            v = qkv[:, pl.ds(2 * width + pair * LANES, LANES)]
            da = grad_rows[part, own]
            dq = jnp.zeros((LANES, 512), F32)
            dk_sum = jnp.zeros((rows, LANES), F32)
            dv_sum = jnp.zeros((rows, LANES), F32)
            for side in range(2):
                head = 2 * pair + side
                q_side = jnp.where(sides[side], q, zero)
                da_side = jnp.where(sides[side], da, zero)
                scores = dot_nt(k, q_side) - lse[pl.ds(head, 1), part]
                probs = jnp.exp(jnp.where(related, scores, -MASK_FILL))
                dprobs = dot_nt(v, da_side)
                inner = jnp.sum(probs * dprobs, 0, keepdims=True)
                dscores = (probs * (dprobs - inner)).astype(BF16)
                dq += dot(jnp.where(turned[side], flipped[own, :], zero), dscores)
                dk_sum += dot(dscores, q_side)
                dv_sum += dot(probs.astype(BF16), da_side)
            dk[:, own] += dk_sum
            dv[:, own] += dv_sum
            dq = dq.T * DH**-0.5
            dproj_out[part, own] = (dq * cosine[part, :] - partner(dq) * sine[part, :]).astype(BF16)
        return carry

    lax.fori_loop(0, rows // 512, attend, 0)

    stream.ready(4)
    gain1 = jnp.zeros((1, width), F32)
    for part in chunks(rows, 256):
        for pair in range(width // LANES):
            own = pl.ds(pair * LANES, LANES)
            held = dk[part, own]
            dproj_out[part, pl.ds(width + pair * LANES, LANES)] = (
                held * cosine[part, :] - partner(held) * sine[part, :]
            ).astype(BF16)
            dproj_out[part, pl.ds(2 * width + pair * LANES, LANES)] = dv[part, own].astype(BF16)
        grad = dot_nt(dproj_out[part, :], attn_in[...])
        hat, inverse = normalize(x1[part, :])
        gain1 += jnp.sum(grad * hat, 0, keepdims=True)
        dx1 = dx1_out[part, :] + norm_backward(grad, table[pl.ds(1, 1), :], hat, inverse)
        dx1_out[part, :] = dx1
        gate_grad[part, :] = 0.5 * jnp.sum(expert[part, :].astype(F32) * dx1, 1, keepdims=True)
        rows_sent[part, :] = (0.5 * gate[part, :] * dx1).astype(BF16)
    terms[pl.ds(1, 1), :] = gain1
    stream.flush(dproj_out, dx1_out, gate_grad, terms)
    scatter_to(slot_row, rows_sent[...], sent)
    stream.flush(*sent)


def final_kernel(frames, blocks, slot_col, table, dx1, dz, embed_weight, _, out):
    for part in chunks(frames.shape[0], 128):
        grad = gathered(slot_col, blocks, part)
        hat, inverse = normalize(frames[part, :].astype(F32))
        dx0 = dx1[part, :] + norm_backward(grad, table[pl.ds(0, 1), :], hat, inverse)
        out[part, :] = dx0 + dot_nt(dz[part, :], embed_weight[...])


def after(value, *others):
    return lax.optimization_barrier((value,) + others)[0]


def shards(
    frames,
    lengths,
    choice_first,
    choice_second,
    embed_weight,
    routers,
    norm_gains,
    attn_in,
    attn_out,
    conv_in,
    conv_kernel,
    bn_shift,
    conv_out,
    expert_in,
    expert_out,
    cotangent,
):
    rows, width = frames.shape
    layers, slice_width, experts = routers.shape
    taps = conv_kernel.shape[0]
    gains = norm_gains.shape[0]
    peers = lax.axis_size("expert")
    dp_count = lax.axis_size("dp")
    dp_bits = bit_count(("dp",))
    capacity = 2 * rows // experts
    hidden = expert_in.shape[3]
    device = lax.axis_index(AXES)
    block = shaped((capacity, width), BF16)
    wide = shaped((rows, width), F32)
    low = shaped((rows, width), BF16)
    column = shaped((rows, 1), F32)

    dp_index = lax.axis_index("dp")[None]

    def shard_of(layer):
        first = expert_in[layer, 0]
        tiles = [first[:, start : start + width] for start in range(0, hidden, width)]
        return jnp.concatenate([expert_out[layer, 0]] + tiles, 0)

    first_weights = lax.all_gather(shard_of(0), "dp", axis=0)
    sent, slot_col1, slot_row1, slot_col2, slot_row2 = call(
        start_kernel,
        ([block] * peers, shaped((rows, 1), I32), shaped((1, rows), I32), shaped((rows, 1), I32), shaped((1, rows), I32)),
        lax.axis_index("expert")[None],
        frames,
        choice_first,
        choice_first.reshape(1, rows),
        choice_second,
        choice_second.reshape(1, rows),
        specs=[SMEM] + [None] * 5,
    )
    first_blocks = swap_blocks(sent)

    small_width = gains + taps + 1 + layers * experts
    small = jnp.concatenate(
        [
            norm_gains.T,
            conv_kernel.T,
            bn_shift[:, None],
            jnp.moveaxis(routers, 1, 0).reshape(slice_width, -1),
            jnp.zeros((slice_width, -small_width % LANES), BF16),
        ],
        1,
    )
    small = after(small, sent[0])
    small_all = gather_everywhere(small).reshape(width, LANES).astype(F32)
    table = small_all[:, : gains + taps + 3].T
    router_table = jnp.pad(
        small_all[:, gains + taps + 1 : small_width], ((0, 0), (0, LANES - layers * experts))
    )
    dense = jnp.concatenate([attn_in, attn_out, conv_in, conv_out], 1)
    dense = lax.all_to_all(
        jnp.broadcast_to(dense[None], (peers,) + dense.shape), "expert", split_axis=0, concat_axis=0, tiled=True
    )
    dense = lax.all_gather(
        dense.reshape(peers * slice_width, 7 * width), "dp", axis=0, tiled=True
    )
    second_weights = lax.all_gather(shard_of(1), "dp", axis=0)

    own_lengths = lax.dynamic_index_in_dim(lengths, device, 0, keepdims=False)
    frame_count = jnp.sum(lengths[:, :-1]).astype(F32)[None]
    (embed_pre, embedded, probs, gate1, gate2, seg_col, seg_row, tap_masks, offsets) = call(
        functools.partial(embed_kernel, experts),
        [
            wide,
            wide,
            shaped((rows, LANES), F32),
            column,
            column,
            shaped((rows, 1), I32),
            shaped((1, rows), I32),
            shaped((rows, LANES), F32),
            column,
        ],
        jnp.cumsum(own_lengths, dtype=I32)[:-1],
        frames,
        embed_weight,
        router_table,
        choice_first,
        choice_second,
        specs=[SMEM] + [None] * 5,
    )
    half = DH // 2
    frequency = 10000.0 ** (-jnp.arange(half, dtype=F32) / half)
    angles = offsets * jnp.tile(frequency, LANES // half)[None, :]
    sign = jnp.asarray(np.where(np.arange(LANES) % DH < half, -1.0, 1.0), F32)
    cosine, sine = jnp.cos(angles), jnp.sin(angles) * sign[None, :]

    def gain(number):
        return table[number : number + 1]

    first_results = swap_blocks(
        [expert_forward(block, gain(0), first_weights, hidden, True) for block in first_blocks]
    )

    def dense_spec(columns, start):
        return pl.BlockSpec((width, columns), lambda i: (0, start // columns))

    attn_in_spec = dense_spec(3 * width, 0)
    attn_out_spec = dense_spec(width, 3 * width)
    conv_in_spec = dense_spec(2 * width, 4 * width)
    conv_out_spec = dense_spec(width, 6 * width)
    sums_shape = shaped((8, width), F32)
    padded = pltpu.VMEM((rows + 16, width), F32)

    first_expert, x1, x2, ua, qkv, lse, attended, uc, gin, depth, moments = call(
        front_kernel,
        [
            low,
            wide,
            wide,
            low,
            shaped((rows, 3 * width), BF16),
            shaped((8, rows), F32),
            low,
            low,
            shaped((rows, 2 * width), F32),
            wide,
            sums_shape,
        ],
        frames,
        first_results,
        slot_col1,
        gate1,
        table,
        Columns(dense, 0, 3 * width),
        Columns(dense, 3 * width, width),
        Columns(dense, 4 * width, 2 * width),
        cosine,
        sine,
        seg_col,
        seg_row,
        tap_masks,
        stages=[0, 0, None, None, None, 1, 2, 2, 1, 1, None, None, 2],
        cost=20,
        scratch=[padded, pltpu.VMEM((width, rows), BF16)],
    )
    moments = sum_everywhere(moments)
    swish, x3, sent = call(
        middle_kernel,
        (low, wide, [block] * peers),
        frame_count,
        depth,
        moments,
        x2,
        table,
        Columns(dense, 6 * width, width),
        slot_row2,
        specs=[SMEM] + [None] * 6,
        stages=[None, 0, None, 0, None, 0, None],
        scratch=[pltpu.VMEM((rows, width), BF16)],
    )

    second_blocks = swap_blocks(sent)
    second_results = swap_blocks(
        [expert_forward(block, gain(3), second_weights, hidden, False) for block in second_blocks]
    )
    block_out, dx4, gate_grad2, gain4, sent = call(
        turn_kernel,
        (low, wide, column, shaped((1, width), F32), [block] * peers),
        x3,
        second_results,
        slot_col2,
        slot_row2,
        gate2,
        table,
        cotangent,
        seg_col,
        stages=[0, 0, None, None, None, None, 0, None],
        scratch=[pltpu.VMEM((rows, width), BF16)],
    )
    second_grads = swap_blocks(sent)
    backs = [
        expert_backward(block, grad, gain(3), second_weights, hidden, False)
        for block, grad in zip(second_blocks, second_grads)
    ]
    back, hid, pre_grads, inputs, _ = zip(*backs)
    second_back = swap_blocks(back)
    (second_grad,) = weight_grads(
        dp_index, inputs, second_grads, hid, pre_grads, dp_count, False
    )
    second_back[1] = after(second_back[1], second_grad)
    second_own = lax.psum_scatter(second_grad, "dp", scatter_dimension=0, tiled=True)[0]

    dx3, dco, dh, sums = call(
        conv_back_kernel,
        [wide, low, wide, sums_shape],
        frame_count,
        dx4,
        second_back,
        slot_col2,
        x3,
        table,
        Columns(dense, 6 * width, width),
        depth,
        moments,
        specs=[SMEM] + [None] * 8,
        stages=[None, 0, 0, None, 0, None, 0, 0, None],
    )
    all_sums = sum_everywhere(sums)
    dgin, dat, dproj, dx1, gate_grad1, terms, sent = call(
        back_kernel,
        (
            shaped((rows, 2 * width), BF16),
            low,
            shaped((rows, 3 * width), BF16),
            wide,
            column,
            shaped((24, width), F32),
            [block] * peers,
        ),
        frame_count,
        dh,
        depth,
        moments,
        all_sums,
        dx3,
        gin,
        x2,
        x1,
        table,
        Columns(dense, 4 * width, 2 * width),
        Columns(dense, 3 * width, width),
        Columns(dense, 0, 3 * width),
        qkv,
        lse,
        cosine,
        sine,
        seg_col,
        seg_row,
        tap_masks,
        first_expert,
        gate1,
        slot_row1,
        specs=[SMEM] + [None] * 22,
        stages=[None, 0, 0, None, None, 2, 1, 2, 4, None, 2, 2, 4, 3, 3, 3, 3, None, None, 1, 4, None, None],
        cost=30,
        scratch=[padded, padded, pltpu.VMEM((rows, width), BF16), pltpu.VMEM((rows, width), F32), pltpu.VMEM((rows, width), F32), pltpu.VMEM((rows, width), BF16), pltpu.VMEM((width, rows), BF16)],
    )
    first_grads = swap_blocks(sent)

    def dp_exchange(values, mask):
        return lax.ppermute(values, "dp", [(i, i ^ mask) for i in range(dp_count)])

    dense_part = shaped((dp_count // 2, 8 * width // dp_count, width), BF16)
    kept, moved, dz, router_terms = call(
        functools.partial(dense_grad_kernel, experts),
        (dense_part, dense_part, low, shaped((LANES, width), F32)),
        ua,
        dproj,
        attended,
        dat,
        uc,
        dgin,
        swish,
        dco,
        gate_grad1,
        gate1,
        choice_first,
        gate_grad2,
        gate2,
        choice_second,
        dp_index,
        probs,
        router_table,
        embed_pre,
        embedded,
        frames,
        specs=[None] * 14 + [SMEM] + [None] * 5,
        stages=[0, 0, 1, 1, 2, 2, 2, 2] + [None] * 8 + [None, 2, 2, 2],
        cost=1,
        scratch=[pltpu.VMEM((rows, LANES), F32), pltpu.VMEM((width, width), BF16)],
    )
    pairs = call(
        pair_kernel,
        [shaped(kept.shape[1:], BF16)] * (dp_count // 2),
        kept,
        dp_exchange(moved, 1),
        vmem=16,
        cost=10,
    )
    dense_own = pairs[0].astype(F32)
    for pair, mask in zip(pairs[1:], chip_masks()[1:]):
        dense_own = dense_own + dp_exchange(pair, mask).astype(F32)
    dense_own = dense_own.astype(BF16).reshape(8, peers, slice_width, width).transpose(1, 2, 0, 3)
    dense_own = lax.all_to_all(
        dense_own.reshape(peers, slice_width, 8 * width), "expert", split_axis=0, concat_axis=0, tiled=True
    )
    owned = [shaped((slice_width, count * width), F32) for count in (3, 1, 2, 1)]
    *dense_own, embed_own = call(
        dense_out_kernel,
        (*owned, shaped((slice_width, width), BF16)),
        dense_own,
        vmem=8,
        cost=10,
    )
    backs = [
        expert_backward(block, grad, gain(0), first_weights, hidden, True)
        for block, grad in zip(first_blocks, first_grads)
    ]
    back, hid, pre_grads, inputs, gain0 = zip(*backs)
    gain0 = sum(gain0)
    first_back = swap_blocks(back)
    kept, moved = weight_grads(dp_index, inputs, first_grads, hid, pre_grads, dp_count, True)
    moved = after(moved, *first_back[1:])

    pairs = call(
        pair_kernel,
        [shaped(kept.shape[1:], BF16)] * (dp_count // 2),
        kept,
        dp_exchange(moved, 1),
        vmem=16,
        cost=20,
    )
    first_parts = [
        dp_exchange(pair, mask) if mask else pair for pair, mask in zip(pairs, chip_masks())
    ]
    in_grad, out_grad = call(
        experts_out_kernel,
        (shaped((layers, 1, width // dp_count, hidden), F32), shaped((layers, 1, hidden // dp_count, width), F32)),
        first_parts,
        second_own,
        vmem=24,
        cost=10,
    )

    small_terms = jnp.concatenate(
        [
            gain0,
            terms[1:3],
            sums[4:5],
            gain4,
            sums[3:4],
            terms[6 : 6 + taps],
            sums[2:3],
            router_terms[: layers * experts],
        ],
        0,
    )
    small_terms = jnp.pad(small_terms.T, ((0, 0), (0, -small_width % 32)))
    lanes = small_terms.shape[1] * slice_width
    small_terms = jnp.pad(small_terms.reshape(-1, lanes), ((0, 0), (0, -lanes % width)))
    high = lax.reduce_precision(small_terms, 8, 7)
    split = jnp.stack([high, small_terms - high], 1).astype(BF16)
    split = split.reshape(split.shape[0], -1, width)
    split = jnp.pad(split, ((0, 0), (0, -split.shape[1] % 16), (0, 0)))
    mixed = jnp.concatenate([split, jnp.broadcast_to(embed_own[None], (split.shape[0],) + embed_own.shape)], 1)
    mixed = lax.all_to_all(mixed, AXES, split_axis=0, concat_axis=0, tiled=True)
    embed_total = mixed[:, split.shape[1] :].reshape(width, width).astype(F32)
    small_sums = jnp.sum(mixed[:, : split.shape[1]].astype(F32), 0)
    count = -(-lanes // width)
    small_sums = (small_sums[:count] + small_sums[count : 2 * count]).reshape(-1)[:lanes]
    small_sums = small_sums.reshape(slice_width, -1).T

    frames_grad = call(
        final_kernel,
        wide,
        frames,
        first_back,
        slot_col1,
        table,
        dx1,
        dz,
        embed_weight,
        second_own,
        specs=[None] * 7 + [ANY],
        cost=40,
    )
    return (
        block_out,
        frames_grad,
        embed_total,
        jnp.moveaxis(
            small_sums[gains + taps + 1 : small_width].reshape(layers, experts, slice_width), 1, 2
        ),
        small_sums[:gains],
        *dense_own[:3],
        small_sums[gains : gains + taps],
        small_sums[gains + taps],
        dense_own[3],
        in_grad,
        out_grad,
    )


def solution(mesh):
    in_specs = (
        P(("dp", "expert"), None),
        P(),
        P(("dp", "expert"), None),
        P(("dp", "expert"), None),
        P(),
        P(None, ("dp", "expert"), None),
        P(None, ("dp", "expert")),
        P(("dp", "expert"), None),
        P(("dp", "expert"), None),
        P(("dp", "expert"), None),
        P(None, ("dp", "expert")),
        P(("dp", "expert")),
        P(("dp", "expert"), None),
        P(None, "expert", "dp", None),
        P(None, "expert", "dp", None),
        P(("dp", "expert"), None),
    )
    out_specs = (
        P(("dp", "expert"), None),
        P(("dp", "expert"), None),
        P(),
        P(None, ("dp", "expert"), None),
        P(None, ("dp", "expert")),
        P(("dp", "expert"), None),
        P(("dp", "expert"), None),
        P(("dp", "expert"), None),
        P(None, ("dp", "expert")),
        P(("dp", "expert")),
        P(("dp", "expert"), None),
        P(None, "expert", "dp", None),
        P(None, "expert", "dp", None),
    )
    return jax.shard_map(shards, mesh=mesh, in_specs=in_specs, out_specs=out_specs, check_vma=False)
```

```python
import functools

import jax
import jax.numpy as jnp
import numpy as np
from jax import lax
from jax.experimental import pallas as pl
from jax.experimental.pallas import tpu as pltpu
from jax.sharding import PartitionSpec as P

H = 8
DH = 64
LANES = 128

EPSILON = 1e-05
MASK_FILL = 1000000000.0
HIGHEST = lax.Precision.HIGHEST
AXES = ("dp", "expert")
BF16 = jnp.bfloat16
F32 = jnp.float32
I32 = jnp.int32
MIB = 1 << 20


def bit_count(axes):
    total = 1
    for name in axes:
        total *= lax.axis_size(name)
    return total.bit_length() - 1


def exchange(values, axes, mask):
    total = 1 << bit_count(axes)
    return lax.ppermute(values, axes, [(i, i ^ mask) for i in range(total)])


def device_groups():
    z_bits = bit_count(("expert",))
    dp_bits = bit_count(("dp",))
    chips = list(range(z_bits + 1, z_bits + dp_bits))
    rests = [chips, list(range(z_bits))]
    return [[z_bits]] + [bits[i : i + 2] for bits in rests for i in range(0, len(bits), 2)]


def masks_of(bits):
    if len(bits) == 1:
        return [1 << bits[0]]
    low, high = 1 << bits[0], 1 << bits[1]
    return [low, high, low | high]


def terms_everywhere(values):
    groups = device_groups()
    for bits in groups[:-1]:
        arrived = [exchange(values, AXES, mask) for mask in masks_of(bits)]
        if len(arrived) == 1:
            values = values + arrived[0]
        else:
            values = (values + arrived[0]) + (arrived[1] + arrived[2])
    return [values] + [exchange(values, AXES, mask) for mask in masks_of(groups[-1])]


def total_of(terms):
    if len(terms) == 2:
        return terms[0][...] + terms[1][...]
    return (terms[0][...] + terms[1][...]) + (terms[2][...] + terms[3][...])


def gather_everywhere(values):
    total = 1 << bit_count(AXES)
    sent = jnp.broadcast_to(values[None], (total,) + values.shape)
    return lax.all_to_all(sent, AXES, split_axis=0, concat_axis=0, tiled=True)


def sum_to_owners(values, axes):
    arrived = lax.all_to_all(values, axes, split_axis=0, concat_axis=0, tiled=True)
    return jnp.sum(arrived.astype(F32), 0)


def swap_blocks(blocks):
    total = lax.axis_size("expert")
    moved = [blocks[0]]
    for k in range(1, total):
        moved.append(lax.ppermute(blocks[k], "expert", [(i, i ^ k) for i in range(total)]))
    return moved


def chip_masks():
    return [core << 1 for core in range(lax.axis_size("dp") // 2)]


class Columns:
    def __init__(self, array, start, count):
        self.array, self.start, self.count = array, start, count


class Stream:
    def __init__(self, arrivals, results, spare):
        self.arrivals, self.results = arrivals, results
        self.spare, self.spared = spare, 0
        self.waited, self.sent = set(), []
        self.begin(0)
        self.begin(1)

    def begin(self, stage):
        for copy in self.arrivals.get(stage, ()):
            copy.start()

    def ready(self, stage):
        for copy in self.arrivals.get(stage, ()):
            copy.wait()
        self.waited.add(stage)
        self.begin(stage + 2)

    def flush(self, *refs):
        for ref in refs:
            held, target, sem = self.results[id(ref)]
            self.send(held, target, sem)

    def flush_rows(self, ref, start, size):
        held, target, _ = self.results[id(ref)]
        rows = pl.ds(start, size)
        self.send(held.at[:, rows], target.at[:, rows], self.spare.at[self.spared])
        self.spared += 1

    def send(self, held, target, sem):
        copy = pltpu.make_async_copy(held, target, sem)
        copy.start()
        self.sent.append(copy)

    def finish(self):
        for copy in self.sent:
            copy.wait()


def call(body, outs, *args, specs=None, out_specs=None, scratch=(), stages=None, vmem=60, cost=5, **kw):
    vmem_spec = pl.BlockSpec(memory_space=pltpu.VMEM)
    any_spec = pl.BlockSpec(memory_space=pl.ANY)
    if specs is None:
        specs = [None] * len(args)
    columns = [arg if isinstance(arg, Columns) else None for arg in args]
    args = [arg.array if isinstance(arg, Columns) else arg for arg in args]
    grid = kw.pop("grid", (1,))
    scratch = list(scratch)
    if stages is None:
        specs = [
            jax.tree.map(lambda _: vmem_spec, arg) if spec is None else spec
            for spec, arg in zip(specs, args)
        ]
        if out_specs is None:
            out_specs = jax.tree.map(lambda _: vmem_spec, outs)
        wrapped = body
    else:
        specs = [
            spec if spec is not None else jax.tree.map(lambda _: vmem_spec if stage is None else any_spec, arg)
            for spec, arg, stage in zip(specs, args, stages)
        ]
        out_specs = jax.tree.map(lambda _: any_spec, outs)
        buffers = []
        for arg, part, stage in zip(args, columns, stages):
            if stage is not None:
                for leaf in jax.tree.leaves(arg):
                    shape = leaf.shape if part is None else (leaf.shape[0], part.count)
                    buffers.append(pltpu.VMEM(shape, leaf.dtype))
        out_leaves, out_tree = jax.tree.flatten(outs)
        buffers += [pltpu.VMEM(leaf.shape, leaf.dtype) for leaf in out_leaves]
        own_scratch, total = len(scratch), len(buffers)
        scratch = scratch + buffers + [pltpu.SemaphoreType.DMA((4,)), pltpu.SemaphoreType.DMA((total,))]

        def wrapped(*refs):
            refs = list(refs)
            ins, out_refs, rest = refs[: len(args)], refs[len(args) : len(args) + out_count], refs[len(args) + out_count :]
            own, held, spare, sems = rest[:own_scratch], rest[own_scratch:-2], rest[-2], rest[-1]
            arrivals, given, used = {}, [], 0
            for ref, part, stage in zip(ins, columns, stages):
                if stage is None:
                    given.append(ref)
                    continue
                leaves, tree = jax.tree.flatten(ref)
                landed = []
                for leaf in leaves:
                    source = leaf if part is None else leaf.at[:, pl.ds(part.start, part.count)]
                    arrivals.setdefault(stage, []).append(
                        pltpu.make_async_copy(source, held[used], sems.at[used])
                    )
                    landed.append(held[used])
                    used += 1
                given.append(jax.tree.unflatten(tree, landed))
            results, places = {}, []
            for ref in jax.tree.leaves(out_refs):
                results[id(held[used])] = (held[used], ref, sems.at[used])
                places.append(held[used])
                used += 1
            stream = Stream(arrivals, results, spare)
            given_outs = jax.tree.unflatten(out_tree, places)
            given_outs = list(given_outs) if isinstance(given_outs, (tuple, list)) else [given_outs]
            body(stream, *given, *given_outs, *own)
            stream.finish()

        out_count = len(outs) if isinstance(outs, (tuple, list)) else 1
    return pl.pallas_call(
        wrapped,
        out_shape=outs,
        in_specs=specs,
        out_specs=out_specs,
        scratch_shapes=scratch,
        grid=grid,
        compiler_params=pltpu.CompilerParams(vmem_limit_bytes=vmem * MIB),
        cost_estimate=pl.CostEstimate(flops=cost * 1153 * 10**6, bytes_accessed=0, transcendentals=0),
        **kw,
    )(*args)


def shaped(shape, dtype):
    return jax.ShapeDtypeStruct(shape, dtype)


SMEM = pl.BlockSpec(memory_space=pltpu.SMEM)
ANY = pl.BlockSpec(memory_space=pl.ANY)


def dot(left, right):
    return lax.dot_general(left, right, (((1,), (0,)), ((), ())), preferred_element_type=F32)


def dot_nt(left, right):
    return lax.dot_general(left, right, (((1,), (1,)), ((), ())), preferred_element_type=F32)


def dot_tn(left, right):
    return lax.dot_general(left, right, (((0,), (0,)), ((), ())), preferred_element_type=F32)


def iota(shape, dim):
    return lax.broadcasted_iota(I32, shape, dim)


def normalize(rows):
    centred = rows - jnp.mean(rows, -1, keepdims=True)
    inverse = lax.rsqrt(jnp.mean(centred * centred, -1, keepdims=True) + EPSILON)
    return centred * inverse, inverse


def norm_backward(grad, gain, hat, inverse):
    scaled = grad * gain
    return inverse * (
        scaled
        - jnp.mean(scaled, -1, keepdims=True)
        - hat * jnp.mean(scaled * hat, -1, keepdims=True)
    )


def sigmoid(values):
    return 1.0 / (1.0 + jnp.exp(-values))


def slope(values, logistic):
    return logistic * (1.0 + values * (1.0 - logistic))


def chunks(total, size):
    return [pl.ds(start, size) for start in range(0, total, size)]


def gathered(slot_col, blocks, rows):
    slot = slot_col[rows, :]
    total = None
    for k, block in enumerate(blocks):
        capacity = block.shape[0]
        pick = (slot == iota((slot.shape[0], capacity), 1) + k * capacity).astype(F32).astype(BF16)
        part = dot(pick, block[...])
        total = part if total is None else total + part
    return total


def scatter_to(slot_row, values, outs):
    for k, out in enumerate(outs):
        capacity = out.shape[0]
        pick = (slot_row[...] == iota((capacity, slot_row.shape[1]), 0) + k * capacity)
        out[...] = dot(pick.astype(F32).astype(BF16), values).astype(BF16)


def start_kernel(own, frames, col1, row1, col2, row2, sent, slot_col1, slot_row1, slot_col2, slot_row2):
    rows = frames.shape[0]
    capacity = sent[0].shape[0]
    below = (iota((rows, rows), 0) > iota((rows, rows), 1)).astype(F32).astype(BF16)
    above = (iota((rows, rows), 0) < iota((rows, rows), 1)).astype(F32).astype(BF16)
    for col, row, out_col, out_row in (
        (col1, row1, slot_col1, slot_row1),
        (col2, row2, slot_col2, slot_row2),
    ):
        hot = (col[...] == iota((rows, LANES), 1)).astype(F32)
        rank = jnp.sum(dot(below, hot.astype(BF16)) * hot, 1, keepdims=True)
        out_col[...] = (col[...] ^ own[0]) * capacity + rank.astype(I32)
        hot = (row[...] == iota((16, rows), 0)).astype(F32)
        rank = jnp.sum(dot(hot.astype(BF16), above) * hot, 0, keepdims=True)
        out_row[...] = (row[...] ^ own[0]) * capacity + rank.astype(I32)
    scatter_to(slot_row1, frames[...], sent)


def expert_specs(weights, hidden, tile):
    count, rows, width = weights.shape
    half = rows // 2
    in_rows = width // count
    first = pl.BlockSpec((count, in_rows, tile), lambda j: (0, half // in_rows + j, 0))
    second = pl.BlockSpec((tile // half, half, width), lambda j: (j, 0, 0))
    return first, second


def flat(ref):
    count, rows, width = ref.shape
    return ref[...].reshape(count * rows, width)


def expert_forward_kernel(with_norm, block, gain, w_in, w_out, out, total, inputs):
    step = pl.program_id(0)

    @pl.when(step == 0)
    def _():
        if with_norm:
            hat, _ = normalize(block[...].astype(F32))
            inputs[...] = (hat * gain[...]).astype(BF16)
        else:
            inputs[...] = block[...]
        total[...] = jnp.zeros_like(total)

    pre = dot(inputs[...], flat(w_in))
    hidden = (pre * sigmoid(pre)).astype(BF16)
    total[...] += dot(hidden, flat(w_out))

    @pl.when(step == pl.num_programs(0) - 1)
    def _():
        out[...] = total[...].astype(BF16)


def expert_forward(block, gain, weights, hidden, with_norm, tile=512):
    capacity, width = block.shape
    first, second = expert_specs(weights, hidden, tile)
    whole = pl.BlockSpec((capacity, width), lambda j: (0, 0))
    return call(
        functools.partial(expert_forward_kernel, with_norm),
        shaped((capacity, width), BF16),
        block,
        gain,
        weights,
        weights,
        specs=[whole, pl.BlockSpec((1, width), lambda j: (0, 0)), first, second],
        out_specs=whole,
        scratch=[pltpu.VMEM((capacity, width), F32), pltpu.VMEM((capacity, width), BF16)],
        grid=(hidden // tile,),
        vmem=12,
        cost=8,
    )


def expert_backward_kernel(
    with_norm, block, grad, gain, w_in, w_out, out, hidden_out, pre_grad_out, input_out, gain_out, total, hats
):
    step = pl.program_id(0)

    @pl.when(step == 0)
    def _():
        if with_norm:
            hat, _ = normalize(block[...].astype(F32))
            hats[...] = hat
            input_out[...] = (hat * gain[...]).astype(BF16)
        else:
            input_out[...] = block[...]
        total[...] = jnp.zeros_like(total)

    first, second = flat(w_in), flat(w_out)
    pre = dot(input_out[...], first)
    logistic = sigmoid(pre)
    hidden_out[...] = (pre * logistic).astype(BF16)
    hidden_grad = dot_nt(grad[...], second)
    pre_grad = (hidden_grad * slope(pre, logistic)).astype(BF16)
    pre_grad_out[...] = pre_grad
    total[...] += dot_nt(pre_grad, first)

    @pl.when(step == pl.num_programs(0) - 1)
    def _():
        back = total[...].astype(BF16)
        out[...] = back
        if with_norm:
            gain_out[...] = jnp.sum(back.astype(F32) * hats[...], 0, keepdims=True)
        else:
            gain_out[...] = jnp.zeros_like(gain_out)


def expert_backward(block, grad, gain, weights, hidden, with_norm, tile=512):
    capacity, width = block.shape
    first, second = expert_specs(weights, hidden, tile)
    whole = pl.BlockSpec((capacity, width), lambda j: (0, 0))
    tiled = pl.BlockSpec((capacity, tile), lambda j: (0, j))
    one = pl.BlockSpec((1, width), lambda j: (0, 0))
    return call(
        functools.partial(expert_backward_kernel, with_norm),
        (
            shaped((capacity, width), BF16),
            shaped((capacity, hidden), BF16),
            shaped((capacity, hidden), BF16),
            shaped((capacity, width), BF16),
            shaped((1, width), F32),
        ),
        block,
        grad,
        gain,
        weights,
        weights,
        specs=[whole, whole, one, first, second],
        out_specs=(whole, tiled, tiled, whole, one),
        scratch=[pltpu.VMEM((capacity, width), F32), pltpu.VMEM((capacity, width), F32)],
        grid=(hidden // tile,),
        vmem=16,
        cost=20,
    )


def weight_grad_kernel(relative, dp_index, inputs, grads, hidden, pre_grads, *refs):
    outs, (first, second) = refs[:-2], refs[-2:]
    step = pl.program_id(0)
    first_sum = second_sum = None
    for block, grad, hid, pre_grad in zip(inputs, grads, hidden, pre_grads):
        part = dot_tn(block[...], pre_grad[...])
        first_sum = part if first_sum is None else first_sum + part
        part = dot_tn(hid[...], grad[...])
        second_sum = part if second_sum is None else second_sum + part
    count = sum(out.shape[0] for out in outs)
    half = outs[0].shape[1] // 2
    in_rows = first_sum.shape[0] // count
    tile = second_sum.shape[0]
    owners = tile // half
    place = pl.ds(pl.multiple_of(half + step * in_rows, in_rows), in_rows)
    if not relative:
        for device in range(count):
            outs[0][device, place, :] = first_sum[device * in_rows : (device + 1) * in_rows].astype(BF16)
        for number in range(owners):
            outs[0][step * owners + number, pl.ds(0, half), :] = second_sum[
                number * half : (number + 1) * half
            ].astype(BF16)
    else:
        first[...] = first_sum.astype(BF16)
        for number in range(count):
            source = pl.multiple_of((dp_index[0] ^ number) * in_rows, in_rows)
            outs[number % 2][number // 2, place, :] = first[pl.ds(source, in_rows), :]
        second[...] = second_sum.astype(BF16)
        for number in range(owners):
            owner = (step * owners + number) ^ dp_index[0]

            @pl.when(owner % 2 == 0)
            def _():
                outs[0][owner // 2, pl.ds(0, half), :] = second[pl.ds(number * half, half), :]

            @pl.when(owner % 2 == 1)
            def _():
                outs[1][owner // 2, pl.ds(0, half), :] = second[pl.ds(number * half, half), :]


def weight_grads(dp_index, inputs, grads, hidden, pre_grads, count, relative, tile=512):
    capacity, width = inputs[0].shape
    units = hidden[0].shape[1]
    whole = pl.BlockSpec((capacity, width), lambda j: (0, 0))
    tiled = pl.BlockSpec((capacity, tile), lambda j: (0, j))
    rows = 2 * units // count
    if relative:
        outs = (shaped((count // 2, rows, width), BF16),) * 2
    else:
        outs = (shaped((count, rows, width), BF16),)
    peers = len(inputs)
    return call(
        functools.partial(weight_grad_kernel, relative),
        outs,
        dp_index,
        list(inputs),
        list(grads),
        list(hidden),
        list(pre_grads),
        specs=[SMEM, [whole] * peers, [whole] * peers, [tiled] * peers, [tiled] * peers],
        out_specs=tuple(pl.BlockSpec(o.shape, lambda j: (0, 0, 0)) for o in outs),
        scratch=[pltpu.VMEM((width, tile), BF16), pltpu.VMEM((tile, width), BF16)],
        grid=(units // tile,),
        vmem=28,
        cost=8,
    )


def dense_grad_kernel(
    experts, stream, ua, dproj, attended, dat, uc, dgin, swish, dco, gate_grad1, gate1, col1, gate_grad2, gate2, col2,
    dp_index, probs, routers, pre, embedded, frames, kept, moved, dz, router_terms, logits, term, turned,
):
    width = ua.shape[1]
    count = 2 * kept.shape[0]
    part_rows = width // count

    def place(left, right, tile):
        turned[...] = left[...].T
        for column in range(right.shape[1] // width):
            term[...] = dot(turned[...], right[:, pl.ds(column * width, width)]).astype(BF16)
            for number in range(count):
                source = pl.multiple_of((dp_index[0] ^ number) * part_rows, part_rows)
                target = moved if number % 2 else kept
                target[number // 2, pl.ds((tile + column) * part_rows, part_rows), :] = term[pl.ds(source, part_rows), :]

    rows = frames.shape[0]
    stream.ready(0)
    stream.ready(1)
    place(ua, dproj, 0)
    place(attended, dat, 3)
    for ref in (kept, moved):
        stream.flush_rows(ref, 0, 4 * part_rows)
    stream.ready(2)
    for part in chunks(rows, 256):
        lane = iota((256, LANES), 1)
        grad = jnp.zeros((256, LANES), F32)
        for number, (gate_grad, gate, col) in enumerate(((gate_grad1, gate1, col1), (gate_grad2, gate2, col2))):
            inside = (lane >= number * experts) & (lane < (number + 1) * experts)
            hot = (lane == col[part, :] + number * experts).astype(F32)
            scale = gate_grad[part, :] * gate[part, :]
            grad = jnp.where(inside, scale * (hot - probs[part, :]), grad)
        logits[part, :] = grad
        demb = dot_nt(grad.astype(BF16), routers[...].astype(BF16))
        held = pre[part, :]
        dz[part, :] = (demb * slope(held, sigmoid(held))).astype(BF16)
    router_terms[...] = dot(logits[...].T.astype(BF16), embedded[...].astype(BF16))
    stream.flush(dz, router_terms)
    place(uc, dgin, 4)
    place(swish, dco, 6)
    place(frames, dz, 7)
    for ref in (kept, moved):
        stream.flush_rows(ref, 4 * part_rows, 4 * part_rows)


def sum_kernel(parts, out):
    total = parts[0][...].astype(F32)
    for part in parts[1:]:
        total = total + part[...].astype(F32)
    out[...] = total.astype(BF16)


def pair_kernel(kept, moved, *outs):
    for number, out in enumerate(outs):
        out[...] = (kept[number].astype(F32) + moved[number].astype(F32)).astype(BF16)


def experts_out_kernel(parts, second, in_out, out_out):
    _, _, in_rows, hidden = in_out.shape
    width = out_out.shape[3]
    half = out_out.shape[2]

    first = parts[0][...].astype(F32)
    for part in parts[1:]:
        first = first + part[...].astype(F32)
    for layer, values in ((0, first), (1, second[...].astype(F32))):
        out_out[layer, 0] = values[:half]
        for tile in range(hidden // width):
            rows = values[half + tile * in_rows : half + (tile + 1) * in_rows]
            in_out[layer, 0, :, tile * width : (tile + 1) * width] = rows


def dense_out_kernel(arrived, *outs):
    start = 0
    for out in outs:
        lanes = pl.ds(start, out.shape[1])
        total = arrived[0, :, lanes].astype(F32)
        for number in range(1, arrived.shape[0]):
            total = total + arrived[number, :, lanes].astype(F32)
        out[...] = total.astype(out.dtype)
        start += out.shape[1]


def embed_kernel(experts, ends, frames, weight, routers, col1, col2, pre_out, embedded_out, probs_out, gate1, gate2, seg_col, seg_row, taps_out, offset_out):
    rows = frames.shape[0]
    for part in chunks(rows, 256):
        pre = dot(frames[part, :], weight[...])
        pre_out[part, :] = pre
        embedded = pre * sigmoid(pre)
        embedded_out[part, :] = embedded
        logits = jnp.dot(embedded, routers[...], precision=HIGHEST, preferred_element_type=F32)
        lane = iota(logits.shape, 1)
        probs = jnp.zeros_like(logits)
        for number, (col, gate) in enumerate(((col1, gate1), (col2, gate2))):
            inside = (lane >= number * experts) & (lane < (number + 1) * experts)
            top = jnp.max(jnp.where(inside, logits, -MASK_FILL), 1, keepdims=True)
            weights = jnp.where(inside, jnp.exp(jnp.where(inside, logits - top, 0.0)), 0.0)
            own = weights / jnp.sum(weights, 1, keepdims=True)
            hot = lane == col[part, :] + number * experts
            gate[part, :] = jnp.sum(jnp.where(hot, own, 0.0), 1, keepdims=True)
            probs = probs + own
        probs_out[part, :] = probs

    def segment_of(place):
        found = jnp.zeros(place.shape, I32)
        for number in range(3):
            found += (place >= ends[number]).astype(I32)
        return found

    segment = segment_of(iota((rows, 1), 0))
    seg_col[...] = segment
    seg_row[...] = segment_of(iota((1, rows), 1))
    place = iota((rows, LANES), 0) + iota((rows, LANES), 1) - 7
    same = (segment_of(place) == segment) & (place >= 0) & (place < rows)
    taps_out[...] = same.astype(F32)
    first = jnp.zeros((rows, 1), I32)
    for number in range(3):
        first = jnp.where(segment > number, ends[number], first)
    offset_out[...] = (iota((rows, 1), 0) - first).astype(F32)


def partner(values):
    half = DH // 2
    lane = iota(values.shape, 1)
    return jnp.where(lane % DH < half, pltpu.roll(values, LANES - half, 1), pltpu.roll(values, half, 1))


def shifts(padded, part):
    size = part.size
    for offset in range(8):
        held = padded[pl.ds(part.start + offset, size + 8), :]
        if offset:
            yield offset - 1, held[:size]
        yield offset + 7, held[8:]


def folded(values):
    return jnp.sum(values.reshape(-1, 8, values.shape[1]), 0)


def front_kernel(
    stream, frames, blocks, slot_col, gate, table, attn_in, attn_out, conv_in, cosine, sine, seg_col, seg_row, taps,
    expert_out, x1_out, x2_out, ua_out, qkv_out, lse_out, attended_out, uc_out, gin_out, depth_out, moments,
    padded, flipped,
):
    rows, width = frames.shape
    gains = lambda n: table[pl.ds(n, 1), :]
    stream.ready(0)
    for part in chunks(rows, 256):
        found = gathered(slot_col, blocks, part)
        expert_out[part, :] = found.astype(BF16)
        x1 = frames[part, :].astype(F32) + 0.5 * gate[part, :] * found
        x1_out[part, :] = x1
        hat, _ = normalize(x1)
        ua_out[part, :] = (hat * gains(1)).astype(BF16)
    stream.flush(expert_out, x1_out, ua_out)
    stream.ready(1)
    for part in chunks(rows, 256):
        ua = ua_out[part, :]
        for piece in range(3 * width // LANES):
            lanes = pl.ds(piece * LANES, LANES)
            if piece % 2 == 0:
                pair = dot(ua, attn_in[:, pl.ds(piece * LANES, 2 * LANES)])
            values = pair[:, :LANES] if piece % 2 == 0 else pair[:, LANES:]
            if piece < 2 * width // LANES:
                values = values * cosine[part, :] + partner(values) * sine[part, :]
            if piece < width // LANES:
                values = values * DH**-0.5
            qkv_out[part, lanes] = values.astype(BF16)

    stream.flush(qkv_out)
    zero = jnp.zeros((), BF16)
    sides = tuple((iota((1, LANES), 1) < DH) == (side == 0) for side in range(2))
    turned = tuple((iota((LANES, 1), 0) < DH) == (side == 0) for side in range(2))
    for pair in range(width // LANES):
        flipped[pl.ds(pair * LANES, LANES), :] = qkv_out[:, pl.ds(2 * width + pair * LANES, LANES)].T

    def attend(part_index, carry):
        part = pl.ds(pl.multiple_of(part_index * 512, 512), 512)
        related = seg_col[...] == seg_row[:, part]
        for pair in range(width // LANES):
            q = qkv_out[part, pl.ds(pair * LANES, LANES)]
            k = qkv_out[:, pl.ds(width + pair * LANES, LANES)]
            v = flipped[pl.ds(pair * LANES, LANES), :]
            result = jnp.zeros((LANES, 512), F32)
            for side in range(2):
                scores = dot_nt(k, jnp.where(sides[side], q, zero))
                scores = jnp.where(related, scores, -MASK_FILL)
                top = jnp.max(scores, 0, keepdims=True)
                weights = jnp.exp(scores - top)
                summed = jnp.sum(weights, 0, keepdims=True)
                probs = (weights * (1.0 / summed)).astype(BF16)
                result += dot(jnp.where(turned[side], v, zero), probs)
                lse_out[pl.ds(2 * pair + side, 1), part] = top + jnp.log(summed)
            attended_out[part, pl.ds(pair * LANES, LANES)] = result.T.astype(BF16)
        return carry

    lax.fori_loop(0, rows // 512, attend, 0)
    stream.flush(attended_out, lse_out)
    stream.ready(2)

    edge = jnp.zeros((8, width), F32)
    padded[pl.ds(0, 8), :] = edge
    padded[pl.ds(rows + 8, 8), :] = edge
    for part in chunks(rows, 256):
        x2 = x1_out[part, :] + dot(attended_out[part, :], attn_out[...])
        x2_out[part, :] = x2
        hat, _ = normalize(x2)
        uc = (hat * gains(2)).astype(BF16)
        uc_out[part, :] = uc
        gin = dot(uc, conv_in[...])
        gin_out[part, :] = gin
        padded[pl.ds(part.start + 8, 256), :] = gin[:, :width] * sigmoid(gin[:, width:])

    stream.flush(x2_out, uc_out, gin_out)
    sums = jnp.zeros((1, width), F32)
    squares = jnp.zeros((1, width), F32)
    for part in chunks(rows, 64):
        depth = jnp.zeros((64, width), F32)
        for tap, shifted in shifts(padded, part):
            depth += table[pl.ds(6 + tap, 1), :] * shifted * taps[part, pl.ds(tap, 1)]
        depth_out[part, :] = depth
        weighted = jnp.where(seg_col[part, :] < 3, depth, 0.0)
        sums += jnp.sum(weighted, 0, keepdims=True)
        squares += jnp.sum(weighted * depth, 0, keepdims=True)
    moments[pl.ds(0, 1), :] = sums
    moments[pl.ds(1, 1), :] = squares
    moments[pl.ds(2, 6), :] = jnp.zeros((6, width), F32)
    stream.flush(depth_out, moments)


def batch_terms(moments, frame_count):
    mean = moments[pl.ds(0, 1), :] / frame_count[0]
    variance = moments[pl.ds(1, 1), :] / frame_count[0] - mean * mean
    return mean, lax.rsqrt(variance + EPSILON)


def middle_kernel(frame_count, depth, terms, x2, table, conv_out, slot_row, swish_out, x3_out, moments, sent, normed):
    rows, width = depth.shape
    moments[...] = total_of(terms)
    mean, scale = batch_terms(moments, frame_count)
    for part in chunks(rows, 256):
        bn = (depth[part, :] - mean) * scale * table[pl.ds(5, 1), :] + table[pl.ds(21, 1), :]
        swish = (bn * sigmoid(bn)).astype(BF16)
        swish_out[part, :] = swish
        x3 = x2[part, :] + dot(swish, conv_out[...])
        x3_out[part, :] = x3
        hat, _ = normalize(x3)
        normed[part, :] = (hat * table[pl.ds(3, 1), :]).astype(BF16)
    scatter_to(slot_row, normed[...], sent)


def turn_kernel(
    x3, blocks, slot_col, slot_row, gate, table, cotangent, seg_col,
    block_out, dx4_out, gate_grad, gain_out, sent, grads,
):
    rows, width = x3.shape
    gain = table[pl.ds(4, 1), :]
    gain_sum = jnp.zeros((1, width), F32)
    for part in chunks(rows, 256):
        found = gathered(slot_col, blocks, part)
        half = 0.5 * gate[part, :]
        x4 = x3[part, :] + half * found
        hat, inverse = normalize(x4)
        valid = seg_col[part, :] < 3
        block_out[part, :] = jnp.where(valid, hat * gain, 0.0).astype(BF16)
        grad = jnp.where(valid, cotangent[part, :].astype(F32), 0.0)
        gain_sum += jnp.sum(grad * hat, 0, keepdims=True)
        dx4 = norm_backward(grad, gain, hat, inverse)
        dx4_out[part, :] = dx4
        gate_grad[part, :] = 0.5 * jnp.sum(found * dx4, 1, keepdims=True)
        grads[part, :] = (half * dx4).astype(BF16)
    gain_out[...] = gain_sum
    scatter_to(slot_row, grads[...], sent)


def conv_back_kernel(
    frame_count, dx4, blocks, slot_col, x3, table, conv_out, depth, moments,
    dx3_out, dco_out, dh_out, sums,
):
    rows, width = x3.shape
    mean, scale = batch_terms(moments, frame_count)
    total = jnp.zeros((1, width), F32)
    moment = jnp.zeros((1, width), F32)
    shift = jnp.zeros((1, width), F32)
    gain5 = jnp.zeros((1, width), F32)
    gain3 = jnp.zeros((1, width), F32)
    for part in chunks(rows, 256):
        grad = gathered(slot_col, blocks, part)
        hat, inverse = normalize(x3[part, :])
        gain3 += jnp.sum(grad * hat, 0, keepdims=True)
        dx3 = dx4[part, :] + norm_backward(grad, table[pl.ds(3, 1), :], hat, inverse)
        dx3_out[part, :] = dx3
        dco = dx3.astype(BF16)
        dco_out[part, :] = dco
        centred = depth[part, :] - mean
        hat = centred * scale
        bn = hat * table[pl.ds(5, 1), :] + table[pl.ds(21, 1), :]
        dbn = dot_nt(dco, conv_out[...]) * slope(bn, sigmoid(bn))
        shift += jnp.sum(dbn, 0, keepdims=True)
        gain5 += jnp.sum(dbn * hat, 0, keepdims=True)
        dh = dbn * table[pl.ds(5, 1), :]
        dh_out[part, :] = dh
        total += jnp.sum(dh, 0, keepdims=True)
        moment += jnp.sum(dh * centred, 0, keepdims=True)
    for number, row in enumerate((total, moment, shift, gain5, gain3)):
        sums[pl.ds(number, 1), :] = row
    sums[pl.ds(5, 3), :] = jnp.zeros((3, width), F32)


def back_kernel(
    stream, frame_count, dh, depth, moments, sum_terms, dx3, gin, x2, x1, table, conv_in, attn_out, attn_in, qkv, lse,
    cosine, sine, seg_col, seg_row, taps, expert, gate, slot_row,
    dgin_out, dat_out, dproj_out, dx1_out, gate_grad, terms, sent,
    padded, glu, grad_rows, dk, dv, rows_sent, flipped,
):
    rows, width = dh.shape
    mean, scale = batch_terms(moments, frame_count)
    sums = total_of(sum_terms)
    total, moment = sums[0:1], sums[1:2]
    var_grad = -0.5 * moment * scale * scale * scale
    mean_grad = -scale * total - 2.0 * mean * var_grad
    edge = jnp.zeros((8, width), F32)
    for ref in (padded, glu):
        ref[pl.ds(0, 8), :] = edge
        ref[pl.ds(rows + 8, 8), :] = edge
    stream.ready(0)
    for part in chunks(rows, 64):
        held = depth[part, :]
        grad = (mean_grad + 2.0 * held * var_grad) * (1.0 / frame_count[0])
        padded[pl.ds(part.start + 8, 64), :] = dh[part, :] * scale + jnp.where(seg_col[part, :] < 3, grad, 0.0)
    stream.ready(1)
    for part in chunks(rows, 64):
        glu[pl.ds(part.start + 8, 64), :] = gin[part, :width] * sigmoid(gin[part, width:])
    kernel_sums = [jnp.zeros((8, width), F32) for _ in range(15)]
    gain2 = jnp.zeros((1, width), F32)
    for part in chunks(rows, 64):
        dglu = jnp.zeros((64, width), F32)
        own = padded[pl.ds(part.start + 8, 64), :]
        for (tap, grad), (_, value) in zip(shifts(padded, part), shifts(glu, part)):
            mask = taps[part, pl.ds(tap, 1)]
            dglu += table[pl.ds(20 - tap, 1), :] * grad * mask
            kernel_sums[tap] += folded(own * value * mask)
        logistic = sigmoid(gin[part, width:])
        dgin_out[part, :width] = (dglu * logistic).astype(BF16)
        dgin_out[part, width:] = (dglu * gin[part, :width] * logistic * (1.0 - logistic)).astype(BF16)
    for tap in range(15):
        terms[pl.ds(6 + tap, 1), :] = jnp.sum(kernel_sums[tap], 0, keepdims=True)
    stream.flush(dgin_out)
    stream.ready(2)
    for part in chunks(rows, 256):
        grad = dot_nt(dgin_out[part, :], conv_in[...])
        hat, inverse = normalize(x2[part, :])
        gain2 += jnp.sum(grad * hat, 0, keepdims=True)
        dx2 = dx3[part, :] + norm_backward(grad, table[pl.ds(2, 1), :], hat, inverse)
        dx1_out[part, :] = dx2
        dat = dx2.astype(BF16)
        dat_out[part, :] = dat
        grad_rows[part, :] = dot_nt(dat, attn_out[...]).astype(BF16)
    terms[pl.ds(2, 1), :] = gain2

    stream.flush(dat_out)
    stream.ready(3)
    zero = jnp.zeros((), BF16)
    sides = tuple((iota((1, LANES), 1) < DH) == (side == 0) for side in range(2))
    turned = tuple((iota((LANES, 1), 0) < DH) == (side == 0) for side in range(2))
    for pair in range(width // LANES):
        flipped[pl.ds(pair * LANES, LANES), :] = qkv[:, pl.ds(width + pair * LANES, LANES)].T
    dk[...] = jnp.zeros_like(dk)
    dv[...] = jnp.zeros_like(dv)

    def attend(part_index, carry):
        part = pl.ds(pl.multiple_of(part_index * 512, 512), 512)
        related = seg_col[...] == seg_row[:, part]
        for pair in range(width // LANES):
            own = pl.ds(pair * LANES, LANES)
            q = qkv[part, own]
            k = qkv[:, pl.ds(width + pair * LANES, LANES)]
            v = qkv[:, pl.ds(2 * width + pair * LANES, LANES)]
            da = grad_rows[part, own]
            dq = jnp.zeros((LANES, 512), F32)
            dk_sum = jnp.zeros((rows, LANES), F32)
            dv_sum = jnp.zeros((rows, LANES), F32)
            for side in range(2):
                head = 2 * pair + side
                q_side = jnp.where(sides[side], q, zero)
                da_side = jnp.where(sides[side], da, zero)
                scores = dot_nt(k, q_side) - lse[pl.ds(head, 1), part]
                probs = jnp.exp(jnp.where(related, scores, -MASK_FILL))
                dprobs = dot_nt(v, da_side)
                inner = jnp.sum(probs * dprobs, 0, keepdims=True)
                dscores = (probs * (dprobs - inner)).astype(BF16)
                dq += dot(jnp.where(turned[side], flipped[own, :], zero), dscores)
                dk_sum += dot(dscores, q_side)
                dv_sum += dot(probs.astype(BF16), da_side)
            dk[:, own] += dk_sum
            dv[:, own] += dv_sum
            dq = dq.T * DH**-0.5
            dproj_out[part, own] = (dq * cosine[part, :] - partner(dq) * sine[part, :]).astype(BF16)
        return carry

    lax.fori_loop(0, rows // 512, attend, 0)

    stream.ready(4)
    gain1 = jnp.zeros((1, width), F32)
    for part in chunks(rows, 256):
        for pair in range(width // LANES):
            own = pl.ds(pair * LANES, LANES)
            held = dk[part, own]
            dproj_out[part, pl.ds(width + pair * LANES, LANES)] = (
                held * cosine[part, :] - partner(held) * sine[part, :]
            ).astype(BF16)
            dproj_out[part, pl.ds(2 * width + pair * LANES, LANES)] = dv[part, own].astype(BF16)
        grad = dot_nt(dproj_out[part, :], attn_in[...])
        hat, inverse = normalize(x1[part, :])
        gain1 += jnp.sum(grad * hat, 0, keepdims=True)
        dx1 = dx1_out[part, :] + norm_backward(grad, table[pl.ds(1, 1), :], hat, inverse)
        dx1_out[part, :] = dx1
        gate_grad[part, :] = 0.5 * jnp.sum(expert[part, :].astype(F32) * dx1, 1, keepdims=True)
        rows_sent[part, :] = (0.5 * gate[part, :] * dx1).astype(BF16)
    terms[pl.ds(1, 1), :] = gain1
    stream.flush(dproj_out, dx1_out, gate_grad, terms)
    scatter_to(slot_row, rows_sent[...], sent)
    stream.flush(*sent)


def final_kernel(frames, blocks, slot_col, table, dx1, dz, embed_weight, _, out):
    for part in chunks(frames.shape[0], 128):
        grad = gathered(slot_col, blocks, part)
        hat, inverse = normalize(frames[part, :].astype(F32))
        dx0 = dx1[part, :] + norm_backward(grad, table[pl.ds(0, 1), :], hat, inverse)
        out[part, :] = dx0 + dot_nt(dz[part, :], embed_weight[...])


def after(value, *others):
    return lax.optimization_barrier((value,) + others)[0]


def shards(
    frames,
    lengths,
    choice_first,
    choice_second,
    embed_weight,
    routers,
    norm_gains,
    attn_in,
    attn_out,
    conv_in,
    conv_kernel,
    bn_shift,
    conv_out,
    expert_in,
    expert_out,
    cotangent,
):
    rows, width = frames.shape
    layers, slice_width, experts = routers.shape
    taps = conv_kernel.shape[0]
    gains = norm_gains.shape[0]
    peers = lax.axis_size("expert")
    dp_count = lax.axis_size("dp")
    dp_bits = bit_count(("dp",))
    capacity = 2 * rows // experts
    hidden = expert_in.shape[3]
    device = lax.axis_index(AXES)
    block = shaped((capacity, width), BF16)
    wide = shaped((rows, width), F32)
    low = shaped((rows, width), BF16)
    column = shaped((rows, 1), F32)

    dp_index = lax.axis_index("dp")[None]

    def shard_of(layer):
        first = expert_in[layer, 0]
        tiles = [first[:, start : start + width] for start in range(0, hidden, width)]
        return jnp.concatenate([expert_out[layer, 0]] + tiles, 0)

    first_weights = lax.all_gather(shard_of(0), "dp", axis=0)
    sent, slot_col1, slot_row1, slot_col2, slot_row2 = call(
        start_kernel,
        ([block] * peers, shaped((rows, 1), I32), shaped((1, rows), I32), shaped((rows, 1), I32), shaped((1, rows), I32)),
        lax.axis_index("expert")[None],
        frames,
        choice_first,
        choice_first.reshape(1, rows),
        choice_second,
        choice_second.reshape(1, rows),
        specs=[SMEM] + [None] * 5,
    )
    first_blocks = swap_blocks(sent)

    small_width = gains + taps + 1 + layers * experts
    small = jnp.concatenate(
        [
            norm_gains.T,
            conv_kernel.T,
            bn_shift[:, None],
            jnp.moveaxis(routers, 1, 0).reshape(slice_width, -1),
            jnp.zeros((slice_width, -small_width % LANES), BF16),
        ],
        1,
    )
    small = after(small, sent[0])
    small_all = gather_everywhere(small).reshape(width, LANES).astype(F32)
    table = small_all[:, : gains + taps + 3].T
    router_table = jnp.pad(
        small_all[:, gains + taps + 1 : small_width], ((0, 0), (0, LANES - layers * experts))
    )
    dense = jnp.concatenate([attn_in, attn_out, conv_in, conv_out], 1)
    dense = lax.all_to_all(
        jnp.broadcast_to(dense[None], (peers,) + dense.shape), "expert", split_axis=0, concat_axis=0, tiled=True
    )
    dense = lax.all_gather(
        dense.reshape(peers * slice_width, 7 * width), "dp", axis=0, tiled=True
    )
    second_weights = lax.all_gather(shard_of(1), "dp", axis=0)

    own_lengths = lax.dynamic_index_in_dim(lengths, device, 0, keepdims=False)
    frame_count = jnp.sum(lengths[:, :-1]).astype(F32)[None]
    (embed_pre, embedded, probs, gate1, gate2, seg_col, seg_row, tap_masks, offsets) = call(
        functools.partial(embed_kernel, experts),
        [
            wide,
            wide,
            shaped((rows, LANES), F32),
            column,
            column,
            shaped((rows, 1), I32),
            shaped((1, rows), I32),
            shaped((rows, LANES), F32),
            column,
        ],
        jnp.cumsum(own_lengths, dtype=I32)[:-1],
        frames,
        embed_weight,
        router_table,
        choice_first,
        choice_second,
        specs=[SMEM] + [None] * 5,
    )
    half = DH // 2
    frequency = 10000.0 ** (-jnp.arange(half, dtype=F32) / half)
    angles = offsets * jnp.tile(frequency, LANES // half)[None, :]
    sign = jnp.asarray(np.where(np.arange(LANES) % DH < half, -1.0, 1.0), F32)
    cosine, sine = jnp.cos(angles), jnp.sin(angles) * sign[None, :]

    def gain(number):
        return table[number : number + 1]

    first_results = swap_blocks(
        [expert_forward(block, gain(0), first_weights, hidden, True) for block in first_blocks]
    )

    def dense_spec(columns, start):
        return pl.BlockSpec((width, columns), lambda i: (0, start // columns))

    attn_in_spec = dense_spec(3 * width, 0)
    attn_out_spec = dense_spec(width, 3 * width)
    conv_in_spec = dense_spec(2 * width, 4 * width)
    conv_out_spec = dense_spec(width, 6 * width)
    sums_shape = shaped((8, width), F32)
    padded = pltpu.VMEM((rows + 16, width), F32)

    first_expert, x1, x2, ua, qkv, lse, attended, uc, gin, depth, moments = call(
        front_kernel,
        [
            low,
            wide,
            wide,
            low,
            shaped((rows, 3 * width), BF16),
            shaped((8, rows), F32),
            low,
            low,
            shaped((rows, 2 * width), F32),
            wide,
            sums_shape,
        ],
        frames,
        first_results,
        slot_col1,
        gate1,
        table,
        Columns(dense, 0, 3 * width),
        Columns(dense, 3 * width, width),
        Columns(dense, 4 * width, 2 * width),
        cosine,
        sine,
        seg_col,
        seg_row,
        tap_masks,
        stages=[0, 0, None, None, None, 1, 2, 2, 1, 1, None, None, 2],
        cost=20,
        scratch=[padded, pltpu.VMEM((width, rows), BF16)],
    )
    moment_terms = terms_everywhere(moments)
    swish, x3, moments, sent = call(
        middle_kernel,
        (low, wide, sums_shape, [block] * peers),
        frame_count,
        depth,
        moment_terms,
        x2,
        table,
        dense,
        slot_row2,
        specs=[SMEM] + [None] * 4 + [conv_out_spec, None],
        scratch=[pltpu.VMEM((rows, width), BF16)],
    )

    second_blocks = swap_blocks(sent)
    second_results = swap_blocks(
        [expert_forward(block, gain(3), second_weights, hidden, False) for block in second_blocks]
    )
    block_out, dx4, gate_grad2, gain4, sent = call(
        turn_kernel,
        (low, wide, column, shaped((1, width), F32), [block] * peers),
        x3,
        second_results,
        slot_col2,
        slot_row2,
        gate2,
        table,
        cotangent,
        seg_col,
        scratch=[pltpu.VMEM((rows, width), BF16)],
    )
    second_grads = swap_blocks(sent)
    backs = [
        expert_backward(block, grad, gain(3), second_weights, hidden, False)
        for block, grad in zip(second_blocks, second_grads)
    ]
    back, hid, pre_grads, inputs, _ = zip(*backs)
    second_back = swap_blocks(back)
    (second_grad,) = weight_grads(
        dp_index, inputs, second_grads, hid, pre_grads, dp_count, False
    )
    second_back[1] = after(second_back[1], second_grad)
    second_own = lax.psum_scatter(second_grad, "dp", scatter_dimension=0, tiled=True)[0]

    dx3, dco, dh, sums = call(
        conv_back_kernel,
        [wide, low, wide, sums_shape],
        frame_count,
        dx4,
        second_back,
        slot_col2,
        x3,
        table,
        dense,
        depth,
        moments,
        specs=[SMEM] + [None] * 5 + [conv_out_spec] + [None] * 2,
    )
    all_sums = terms_everywhere(sums)
    dgin, dat, dproj, dx1, gate_grad1, terms, sent = call(
        back_kernel,
        (
            shaped((rows, 2 * width), BF16),
            low,
            shaped((rows, 3 * width), BF16),
            wide,
            column,
            shaped((24, width), F32),
            [block] * peers,
        ),
        frame_count,
        dh,
        depth,
        moments,
        all_sums,
        dx3,
        gin,
        x2,
        x1,
        table,
        Columns(dense, 4 * width, 2 * width),
        Columns(dense, 3 * width, width),
        Columns(dense, 0, 3 * width),
        qkv,
        lse,
        cosine,
        sine,
        seg_col,
        seg_row,
        tap_masks,
        first_expert,
        gate1,
        slot_row1,
        specs=[SMEM] + [None] * 22,
        stages=[None, 0, 0, None, None, 2, 1, 2, 4, None, 2, 2, 4, 3, 3, 3, 3, None, None, 1, 4, None, None],
        cost=30,
        scratch=[padded, padded, pltpu.VMEM((rows, width), BF16), pltpu.VMEM((rows, width), F32), pltpu.VMEM((rows, width), F32), pltpu.VMEM((rows, width), BF16), pltpu.VMEM((width, rows), BF16)],
    )
    first_grads = swap_blocks(sent)

    def dp_exchange(values, mask):
        return lax.ppermute(values, "dp", [(i, i ^ mask) for i in range(dp_count)])

    dense_part = shaped((dp_count // 2, 8 * width // dp_count, width), BF16)
    kept, moved, dz, router_terms = call(
        functools.partial(dense_grad_kernel, experts),
        (dense_part, dense_part, low, shaped((LANES, width), F32)),
        ua,
        dproj,
        attended,
        dat,
        uc,
        dgin,
        swish,
        dco,
        gate_grad1,
        gate1,
        choice_first,
        gate_grad2,
        gate2,
        choice_second,
        dp_index,
        probs,
        router_table,
        embed_pre,
        embedded,
        frames,
        specs=[None] * 14 + [SMEM] + [None] * 5,
        stages=[0, 0, 1, 1, 2, 2, 2, 2] + [None] * 8 + [None, 2, 2, 2],
        cost=1,
        scratch=[pltpu.VMEM((rows, LANES), F32), pltpu.VMEM((width, width), BF16), pltpu.VMEM((width, rows), BF16)],
    )
    pairs = call(
        pair_kernel,
        [shaped(kept.shape[1:], BF16)] * (dp_count // 2),
        kept,
        dp_exchange(moved, 1),
        vmem=16,
        cost=10,
    )
    dense_own = call(
        sum_kernel,
        shaped(pairs[0].shape, BF16),
        [dp_exchange(pair, mask) if mask else pair for pair, mask in zip(pairs, chip_masks())],
        vmem=8,
        cost=60,
    )
    dense_own = dense_own.reshape(8, peers, slice_width, width).transpose(1, 2, 0, 3)
    backs = [
        expert_backward(block, grad, gain(0), first_weights, hidden, True)
        for block, grad in zip(first_blocks, first_grads)
    ]
    back, hid, pre_grads, inputs, gain0 = zip(*backs)
    gain0 = sum(gain0)
    first_back = swap_blocks(back)
    kept, moved = weight_grads(dp_index, inputs, first_grads, hid, pre_grads, dp_count, True)
    moved = after(moved, *first_back[1:])

    pairs = call(
        pair_kernel,
        [shaped(kept.shape[1:], BF16)] * (dp_count // 2),
        kept,
        dp_exchange(moved, 1),
        vmem=16,
        cost=20,
    )
    dense_own = after(dense_own, *pairs)
    dense_own = lax.all_to_all(
        dense_own.reshape(peers, slice_width, 8 * width), "expert", split_axis=0, concat_axis=0, tiled=True
    )
    first_parts = [
        dp_exchange(pair, mask) if mask else pair for pair, mask in zip(pairs, chip_masks())
    ]
    owned = [shaped((slice_width, count * width), F32) for count in (3, 1, 2, 1)]
    *dense_own, embed_own = call(
        dense_out_kernel,
        (*owned, shaped((slice_width, width), BF16)),
        dense_own,
        vmem=8,
        cost=10,
    )
    in_grad, out_grad = call(
        experts_out_kernel,
        (shaped((layers, 1, width // dp_count, hidden), F32), shaped((layers, 1, hidden // dp_count, width), F32)),
        first_parts,
        second_own,
        vmem=24,
        cost=10,
    )

    small_terms = jnp.concatenate(
        [
            gain0,
            terms[1:3],
            sums[4:5],
            gain4,
            sums[3:4],
            terms[6 : 6 + taps],
            sums[2:3],
            router_terms[: layers * experts],
        ],
        0,
    )
    small_terms = small_terms.T
    high = lax.reduce_precision(small_terms, 8, 7)
    split = jnp.concatenate([high, small_terms - high], 1).astype(BF16)
    split = jnp.pad(split, ((0, 0), (0, LANES - 2 * small_width))).reshape(-1, slice_width, LANES)
    mixed = jnp.concatenate([jnp.broadcast_to(embed_own[None], (split.shape[0],) + embed_own.shape), split], 2)
    mixed = lax.all_to_all(mixed, AXES, split_axis=0, concat_axis=0, tiled=True)
    embed_total = mixed[:, :, :width].reshape(width, width).astype(F32)
    small_sums = jnp.sum(mixed[:, :, width:].astype(F32), 0)
    small_sums = (small_sums[:, :small_width] + small_sums[:, small_width : 2 * small_width]).T

    frames_grad = call(
        final_kernel,
        wide,
        frames,
        first_back,
        slot_col1,
        table,
        dx1,
        dz,
        embed_weight,
        second_own,
        specs=[None] * 7 + [ANY],
        cost=40,
    )
    return (
        block_out,
        frames_grad,
        embed_total,
        jnp.moveaxis(
            small_sums[gains + taps + 1 : small_width].reshape(layers, experts, slice_width), 1, 2
        ),
        small_sums[:gains],
        *dense_own[:3],
        small_sums[gains : gains + taps],
        small_sums[gains + taps],
        dense_own[3],
        in_grad,
        out_grad,
    )


def solution(mesh):
    in_specs = (
        P(("dp", "expert"), None),
        P(),
        P(("dp", "expert"), None),
        P(("dp", "expert"), None),
        P(),
        P(None, ("dp", "expert"), None),
        P(None, ("dp", "expert")),
        P(("dp", "expert"), None),
        P(("dp", "expert"), None),
        P(("dp", "expert"), None),
        P(None, ("dp", "expert")),
        P(("dp", "expert")),
        P(("dp", "expert"), None),
        P(None, "expert", "dp", None),
        P(None, "expert", "dp", None),
        P(("dp", "expert"), None),
    )
    out_specs = (
        P(("dp", "expert"), None),
        P(("dp", "expert"), None),
        P(),
        P(None, ("dp", "expert"), None),
        P(None, ("dp", "expert")),
        P(("dp", "expert"), None),
        P(("dp", "expert"), None),
        P(("dp", "expert"), None),
        P(None, ("dp", "expert")),
        P(("dp", "expert")),
        P(("dp", "expert"), None),
        P(None, "expert", "dp", None),
        P(None, "expert", "dp", None),
    )
    return jax.shard_map(shards, mesh=mesh, in_specs=in_specs, out_specs=out_specs, check_vma=False)
```

```python
import functools

import jax
import jax.numpy as jnp
import numpy as np
from jax import lax
from jax.experimental import pallas as pl
from jax.experimental.pallas import tpu as pltpu
from jax.sharding import PartitionSpec as P

H = 8
DH = 64
LANES = 128

EPSILON = 1e-05
MASK_FILL = 1000000000.0
HIGHEST = lax.Precision.HIGHEST
AXES = ("dp", "expert")
BF16 = jnp.bfloat16
F32 = jnp.float32
I32 = jnp.int32
MIB = 1 << 20


def bit_count(axes):
    total = 1
    for name in axes:
        total *= lax.axis_size(name)
    return total.bit_length() - 1


def exchange(values, axes, mask):
    total = 1 << bit_count(axes)
    return lax.ppermute(values, axes, [(i, i ^ mask) for i in range(total)])


def device_groups():
    z_bits = bit_count(("expert",))
    dp_bits = bit_count(("dp",))
    chips = list(range(z_bits + 1, z_bits + dp_bits))
    rests = [chips, list(range(z_bits))]
    return [[z_bits]] + [bits[i : i + 2] for bits in rests for i in range(0, len(bits), 2)]


def masks_of(bits):
    if len(bits) == 1:
        return [1 << bits[0]]
    low, high = 1 << bits[0], 1 << bits[1]
    return [low, high, low | high]


def terms_everywhere(values):
    groups = device_groups()
    for bits in groups[:-1]:
        arrived = [exchange(values, AXES, mask) for mask in masks_of(bits)]
        if len(arrived) == 1:
            values = values + arrived[0]
        else:
            values = (values + arrived[0]) + (arrived[1] + arrived[2])
    return [values] + [exchange(values, AXES, mask) for mask in masks_of(groups[-1])]


def total_of(terms):
    if len(terms) == 2:
        return terms[0][...] + terms[1][...]
    return (terms[0][...] + terms[1][...]) + (terms[2][...] + terms[3][...])


def gather_everywhere(values):
    total = 1 << bit_count(AXES)
    sent = jnp.broadcast_to(values[None], (total,) + values.shape)
    return lax.all_to_all(sent, AXES, split_axis=0, concat_axis=0, tiled=True)


def sum_to_owners(values, axes):
    arrived = lax.all_to_all(values, axes, split_axis=0, concat_axis=0, tiled=True)
    return jnp.sum(arrived.astype(F32), 0)


def swap_blocks(blocks):
    total = lax.axis_size("expert")
    moved = [blocks[0]]
    for k in range(1, total):
        moved.append(lax.ppermute(blocks[k], "expert", [(i, i ^ k) for i in range(total)]))
    return moved


def chip_masks():
    return [core << 1 for core in range(lax.axis_size("dp") // 2)]


class Columns:
    def __init__(self, array, start, count):
        self.array, self.start, self.count = array, start, count


class Stream:
    def __init__(self, arrivals, results, spare):
        self.arrivals, self.results = arrivals, results
        self.spare, self.spared = spare, 0
        self.waited, self.sent = set(), []
        self.begin(0)
        self.begin(1)

    def begin(self, stage):
        for copy in self.arrivals.get(stage, ()):
            copy.start()

    def ready(self, stage):
        for copy in self.arrivals.get(stage, ()):
            copy.wait()
        self.waited.add(stage)
        self.begin(stage + 2)

    def flush(self, *refs):
        for ref in refs:
            held, target, sem = self.results[id(ref)]
            self.send(held, target, sem)

    def flush_rows(self, ref, start, size):
        held, target, _ = self.results[id(ref)]
        rows = pl.ds(start, size)
        self.send(held.at[:, rows], target.at[:, rows], self.spare.at[self.spared])
        self.spared += 1

    def send(self, held, target, sem):
        copy = pltpu.make_async_copy(held, target, sem)
        copy.start()
        self.sent.append(copy)

    def finish(self):
        for copy in self.sent:
            copy.wait()


def call(body, outs, *args, specs=None, out_specs=None, scratch=(), stages=None, vmem=60, cost=5, **kw):
    vmem_spec = pl.BlockSpec(memory_space=pltpu.VMEM)
    any_spec = pl.BlockSpec(memory_space=pl.ANY)
    if specs is None:
        specs = [None] * len(args)
    columns = [arg if isinstance(arg, Columns) else None for arg in args]
    args = [arg.array if isinstance(arg, Columns) else arg for arg in args]
    grid = kw.pop("grid", (1,))
    scratch = list(scratch)
    if stages is None:
        specs = [
            jax.tree.map(lambda _: vmem_spec, arg) if spec is None else spec
            for spec, arg in zip(specs, args)
        ]
        if out_specs is None:
            out_specs = jax.tree.map(lambda _: vmem_spec, outs)
        wrapped = body
    else:
        specs = [
            spec if spec is not None else jax.tree.map(lambda _: vmem_spec if stage is None else any_spec, arg)
            for spec, arg, stage in zip(specs, args, stages)
        ]
        out_specs = jax.tree.map(lambda _: any_spec, outs)
        buffers = []
        for arg, part, stage in zip(args, columns, stages):
            if stage is not None:
                for leaf in jax.tree.leaves(arg):
                    shape = leaf.shape if part is None else (leaf.shape[0], part.count)
                    buffers.append(pltpu.VMEM(shape, leaf.dtype))
        out_leaves, out_tree = jax.tree.flatten(outs)
        buffers += [pltpu.VMEM(leaf.shape, leaf.dtype) for leaf in out_leaves]
        own_scratch, total = len(scratch), len(buffers)
        scratch = scratch + buffers + [pltpu.SemaphoreType.DMA((4,)), pltpu.SemaphoreType.DMA((total,))]

        def wrapped(*refs):
            refs = list(refs)
            ins, out_refs, rest = refs[: len(args)], refs[len(args) : len(args) + out_count], refs[len(args) + out_count :]
            own, held, spare, sems = rest[:own_scratch], rest[own_scratch:-2], rest[-2], rest[-1]
            arrivals, given, used = {}, [], 0
            for ref, part, stage in zip(ins, columns, stages):
                if stage is None:
                    given.append(ref)
                    continue
                leaves, tree = jax.tree.flatten(ref)
                landed = []
                for leaf in leaves:
                    source = leaf if part is None else leaf.at[:, pl.ds(part.start, part.count)]
                    arrivals.setdefault(stage, []).append(
                        pltpu.make_async_copy(source, held[used], sems.at[used])
                    )
                    landed.append(held[used])
                    used += 1
                given.append(jax.tree.unflatten(tree, landed))
            results, places = {}, []
            for ref in jax.tree.leaves(out_refs):
                results[id(held[used])] = (held[used], ref, sems.at[used])
                places.append(held[used])
                used += 1
            stream = Stream(arrivals, results, spare)
            given_outs = jax.tree.unflatten(out_tree, places)
            given_outs = list(given_outs) if isinstance(given_outs, (tuple, list)) else [given_outs]
            body(stream, *given, *given_outs, *own)
            stream.finish()

        out_count = len(outs) if isinstance(outs, (tuple, list)) else 1
    return pl.pallas_call(
        wrapped,
        out_shape=outs,
        in_specs=specs,
        out_specs=out_specs,
        scratch_shapes=scratch,
        grid=grid,
        compiler_params=pltpu.CompilerParams(vmem_limit_bytes=vmem * MIB),
        cost_estimate=pl.CostEstimate(flops=cost * 1153 * 10**6, bytes_accessed=0, transcendentals=0),
        **kw,
    )(*args)


def shaped(shape, dtype):
    return jax.ShapeDtypeStruct(shape, dtype)


SMEM = pl.BlockSpec(memory_space=pltpu.SMEM)
ANY = pl.BlockSpec(memory_space=pl.ANY)


def dot(left, right):
    return lax.dot_general(left, right, (((1,), (0,)), ((), ())), preferred_element_type=F32)


def dot_nt(left, right):
    return lax.dot_general(left, right, (((1,), (1,)), ((), ())), preferred_element_type=F32)


def dot_tn(left, right):
    return lax.dot_general(left, right, (((0,), (0,)), ((), ())), preferred_element_type=F32)


def iota(shape, dim):
    return lax.broadcasted_iota(I32, shape, dim)


def normalize(rows):
    centred = rows - jnp.mean(rows, -1, keepdims=True)
    inverse = lax.rsqrt(jnp.mean(centred * centred, -1, keepdims=True) + EPSILON)
    return centred * inverse, inverse


def norm_backward(grad, gain, hat, inverse):
    scaled = grad * gain
    return inverse * (
        scaled
        - jnp.mean(scaled, -1, keepdims=True)
        - hat * jnp.mean(scaled * hat, -1, keepdims=True)
    )


def sigmoid(values):
    return 1.0 / (1.0 + jnp.exp(-values))


def slope(values, logistic):
    return logistic * (1.0 + values * (1.0 - logistic))


def chunks(total, size):
    return [pl.ds(start, size) for start in range(0, total, size)]


def gathered(slot_col, blocks, rows):
    slot = slot_col[rows, :]
    total = None
    for k, block in enumerate(blocks):
        capacity = block.shape[0]
        pick = (slot == iota((slot.shape[0], capacity), 1) + k * capacity).astype(F32).astype(BF16)
        part = dot(pick, block[...])
        total = part if total is None else total + part
    return total


def scatter_to(slot_row, values, outs):
    for k, out in enumerate(outs):
        capacity = out.shape[0]
        pick = (slot_row[...] == iota((capacity, slot_row.shape[1]), 0) + k * capacity)
        out[...] = dot(pick.astype(F32).astype(BF16), values).astype(BF16)


def start_kernel(own, frames, col1, row1, col2, row2, sent, slot_col1, slot_row1, slot_col2, slot_row2):
    rows = frames.shape[0]
    capacity = sent[0].shape[0]
    below = (iota((rows, rows), 0) > iota((rows, rows), 1)).astype(F32).astype(BF16)
    above = (iota((rows, rows), 0) < iota((rows, rows), 1)).astype(F32).astype(BF16)
    for col, row, out_col, out_row in (
        (col1, row1, slot_col1, slot_row1),
        (col2, row2, slot_col2, slot_row2),
    ):
        hot = (col[...] == iota((rows, LANES), 1)).astype(F32)
        rank = jnp.sum(dot(below, hot.astype(BF16)) * hot, 1, keepdims=True)
        out_col[...] = (col[...] ^ own[0]) * capacity + rank.astype(I32)
        hot = (row[...] == iota((16, rows), 0)).astype(F32)
        rank = jnp.sum(dot(hot.astype(BF16), above) * hot, 0, keepdims=True)
        out_row[...] = (row[...] ^ own[0]) * capacity + rank.astype(I32)
    scatter_to(slot_row1, frames[...], sent)


def expert_specs(weights, hidden, tile):
    count, rows, width = weights.shape
    half = rows // 2
    in_rows = width // count
    rows = in_rows * (tile // width)
    first = pl.BlockSpec((count, rows, width), lambda j: (0, half // rows + j, 0))
    second = pl.BlockSpec((tile // half, half, width), lambda j: (j, 0, 0))
    return first, second


def tiles_of(w_in, w_out):
    count, rows, width = w_in.shape
    owners, half, _ = w_out.shape
    tiles = owners * half // width
    in_rows, per_tile = rows // tiles, owners // tiles
    for tile in range(tiles):
        first = w_in[:, tile * in_rows : (tile + 1) * in_rows, :].reshape(count * in_rows, width)
        second = w_out[tile * per_tile : (tile + 1) * per_tile].reshape(width, width)
        yield pl.ds(tile * width, width), first, second


def expert_forward_kernel(with_norm, block, gain, w_in, w_out, out, total, inputs):
    step = pl.program_id(0)

    @pl.when(step == 0)
    def _():
        if with_norm:
            hat, _ = normalize(block[...].astype(F32))
            inputs[...] = (hat * gain[...]).astype(BF16)
        else:
            inputs[...] = block[...]
        total[...] = jnp.zeros_like(total)

    for _, first, second in tiles_of(w_in, w_out):
        pre = dot(inputs[...], first)
        hidden = (pre * sigmoid(pre)).astype(BF16)
        total[...] += dot(hidden, second)

    @pl.when(step == pl.num_programs(0) - 1)
    def _():
        out[...] = total[...].astype(BF16)


def expert_forward(block, gain, weights, hidden, with_norm, tile=1024):
    capacity, width = block.shape
    first, second = expert_specs(weights, hidden, tile)
    whole = pl.BlockSpec((capacity, width), lambda j: (0, 0))
    return call(
        functools.partial(expert_forward_kernel, with_norm),
        shaped((capacity, width), BF16),
        block,
        gain,
        weights,
        weights,
        specs=[whole, pl.BlockSpec((1, width), lambda j: (0, 0)), first, second],
        out_specs=whole,
        scratch=[pltpu.VMEM((capacity, width), F32), pltpu.VMEM((capacity, width), BF16)],
        grid=(hidden // tile,),
        vmem=16,
        cost=8,
    )


def expert_backward_kernel(
    with_norm, block, grad, gain, w_in, w_out, out, hidden_out, pre_grad_out, input_out, gain_out, total, hats
):
    step = pl.program_id(0)

    @pl.when(step == 0)
    def _():
        if with_norm:
            hat, _ = normalize(block[...].astype(F32))
            hats[...] = hat
            input_out[...] = (hat * gain[...]).astype(BF16)
        else:
            input_out[...] = block[...]
        total[...] = jnp.zeros_like(total)

    for lanes, first, second in tiles_of(w_in, w_out):
        pre = dot(input_out[...], first)
        logistic = sigmoid(pre)
        hidden_out[:, lanes] = (pre * logistic).astype(BF16)
        hidden_grad = dot_nt(grad[...], second)
        pre_grad = (hidden_grad * slope(pre, logistic)).astype(BF16)
        pre_grad_out[:, lanes] = pre_grad
        total[...] += dot_nt(pre_grad, first)

    @pl.when(step == pl.num_programs(0) - 1)
    def _():
        back = total[...].astype(BF16)
        out[...] = back
        if with_norm:
            gain_out[...] = jnp.sum(back.astype(F32) * hats[...], 0, keepdims=True)
        else:
            gain_out[...] = jnp.zeros_like(gain_out)


def expert_backward(block, grad, gain, weights, hidden, with_norm, tile=1024):
    capacity, width = block.shape
    first, second = expert_specs(weights, hidden, tile)
    whole = pl.BlockSpec((capacity, width), lambda j: (0, 0))
    tiled = pl.BlockSpec((capacity, tile), lambda j: (0, j))
    one = pl.BlockSpec((1, width), lambda j: (0, 0))
    return call(
        functools.partial(expert_backward_kernel, with_norm),
        (
            shaped((capacity, width), BF16),
            shaped((capacity, hidden), BF16),
            shaped((capacity, hidden), BF16),
            shaped((capacity, width), BF16),
            shaped((1, width), F32),
        ),
        block,
        grad,
        gain,
        weights,
        weights,
        specs=[whole, whole, one, first, second],
        out_specs=(whole, tiled, tiled, whole, one),
        scratch=[pltpu.VMEM((capacity, width), F32), pltpu.VMEM((capacity, width), F32)],
        grid=(hidden // tile,),
        vmem=24,
        cost=20,
    )


def weight_grad_kernel(relative, dp_index, inputs, grads, hidden, pre_grads, *refs):
    outs, (first, second) = refs[:-2], refs[-2:]
    step = pl.program_id(0)
    first_sum = second_sum = None
    for block, grad, hid, pre_grad in zip(inputs, grads, hidden, pre_grads):
        part = dot_tn(block[...], pre_grad[...])
        first_sum = part if first_sum is None else first_sum + part
        part = dot_tn(hid[...], grad[...])
        second_sum = part if second_sum is None else second_sum + part
    count = sum(out.shape[0] for out in outs)
    half = outs[0].shape[1] // 2
    in_rows = first_sum.shape[0] // count
    tile = second_sum.shape[0]
    owners = tile // half
    place = pl.ds(pl.multiple_of(half + step * in_rows, in_rows), in_rows)
    if not relative:
        for device in range(count):
            outs[0][device, place, :] = first_sum[device * in_rows : (device + 1) * in_rows].astype(BF16)
        for number in range(owners):
            outs[0][step * owners + number, pl.ds(0, half), :] = second_sum[
                number * half : (number + 1) * half
            ].astype(BF16)
    else:
        first[...] = first_sum.astype(BF16)
        for number in range(count):
            source = pl.multiple_of((dp_index[0] ^ number) * in_rows, in_rows)
            outs[number % 2][number // 2, place, :] = first[pl.ds(source, in_rows), :]
        second[...] = second_sum.astype(BF16)
        for number in range(owners):
            owner = (step * owners + number) ^ dp_index[0]

            @pl.when(owner % 2 == 0)
            def _():
                outs[0][owner // 2, pl.ds(0, half), :] = second[pl.ds(number * half, half), :]

            @pl.when(owner % 2 == 1)
            def _():
                outs[1][owner // 2, pl.ds(0, half), :] = second[pl.ds(number * half, half), :]


def weight_grads(dp_index, inputs, grads, hidden, pre_grads, count, relative, tile=512):
    capacity, width = inputs[0].shape
    units = hidden[0].shape[1]
    whole = pl.BlockSpec((capacity, width), lambda j: (0, 0))
    tiled = pl.BlockSpec((capacity, tile), lambda j: (0, j))
    rows = 2 * units // count
    if relative:
        outs = (shaped((count // 2, rows, width), BF16),) * 2
    else:
        outs = (shaped((count, rows, width), BF16),)
    peers = len(inputs)
    return call(
        functools.partial(weight_grad_kernel, relative),
        outs,
        dp_index,
        list(inputs),
        list(grads),
        list(hidden),
        list(pre_grads),
        specs=[SMEM, [whole] * peers, [whole] * peers, [tiled] * peers, [tiled] * peers],
        out_specs=tuple(pl.BlockSpec(o.shape, lambda j: (0, 0, 0)) for o in outs),
        scratch=[pltpu.VMEM((width, tile), BF16), pltpu.VMEM((tile, width), BF16)],
        grid=(units // tile,),
        vmem=28,
        cost=8,
    )


def dense_grad_kernel(
    experts, stream, ua, dproj, attended, dat, uc, dgin, swish, dco, gate_grad1, gate1, col1, gate_grad2, gate2, col2,
    dp_index, probs, routers, pre, embedded, frames, kept, moved, dz, router_terms, logits, term, turned,
):
    width = ua.shape[1]
    count = 2 * kept.shape[0]
    part_rows = width // count

    def place(left, right, tile):
        turned[...] = left[...].T
        for column in range(right.shape[1] // width):
            term[...] = dot(turned[...], right[:, pl.ds(column * width, width)]).astype(BF16)
            for number in range(count):
                source = pl.multiple_of((dp_index[0] ^ number) * part_rows, part_rows)
                target = moved if number % 2 else kept
                target[number // 2, pl.ds((tile + column) * part_rows, part_rows), :] = term[pl.ds(source, part_rows), :]

    rows = frames.shape[0]
    stream.ready(0)
    stream.ready(1)
    place(ua, dproj, 0)
    place(attended, dat, 3)
    for ref in (kept, moved):
        stream.flush_rows(ref, 0, 4 * part_rows)
    stream.ready(2)
    for part in chunks(rows, 256):
        lane = iota((256, LANES), 1)
        grad = jnp.zeros((256, LANES), F32)
        for number, (gate_grad, gate, col) in enumerate(((gate_grad1, gate1, col1), (gate_grad2, gate2, col2))):
            inside = (lane >= number * experts) & (lane < (number + 1) * experts)
            hot = (lane == col[part, :] + number * experts).astype(F32)
            scale = gate_grad[part, :] * gate[part, :]
            grad = jnp.where(inside, scale * (hot - probs[part, :]), grad)
        logits[part, :] = grad
        demb = dot_nt(grad.astype(BF16), routers[...].astype(BF16))
        held = pre[part, :]
        dz[part, :] = (demb * slope(held, sigmoid(held))).astype(BF16)
    router_terms[...] = dot(logits[...].T.astype(BF16), embedded[...].astype(BF16))
    stream.flush(dz, router_terms)
    place(uc, dgin, 4)
    place(swish, dco, 6)
    place(frames, dz, 7)
    for ref in (kept, moved):
        stream.flush_rows(ref, 4 * part_rows, 4 * part_rows)


def sum_kernel(parts, out):
    total = parts[0][...].astype(F32)
    for part in parts[1:]:
        total = total + part[...].astype(F32)
    out[...] = total.astype(BF16)


def pair_kernel(kept, moved, *outs):
    for number, out in enumerate(outs):
        out[...] = (kept[number].astype(F32) + moved[number].astype(F32)).astype(BF16)


def experts_out_kernel(parts, second, in_out, out_out):
    _, _, in_rows, hidden = in_out.shape
    width = out_out.shape[3]
    half = out_out.shape[2]

    first = parts[0][...].astype(F32)
    for part in parts[1:]:
        first = first + part[...].astype(F32)
    for layer, values in ((0, first), (1, second[...].astype(F32))):
        out_out[layer, 0] = values[:half]
        for tile in range(hidden // width):
            rows = values[half + tile * in_rows : half + (tile + 1) * in_rows]
            in_out[layer, 0, :, tile * width : (tile + 1) * width] = rows


def dense_out_kernel(arrived, *outs):
    start = 0
    for out in outs:
        lanes = pl.ds(start, out.shape[1])
        total = arrived[0, :, lanes].astype(F32)
        for number in range(1, arrived.shape[0]):
            total = total + arrived[number, :, lanes].astype(F32)
        out[...] = total.astype(out.dtype)
        start += out.shape[1]


def embed_kernel(experts, ends, frames, weight, routers, col1, col2, pre_out, embedded_out, probs_out, gate1, gate2, seg_col, seg_row, taps_out, offset_out):
    rows = frames.shape[0]
    for part in chunks(rows, 256):
        pre = dot(frames[part, :], weight[...])
        pre_out[part, :] = pre
        embedded = pre * sigmoid(pre)
        embedded_out[part, :] = embedded
        logits = jnp.dot(embedded, routers[...], precision=HIGHEST, preferred_element_type=F32)
        lane = iota(logits.shape, 1)
        probs = jnp.zeros_like(logits)
        for number, (col, gate) in enumerate(((col1, gate1), (col2, gate2))):
            inside = (lane >= number * experts) & (lane < (number + 1) * experts)
            top = jnp.max(jnp.where(inside, logits, -MASK_FILL), 1, keepdims=True)
            weights = jnp.where(inside, jnp.exp(jnp.where(inside, logits - top, 0.0)), 0.0)
            own = weights / jnp.sum(weights, 1, keepdims=True)
            hot = lane == col[part, :] + number * experts
            gate[part, :] = jnp.sum(jnp.where(hot, own, 0.0), 1, keepdims=True)
            probs = probs + own
        probs_out[part, :] = probs

    def segment_of(place):
        found = jnp.zeros(place.shape, I32)
        for number in range(3):
            found += (place >= ends[number]).astype(I32)
        return found

    segment = segment_of(iota((rows, 1), 0))
    seg_col[...] = segment
    seg_row[...] = segment_of(iota((1, rows), 1))
    place = iota((rows, LANES), 0) + iota((rows, LANES), 1) - 7
    same = (segment_of(place) == segment) & (place >= 0) & (place < rows)
    taps_out[...] = same.astype(F32)
    first = jnp.zeros((rows, 1), I32)
    for number in range(3):
        first = jnp.where(segment > number, ends[number], first)
    offset_out[...] = (iota((rows, 1), 0) - first).astype(F32)


def partner(values):
    half = DH // 2
    lane = iota(values.shape, 1)
    return jnp.where(lane % DH < half, pltpu.roll(values, LANES - half, 1), pltpu.roll(values, half, 1))


def shifts(padded, part):
    size = part.size
    for offset in range(8):
        held = padded[pl.ds(part.start + offset, size + 8), :]
        if offset:
            yield offset - 1, held[:size]
        yield offset + 7, held[8:]


def folded(values):
    return jnp.sum(values.reshape(-1, 8, values.shape[1]), 0)


def front_kernel(
    stream, frames, blocks, slot_col, gate, table, attn_in, attn_out, conv_in, cosine, sine, seg_col, seg_row, taps,
    expert_out, x1_out, x2_out, ua_out, qkv_out, lse_out, attended_out, uc_out, gin_out, depth_out, moments,
    padded, flipped,
):
    rows, width = frames.shape
    gains = lambda n: table[pl.ds(n, 1), :]
    stream.ready(0)
    for part in chunks(rows, 256):
        found = gathered(slot_col, blocks, part)
        expert_out[part, :] = found.astype(BF16)
        x1 = frames[part, :].astype(F32) + 0.5 * gate[part, :] * found
        x1_out[part, :] = x1
        hat, _ = normalize(x1)
        ua_out[part, :] = (hat * gains(1)).astype(BF16)
    stream.flush(expert_out, x1_out, ua_out)
    stream.ready(1)
    for part in chunks(rows, 256):
        ua = ua_out[part, :]
        for piece in range(3 * width // LANES):
            lanes = pl.ds(piece * LANES, LANES)
            if piece % 2 == 0:
                pair = dot(ua, attn_in[:, pl.ds(piece * LANES, 2 * LANES)])
            values = pair[:, :LANES] if piece % 2 == 0 else pair[:, LANES:]
            if piece < 2 * width // LANES:
                values = values * cosine[part, :] + partner(values) * sine[part, :]
            if piece < width // LANES:
                values = values * DH**-0.5
            qkv_out[part, lanes] = values.astype(BF16)

    stream.flush(qkv_out)
    zero = jnp.zeros((), BF16)
    sides = tuple((iota((1, LANES), 1) < DH) == (side == 0) for side in range(2))
    turned = tuple((iota((LANES, 1), 0) < DH) == (side == 0) for side in range(2))
    for pair in range(width // LANES):
        flipped[pl.ds(pair * LANES, LANES), :] = qkv_out[:, pl.ds(2 * width + pair * LANES, LANES)].T

    def attend(part_index, carry):
        part = pl.ds(pl.multiple_of(part_index * 512, 512), 512)
        related = seg_col[...] == seg_row[:, part]
        for pair in range(width // LANES):
            q = qkv_out[part, pl.ds(pair * LANES, LANES)]
            k = qkv_out[:, pl.ds(width + pair * LANES, LANES)]
            v = flipped[pl.ds(pair * LANES, LANES), :]
            result = jnp.zeros((LANES, 512), F32)
            for side in range(2):
                scores = dot_nt(k, jnp.where(sides[side], q, zero))
                scores = jnp.where(related, scores, -MASK_FILL)
                top = jnp.max(scores, 0, keepdims=True)
                weights = jnp.exp(scores - top)
                summed = jnp.sum(weights, 0, keepdims=True)
                probs = (weights * (1.0 / summed)).astype(BF16)
                result += dot(jnp.where(turned[side], v, zero), probs)
                lse_out[pl.ds(2 * pair + side, 1), part] = top + jnp.log(summed)
            attended_out[part, pl.ds(pair * LANES, LANES)] = result.T.astype(BF16)
        return carry

    lax.fori_loop(0, rows // 512, attend, 0)
    stream.flush(attended_out, lse_out)
    stream.ready(2)

    edge = jnp.zeros((8, width), F32)
    padded[pl.ds(0, 8), :] = edge
    padded[pl.ds(rows + 8, 8), :] = edge
    for part in chunks(rows, 256):
        x2 = x1_out[part, :] + dot(attended_out[part, :], attn_out[...])
        x2_out[part, :] = x2
        hat, _ = normalize(x2)
        uc = (hat * gains(2)).astype(BF16)
        uc_out[part, :] = uc
        gin = dot(uc, conv_in[...])
        gin_out[part, :] = gin
        padded[pl.ds(part.start + 8, 256), :] = gin[:, :width] * sigmoid(gin[:, width:])

    stream.flush(x2_out, uc_out, gin_out)
    sums = jnp.zeros((1, width), F32)
    squares = jnp.zeros((1, width), F32)
    for part in chunks(rows, 64):
        depth = jnp.zeros((64, width), F32)
        for tap, shifted in shifts(padded, part):
            depth += table[pl.ds(6 + tap, 1), :] * shifted * taps[part, pl.ds(tap, 1)]
        depth_out[part, :] = depth
        weighted = jnp.where(seg_col[part, :] < 3, depth, 0.0)
        sums += jnp.sum(weighted, 0, keepdims=True)
        squares += jnp.sum(weighted * depth, 0, keepdims=True)
    moments[pl.ds(0, 1), :] = sums
    moments[pl.ds(1, 1), :] = squares
    moments[pl.ds(2, 6), :] = jnp.zeros((6, width), F32)
    stream.flush(depth_out, moments)


def batch_terms(moments, frame_count):
    mean = moments[pl.ds(0, 1), :] / frame_count[0]
    variance = moments[pl.ds(1, 1), :] / frame_count[0] - mean * mean
    return mean, lax.rsqrt(variance + EPSILON)


def middle_kernel(frame_count, depth, terms, x2, table, conv_out, slot_row, swish_out, x3_out, moments, sent, normed):
    rows, width = depth.shape
    moments[...] = total_of(terms)
    mean, scale = batch_terms(moments, frame_count)
    for part in chunks(rows, 256):
        bn = (depth[part, :] - mean) * scale * table[pl.ds(5, 1), :] + table[pl.ds(21, 1), :]
        swish = (bn * sigmoid(bn)).astype(BF16)
        swish_out[part, :] = swish
        x3 = x2[part, :] + dot(swish, conv_out[...])
        x3_out[part, :] = x3
        hat, _ = normalize(x3)
        normed[part, :] = (hat * table[pl.ds(3, 1), :]).astype(BF16)
    scatter_to(slot_row, normed[...], sent)


def turn_kernel(
    x3, blocks, slot_col, slot_row, gate, table, cotangent, seg_col,
    block_out, dx4_out, gate_grad, gain_out, sent, grads,
):
    rows, width = x3.shape
    gain = table[pl.ds(4, 1), :]
    gain_sum = jnp.zeros((1, width), F32)
    for part in chunks(rows, 256):
        found = gathered(slot_col, blocks, part)
        half = 0.5 * gate[part, :]
        x4 = x3[part, :] + half * found
        hat, inverse = normalize(x4)
        valid = seg_col[part, :] < 3
        block_out[part, :] = jnp.where(valid, hat * gain, 0.0).astype(BF16)
        grad = jnp.where(valid, cotangent[part, :].astype(F32), 0.0)
        gain_sum += jnp.sum(grad * hat, 0, keepdims=True)
        dx4 = norm_backward(grad, gain, hat, inverse)
        dx4_out[part, :] = dx4
        gate_grad[part, :] = 0.5 * jnp.sum(found * dx4, 1, keepdims=True)
        grads[part, :] = (half * dx4).astype(BF16)
    gain_out[...] = gain_sum
    scatter_to(slot_row, grads[...], sent)


def conv_back_kernel(
    frame_count, dx4, blocks, slot_col, x3, table, conv_out, depth, moments,
    dx3_out, dco_out, dh_out, sums,
):
    rows, width = x3.shape
    mean, scale = batch_terms(moments, frame_count)
    total = jnp.zeros((1, width), F32)
    moment = jnp.zeros((1, width), F32)
    shift = jnp.zeros((1, width), F32)
    gain5 = jnp.zeros((1, width), F32)
    gain3 = jnp.zeros((1, width), F32)
    for part in chunks(rows, 256):
        grad = gathered(slot_col, blocks, part)
        hat, inverse = normalize(x3[part, :])
        gain3 += jnp.sum(grad * hat, 0, keepdims=True)
        dx3 = dx4[part, :] + norm_backward(grad, table[pl.ds(3, 1), :], hat, inverse)
        dx3_out[part, :] = dx3
        dco = dx3.astype(BF16)
        dco_out[part, :] = dco
        centred = depth[part, :] - mean
        hat = centred * scale
        bn = hat * table[pl.ds(5, 1), :] + table[pl.ds(21, 1), :]
        dbn = dot_nt(dco, conv_out[...]) * slope(bn, sigmoid(bn))
        shift += jnp.sum(dbn, 0, keepdims=True)
        gain5 += jnp.sum(dbn * hat, 0, keepdims=True)
        dh = dbn * table[pl.ds(5, 1), :]
        dh_out[part, :] = dh
        total += jnp.sum(dh, 0, keepdims=True)
        moment += jnp.sum(dh * centred, 0, keepdims=True)
    for number, row in enumerate((total, moment, shift, gain5, gain3)):
        sums[pl.ds(number, 1), :] = row
    sums[pl.ds(5, 3), :] = jnp.zeros((3, width), F32)


def back_kernel(
    stream, frame_count, dh, depth, moments, sum_terms, dx3, gin, x2, x1, table, conv_in, attn_out, attn_in, qkv, attended, lse,
    cosine, sine, seg_col, seg_row, taps, expert, gate, slot_row,
    dgin_out, dat_out, dproj_out, dx1_out, gate_grad, terms, sent,
    padded, glu, grad_rows, dk, dv, rows_sent, flipped,
):
    rows, width = dh.shape
    mean, scale = batch_terms(moments, frame_count)
    sums = total_of(sum_terms)
    total, moment = sums[0:1], sums[1:2]
    var_grad = -0.5 * moment * scale * scale * scale
    mean_grad = -scale * total - 2.0 * mean * var_grad
    edge = jnp.zeros((8, width), F32)
    for ref in (padded, glu):
        ref[pl.ds(0, 8), :] = edge
        ref[pl.ds(rows + 8, 8), :] = edge
    stream.ready(0)
    for part in chunks(rows, 64):
        held = depth[part, :]
        grad = (mean_grad + 2.0 * held * var_grad) * (1.0 / frame_count[0])
        padded[pl.ds(part.start + 8, 64), :] = dh[part, :] * scale + jnp.where(seg_col[part, :] < 3, grad, 0.0)
    stream.ready(1)
    for part in chunks(rows, 64):
        glu[pl.ds(part.start + 8, 64), :] = gin[part, :width] * sigmoid(gin[part, width:])
    kernel_sums = [jnp.zeros((8, width), F32) for _ in range(15)]
    gain2 = jnp.zeros((1, width), F32)
    for part in chunks(rows, 64):
        dglu = jnp.zeros((64, width), F32)
        own = padded[pl.ds(part.start + 8, 64), :]
        for (tap, grad), (_, value) in zip(shifts(padded, part), shifts(glu, part)):
            mask = taps[part, pl.ds(tap, 1)]
            dglu += table[pl.ds(20 - tap, 1), :] * grad * mask
            kernel_sums[tap] += folded(own * value * mask)
        logistic = sigmoid(gin[part, width:])
        dgin_out[part, :width] = (dglu * logistic).astype(BF16)
        dgin_out[part, width:] = (dglu * gin[part, :width] * logistic * (1.0 - logistic)).astype(BF16)
    for tap in range(15):
        terms[pl.ds(6 + tap, 1), :] = jnp.sum(kernel_sums[tap], 0, keepdims=True)
    stream.flush(dgin_out)
    stream.ready(2)
    for part in chunks(rows, 256):
        grad = dot_nt(dgin_out[part, :], conv_in[...])
        hat, inverse = normalize(x2[part, :])
        gain2 += jnp.sum(grad * hat, 0, keepdims=True)
        dx2 = dx3[part, :] + norm_backward(grad, table[pl.ds(2, 1), :], hat, inverse)
        dx1_out[part, :] = dx2
        dat = dx2.astype(BF16)
        dat_out[part, :] = dat
        grad_rows[part, :] = dot_nt(dat, attn_out[...]).astype(BF16)
    terms[pl.ds(2, 1), :] = gain2

    stream.flush(dat_out)
    stream.ready(3)
    zero = jnp.zeros((), BF16)
    sides = tuple((iota((1, LANES), 1) < DH) == (side == 0) for side in range(2))
    turned = tuple((iota((LANES, 1), 0) < DH) == (side == 0) for side in range(2))
    for pair in range(width // LANES):
        flipped[pl.ds(pair * LANES, LANES), :] = qkv[:, pl.ds(width + pair * LANES, LANES)].T

    for pair in range(width // LANES):
        own = pl.ds(pair * LANES, LANES)
        q, da = qkv[:, own], grad_rows[:, own]
        products = (attended[:, own].astype(F32) * da.astype(F32)).T
        dq = jnp.zeros((LANES, rows), F32)
        for start in range(0, rows, 512):
            keys = pl.ds(start, 512)
            related = seg_col[keys, :] == seg_row[...]
            k = qkv[keys, pl.ds(width + pair * LANES, LANES)]
            v = qkv[keys, pl.ds(2 * width + pair * LANES, LANES)]
            dk_sum = jnp.zeros((512, LANES), F32)
            dv_sum = jnp.zeros((512, LANES), F32)
            for side in range(2):
                inner = jnp.sum(products[side * DH : (side + 1) * DH], 0, keepdims=True)
                q_side = jnp.where(sides[side], q, zero)
                da_side = jnp.where(sides[side], da, zero)
                scores = dot_nt(k, q_side) - lse[pl.ds(2 * pair + side, 1), :]
                probs = jnp.exp(jnp.where(related, scores, -MASK_FILL))
                dscores = (probs * (dot_nt(v, da_side) - inner)).astype(BF16)
                dq += dot(jnp.where(turned[side], flipped[own, keys], zero), dscores)
                dk_sum += dot(dscores, q_side)
                dv_sum += dot(probs.astype(BF16), da_side)
            dk[keys, own] = dk_sum
            dv[keys, own] = dv_sum
        dq = dq.T * DH**-0.5
        dproj_out[:, own] = (dq * cosine[...] - partner(dq) * sine[...]).astype(BF16)

    stream.ready(4)
    gain1 = jnp.zeros((1, width), F32)
    for part in chunks(rows, 256):
        for pair in range(width // LANES):
            own = pl.ds(pair * LANES, LANES)
            held = dk[part, own]
            dproj_out[part, pl.ds(width + pair * LANES, LANES)] = (
                held * cosine[part, :] - partner(held) * sine[part, :]
            ).astype(BF16)
            dproj_out[part, pl.ds(2 * width + pair * LANES, LANES)] = dv[part, own].astype(BF16)
        grad = dot_nt(dproj_out[part, :], attn_in[...])
        hat, inverse = normalize(x1[part, :])
        gain1 += jnp.sum(grad * hat, 0, keepdims=True)
        dx1 = dx1_out[part, :] + norm_backward(grad, table[pl.ds(1, 1), :], hat, inverse)
        dx1_out[part, :] = dx1
        gate_grad[part, :] = 0.5 * jnp.sum(expert[part, :].astype(F32) * dx1, 1, keepdims=True)
        rows_sent[part, :] = (0.5 * gate[part, :] * dx1).astype(BF16)
    terms[pl.ds(1, 1), :] = gain1
    stream.flush(dproj_out, dx1_out, gate_grad, terms)
    scatter_to(slot_row, rows_sent[...], sent)
    stream.flush(*sent)


def final_kernel(frames, blocks, slot_col, table, dx1, dz, embed_weight, _, out):
    for part in chunks(frames.shape[0], 128):
        grad = gathered(slot_col, blocks, part)
        hat, inverse = normalize(frames[part, :].astype(F32))
        dx0 = dx1[part, :] + norm_backward(grad, table[pl.ds(0, 1), :], hat, inverse)
        out[part, :] = dx0 + dot_nt(dz[part, :], embed_weight[...])


def after(value, *others):
    return lax.optimization_barrier((value,) + others)[0]


def shards(
    frames,
    lengths,
    choice_first,
    choice_second,
    embed_weight,
    routers,
    norm_gains,
    attn_in,
    attn_out,
    conv_in,
    conv_kernel,
    bn_shift,
    conv_out,
    expert_in,
    expert_out,
    cotangent,
):
    rows, width = frames.shape
    layers, slice_width, experts = routers.shape
    taps = conv_kernel.shape[0]
    gains = norm_gains.shape[0]
    peers = lax.axis_size("expert")
    dp_count = lax.axis_size("dp")
    dp_bits = bit_count(("dp",))
    capacity = 2 * rows // experts
    hidden = expert_in.shape[3]
    device = lax.axis_index(AXES)
    block = shaped((capacity, width), BF16)
    wide = shaped((rows, width), F32)
    low = shaped((rows, width), BF16)
    column = shaped((rows, 1), F32)

    dp_index = lax.axis_index("dp")[None]

    def shard_of(layer):
        first = expert_in[layer, 0]
        tiles = [first[:, start : start + width] for start in range(0, hidden, width)]
        return jnp.concatenate([expert_out[layer, 0]] + tiles, 0)

    first_weights = lax.all_gather(shard_of(0), "dp", axis=0)
    sent, slot_col1, slot_row1, slot_col2, slot_row2 = call(
        start_kernel,
        ([block] * peers, shaped((rows, 1), I32), shaped((1, rows), I32), shaped((rows, 1), I32), shaped((1, rows), I32)),
        lax.axis_index("expert")[None],
        frames,
        choice_first,
        choice_first.reshape(1, rows),
        choice_second,
        choice_second.reshape(1, rows),
        specs=[SMEM] + [None] * 5,
    )
    first_blocks = swap_blocks(sent)

    small_width = gains + taps + 1 + layers * experts
    small = jnp.concatenate(
        [
            norm_gains.T,
            conv_kernel.T,
            bn_shift[:, None],
            jnp.moveaxis(routers, 1, 0).reshape(slice_width, -1),
            jnp.zeros((slice_width, -small_width % LANES), BF16),
        ],
        1,
    )
    small = after(small, sent[0])
    small_all = gather_everywhere(small).reshape(width, LANES).astype(F32)
    table = small_all[:, : gains + taps + 3].T
    router_table = jnp.pad(
        small_all[:, gains + taps + 1 : small_width], ((0, 0), (0, LANES - layers * experts))
    )
    dense = jnp.concatenate([attn_in, attn_out, conv_in, conv_out], 1)
    dense = lax.all_to_all(
        jnp.broadcast_to(dense[None], (peers,) + dense.shape), "expert", split_axis=0, concat_axis=0, tiled=True
    )
    dense = lax.all_gather(
        dense.reshape(peers * slice_width, 7 * width), "dp", axis=0, tiled=True
    )
    second_weights = lax.all_gather(shard_of(1), "dp", axis=0)

    own_lengths = lax.dynamic_index_in_dim(lengths, device, 0, keepdims=False)
    frame_count = jnp.sum(lengths[:, :-1]).astype(F32)[None]
    (embed_pre, embedded, probs, gate1, gate2, seg_col, seg_row, tap_masks, offsets) = call(
        functools.partial(embed_kernel, experts),
        [
            wide,
            wide,
            shaped((rows, LANES), F32),
            column,
            column,
            shaped((rows, 1), I32),
            shaped((1, rows), I32),
            shaped((rows, LANES), F32),
            column,
        ],
        jnp.cumsum(own_lengths, dtype=I32)[:-1],
        frames,
        embed_weight,
        router_table,
        choice_first,
        choice_second,
        specs=[SMEM] + [None] * 5,
    )
    half = DH // 2
    frequency = 10000.0 ** (-jnp.arange(half, dtype=F32) / half)
    angles = offsets * jnp.tile(frequency, LANES // half)[None, :]
    sign = jnp.asarray(np.where(np.arange(LANES) % DH < half, -1.0, 1.0), F32)
    cosine, sine = jnp.cos(angles), jnp.sin(angles) * sign[None, :]

    def gain(number):
        return table[number : number + 1]

    first_results = swap_blocks(
        [expert_forward(block, gain(0), first_weights, hidden, True) for block in first_blocks]
    )

    def dense_spec(columns, start):
        return pl.BlockSpec((width, columns), lambda i: (0, start // columns))

    attn_in_spec = dense_spec(3 * width, 0)
    attn_out_spec = dense_spec(width, 3 * width)
    conv_in_spec = dense_spec(2 * width, 4 * width)
    conv_out_spec = dense_spec(width, 6 * width)
    sums_shape = shaped((8, width), F32)
    padded = pltpu.VMEM((rows + 16, width), F32)

    first_expert, x1, x2, ua, qkv, lse, attended, uc, gin, depth, moments = call(
        front_kernel,
        [
            low,
            wide,
            wide,
            low,
            shaped((rows, 3 * width), BF16),
            shaped((8, rows), F32),
            low,
            low,
            shaped((rows, 2 * width), F32),
            wide,
            sums_shape,
        ],
        frames,
        first_results,
        slot_col1,
        gate1,
        table,
        Columns(dense, 0, 3 * width),
        Columns(dense, 3 * width, width),
        Columns(dense, 4 * width, 2 * width),
        cosine,
        sine,
        seg_col,
        seg_row,
        tap_masks,
        stages=[0, 0, None, None, None, 1, 2, 2, 1, 1, None, None, 2],
        cost=20,
        scratch=[padded, pltpu.VMEM((width, rows), BF16)],
    )
    moment_terms = terms_everywhere(moments)
    swish, x3, moments, sent = call(
        middle_kernel,
        (low, wide, sums_shape, [block] * peers),
        frame_count,
        depth,
        moment_terms,
        x2,
        table,
        dense,
        slot_row2,
        specs=[SMEM] + [None] * 4 + [conv_out_spec, None],
        scratch=[pltpu.VMEM((rows, width), BF16)],
    )

    second_blocks = swap_blocks(sent)
    second_results = swap_blocks(
        [expert_forward(block, gain(3), second_weights, hidden, False) for block in second_blocks]
    )
    block_out, dx4, gate_grad2, gain4, sent = call(
        turn_kernel,
        (low, wide, column, shaped((1, width), F32), [block] * peers),
        x3,
        second_results,
        slot_col2,
        slot_row2,
        gate2,
        table,
        cotangent,
        seg_col,
        scratch=[pltpu.VMEM((rows, width), BF16)],
    )
    second_grads = swap_blocks(sent)
    backs = [
        expert_backward(block, grad, gain(3), second_weights, hidden, False)
        for block, grad in zip(second_blocks, second_grads)
    ]
    back, hid, pre_grads, inputs, _ = zip(*backs)
    second_back = swap_blocks(back)
    (second_grad,) = weight_grads(
        dp_index, inputs, second_grads, hid, pre_grads, dp_count, False
    )
    second_back[1] = after(second_back[1], second_grad)
    second_own = lax.psum_scatter(second_grad, "dp", scatter_dimension=0, tiled=True)[0]

    dx3, dco, dh, sums = call(
        conv_back_kernel,
        [wide, low, wide, sums_shape],
        frame_count,
        dx4,
        second_back,
        slot_col2,
        x3,
        table,
        dense,
        depth,
        moments,
        specs=[SMEM] + [None] * 5 + [conv_out_spec] + [None] * 2,
    )
    all_sums = terms_everywhere(sums)
    dgin, dat, dproj, dx1, gate_grad1, terms, sent = call(
        back_kernel,
        (
            shaped((rows, 2 * width), BF16),
            low,
            shaped((rows, 3 * width), BF16),
            wide,
            column,
            shaped((24, width), F32),
            [block] * peers,
        ),
        frame_count,
        dh,
        depth,
        moments,
        all_sums,
        dx3,
        gin,
        x2,
        x1,
        table,
        Columns(dense, 4 * width, 2 * width),
        Columns(dense, 3 * width, width),
        Columns(dense, 0, 3 * width),
        qkv,
        attended,
        lse,
        cosine,
        sine,
        seg_col,
        seg_row,
        tap_masks,
        first_expert,
        gate1,
        slot_row1,
        specs=[SMEM] + [None] * 23,
        stages=[None, 0, 0, None, None, 2, 1, 2, 4, None, 2, 2, 4, 3, 3, 3, 3, 3, None, None, 1, 4, None, None],
        cost=30,
        scratch=[padded, padded, pltpu.VMEM((rows, width), BF16), pltpu.VMEM((rows, width), F32), pltpu.VMEM((rows, width), F32), pltpu.VMEM((rows, width), BF16), pltpu.VMEM((width, rows), BF16)],
    )
    first_grads = swap_blocks(sent)

    def dp_exchange(values, mask):
        return lax.ppermute(values, "dp", [(i, i ^ mask) for i in range(dp_count)])

    dense_part = shaped((dp_count // 2, 8 * width // dp_count, width), BF16)
    kept, moved, dz, router_terms = call(
        functools.partial(dense_grad_kernel, experts),
        (dense_part, dense_part, low, shaped((LANES, width), F32)),
        ua,
        dproj,
        attended,
        dat,
        uc,
        dgin,
        swish,
        dco,
        gate_grad1,
        gate1,
        choice_first,
        gate_grad2,
        gate2,
        choice_second,
        dp_index,
        probs,
        router_table,
        embed_pre,
        embedded,
        frames,
        specs=[None] * 14 + [SMEM] + [None] * 5,
        stages=[0, 0, 1, 1, 2, 2, 2, 2] + [None] * 8 + [None, 2, 2, 2],
        cost=1,
        scratch=[pltpu.VMEM((rows, LANES), F32), pltpu.VMEM((width, width), BF16), pltpu.VMEM((width, rows), BF16)],
    )
    pairs = call(
        pair_kernel,
        [shaped(kept.shape[1:], BF16)] * (dp_count // 2),
        kept,
        dp_exchange(moved, 1),
        vmem=16,
        cost=10,
    )
    dense_own = call(
        sum_kernel,
        shaped(pairs[0].shape, BF16),
        [dp_exchange(pair, mask) if mask else pair for pair, mask in zip(pairs, chip_masks())],
        vmem=8,
        cost=60,
    )
    dense_own = dense_own.reshape(8, peers, slice_width, width).transpose(1, 2, 0, 3)
    backs = [
        expert_backward(block, grad, gain(0), first_weights, hidden, True)
        for block, grad in zip(first_blocks, first_grads)
    ]
    back, hid, pre_grads, inputs, gain0 = zip(*backs)
    gain0 = sum(gain0)
    first_back = swap_blocks(back)
    kept, moved = weight_grads(dp_index, inputs, first_grads, hid, pre_grads, dp_count, True)
    moved = after(moved, *first_back[1:])

    pairs = call(
        pair_kernel,
        [shaped(kept.shape[1:], BF16)] * (dp_count // 2),
        kept,
        dp_exchange(moved, 1),
        vmem=16,
        cost=20,
    )
    dense_own = after(dense_own, *pairs)
    dense_own = lax.all_to_all(
        dense_own.reshape(peers, slice_width, 8 * width), "expert", split_axis=0, concat_axis=0, tiled=True
    )
    first_parts = [
        dp_exchange(pair, mask) if mask else pair for pair, mask in zip(pairs, chip_masks())
    ]
    owned = [shaped((slice_width, count * width), F32) for count in (3, 1, 2, 1)]
    *dense_own, embed_own = call(
        dense_out_kernel,
        (*owned, shaped((slice_width, width), BF16)),
        dense_own,
        vmem=8,
        cost=10,
    )
    in_grad, out_grad = call(
        experts_out_kernel,
        (shaped((layers, 1, width // dp_count, hidden), F32), shaped((layers, 1, hidden // dp_count, width), F32)),
        first_parts,
        second_own,
        vmem=24,
        cost=10,
    )

    small_terms = jnp.concatenate(
        [
            gain0,
            terms[1:3],
            sums[4:5],
            gain4,
            sums[3:4],
            terms[6 : 6 + taps],
            sums[2:3],
            router_terms[: layers * experts],
        ],
        0,
    )
    small_terms = small_terms.T
    high = lax.reduce_precision(small_terms, 8, 7)
    split = jnp.concatenate([high, small_terms - high], 1).astype(BF16)
    split = jnp.pad(split, ((0, 0), (0, LANES - 2 * small_width))).reshape(-1, slice_width, LANES)
    mixed = jnp.concatenate([jnp.broadcast_to(embed_own[None], (split.shape[0],) + embed_own.shape), split], 2)
    mixed = lax.all_to_all(mixed, AXES, split_axis=0, concat_axis=0, tiled=True)
    embed_total = mixed[:, :, :width].reshape(width, width).astype(F32)
    small_sums = jnp.sum(mixed[:, :, width:].astype(F32), 0)
    small_sums = (small_sums[:, :small_width] + small_sums[:, small_width : 2 * small_width]).T

    frames_grad = call(
        final_kernel,
        wide,
        frames,
        first_back,
        slot_col1,
        table,
        dx1,
        dz,
        embed_weight,
        second_own,
        specs=[None] * 7 + [ANY],
        cost=40,
    )
    return (
        block_out,
        frames_grad,
        embed_total,
        jnp.moveaxis(
            small_sums[gains + taps + 1 : small_width].reshape(layers, experts, slice_width), 1, 2
        ),
        small_sums[:gains],
        *dense_own[:3],
        small_sums[gains : gains + taps],
        small_sums[gains + taps],
        dense_own[3],
        in_grad,
        out_grad,
    )


def solution(mesh):
    in_specs = (
        P(("dp", "expert"), None),
        P(),
        P(("dp", "expert"), None),
        P(("dp", "expert"), None),
        P(),
        P(None, ("dp", "expert"), None),
        P(None, ("dp", "expert")),
        P(("dp", "expert"), None),
        P(("dp", "expert"), None),
        P(("dp", "expert"), None),
        P(None, ("dp", "expert")),
        P(("dp", "expert")),
        P(("dp", "expert"), None),
        P(None, "expert", "dp", None),
        P(None, "expert", "dp", None),
        P(("dp", "expert"), None),
    )
    out_specs = (
        P(("dp", "expert"), None),
        P(("dp", "expert"), None),
        P(),
        P(None, ("dp", "expert"), None),
        P(None, ("dp", "expert")),
        P(("dp", "expert"), None),
        P(("dp", "expert"), None),
        P(("dp", "expert"), None),
        P(None, ("dp", "expert")),
        P(("dp", "expert")),
        P(("dp", "expert"), None),
        P(None, "expert", "dp", None),
        P(None, "expert", "dp", None),
    )
    return jax.shard_map(shards, mesh=mesh, in_specs=in_specs, out_specs=out_specs, check_vma=False)
```

```python
import functools

import jax
import jax.numpy as jnp
import numpy as np
from jax import lax
from jax.experimental import pallas as pl
from jax.experimental.pallas import tpu as pltpu
from jax.sharding import PartitionSpec as P

H = 8
DH = 64
LANES = 128

EPSILON = 1e-05
MASK_FILL = 1000000000.0
HIGHEST = lax.Precision.HIGHEST
AXES = ("dp", "expert")
BF16 = jnp.bfloat16
F32 = jnp.float32
I32 = jnp.int32
MIB = 1 << 20


def bit_count(axes):
    total = 1
    for name in axes:
        total *= lax.axis_size(name)
    return total.bit_length() - 1


def exchange(values, axes, mask):
    total = 1 << bit_count(axes)
    return lax.ppermute(values, axes, [(i, i ^ mask) for i in range(total)])


def device_groups():
    z_bits = bit_count(("expert",))
    dp_bits = bit_count(("dp",))
    chips = list(range(z_bits + 1, z_bits + dp_bits))
    rests = [chips, list(range(z_bits))]
    return [[z_bits]] + [bits[i : i + 2] for bits in rests for i in range(0, len(bits), 2)]


def masks_of(bits):
    if len(bits) == 1:
        return [1 << bits[0]]
    low, high = 1 << bits[0], 1 << bits[1]
    return [low, high, low | high]


def terms_everywhere(values):
    groups = device_groups()
    for bits in groups[:-1]:
        arrived = [exchange(values, AXES, mask) for mask in masks_of(bits)]
        if len(arrived) == 1:
            values = values + arrived[0]
        else:
            values = (values + arrived[0]) + (arrived[1] + arrived[2])
    return [values] + [exchange(values, AXES, mask) for mask in masks_of(groups[-1])]


def total_of(terms):
    if len(terms) == 2:
        return terms[0][...] + terms[1][...]
    return (terms[0][...] + terms[1][...]) + (terms[2][...] + terms[3][...])


def gather_everywhere(values):
    total = 1 << bit_count(AXES)
    sent = jnp.broadcast_to(values[None], (total,) + values.shape)
    return lax.all_to_all(sent, AXES, split_axis=0, concat_axis=0, tiled=True)


def sum_to_owners(values, axes):
    arrived = lax.all_to_all(values, axes, split_axis=0, concat_axis=0, tiled=True)
    return jnp.sum(arrived.astype(F32), 0)


def swap_blocks(blocks):
    total = lax.axis_size("expert")
    moved = [blocks[0]]
    for k in range(1, total):
        moved.append(lax.ppermute(blocks[k], "expert", [(i, i ^ k) for i in range(total)]))
    return moved


def chip_masks():
    return [core << 1 for core in range(lax.axis_size("dp") // 2)]


class Columns:
    def __init__(self, array, start, count):
        self.array, self.start, self.count = array, start, count


class Stream:
    def __init__(self, arrivals, results, spare):
        self.arrivals, self.results = arrivals, results
        self.spare, self.spared = spare, 0
        self.waited, self.sent = set(), []
        self.begin(0)
        self.begin(1)

    def begin(self, stage):
        for copy in self.arrivals.get(stage, ()):
            copy.start()

    def ready(self, stage):
        for copy in self.arrivals.get(stage, ()):
            copy.wait()
        self.waited.add(stage)
        self.begin(stage + 2)

    def flush(self, *refs):
        for ref in refs:
            held, target, sem = self.results[id(ref)]
            self.send(held, target, sem)

    def flush_rows(self, ref, start, size):
        held, target, _ = self.results[id(ref)]
        rows = pl.ds(start, size)
        self.send(held.at[:, rows], target.at[:, rows], self.spare.at[self.spared])
        self.spared += 1

    def send(self, held, target, sem):
        copy = pltpu.make_async_copy(held, target, sem)
        copy.start()
        self.sent.append(copy)

    def finish(self):
        for copy in self.sent:
            copy.wait()


def call(body, outs, *args, specs=None, out_specs=None, scratch=(), stages=None, vmem=60, cost=5, **kw):
    vmem_spec = pl.BlockSpec(memory_space=pltpu.VMEM)
    any_spec = pl.BlockSpec(memory_space=pl.ANY)
    if specs is None:
        specs = [None] * len(args)
    columns = [arg if isinstance(arg, Columns) else None for arg in args]
    args = [arg.array if isinstance(arg, Columns) else arg for arg in args]
    grid = kw.pop("grid", (1,))
    scratch = list(scratch)
    if stages is None:
        specs = [
            jax.tree.map(lambda _: vmem_spec, arg) if spec is None else spec
            for spec, arg in zip(specs, args)
        ]
        if out_specs is None:
            out_specs = jax.tree.map(lambda _: vmem_spec, outs)
        wrapped = body
    else:
        specs = [
            spec if spec is not None else jax.tree.map(lambda _: vmem_spec if stage is None else any_spec, arg)
            for spec, arg, stage in zip(specs, args, stages)
        ]
        out_specs = jax.tree.map(lambda _: any_spec, outs)
        buffers = []
        for arg, part, stage in zip(args, columns, stages):
            if stage is not None:
                for leaf in jax.tree.leaves(arg):
                    shape = leaf.shape if part is None else (leaf.shape[0], part.count)
                    buffers.append(pltpu.VMEM(shape, leaf.dtype))
        out_leaves, out_tree = jax.tree.flatten(outs)
        buffers += [pltpu.VMEM(leaf.shape, leaf.dtype) for leaf in out_leaves]
        own_scratch, total = len(scratch), len(buffers)
        scratch = scratch + buffers + [pltpu.SemaphoreType.DMA((4,)), pltpu.SemaphoreType.DMA((total,))]

        def wrapped(*refs):
            refs = list(refs)
            ins, out_refs, rest = refs[: len(args)], refs[len(args) : len(args) + out_count], refs[len(args) + out_count :]
            own, held, spare, sems = rest[:own_scratch], rest[own_scratch:-2], rest[-2], rest[-1]
            arrivals, given, used = {}, [], 0
            for ref, part, stage in zip(ins, columns, stages):
                if stage is None:
                    given.append(ref)
                    continue
                leaves, tree = jax.tree.flatten(ref)
                landed = []
                for leaf in leaves:
                    source = leaf if part is None else leaf.at[:, pl.ds(part.start, part.count)]
                    arrivals.setdefault(stage, []).append(
                        pltpu.make_async_copy(source, held[used], sems.at[used])
                    )
                    landed.append(held[used])
                    used += 1
                given.append(jax.tree.unflatten(tree, landed))
            results, places = {}, []
            for ref in jax.tree.leaves(out_refs):
                results[id(held[used])] = (held[used], ref, sems.at[used])
                places.append(held[used])
                used += 1
            stream = Stream(arrivals, results, spare)
            given_outs = jax.tree.unflatten(out_tree, places)
            given_outs = list(given_outs) if isinstance(given_outs, (tuple, list)) else [given_outs]
            body(stream, *given, *given_outs, *own)
            stream.finish()

        out_count = len(outs) if isinstance(outs, (tuple, list)) else 1
    return pl.pallas_call(
        wrapped,
        out_shape=outs,
        in_specs=specs,
        out_specs=out_specs,
        scratch_shapes=scratch,
        grid=grid,
        compiler_params=pltpu.CompilerParams(vmem_limit_bytes=vmem * MIB),
        cost_estimate=pl.CostEstimate(flops=cost * 1153 * 10**6, bytes_accessed=0, transcendentals=0),
        **kw,
    )(*args)


def shaped(shape, dtype):
    return jax.ShapeDtypeStruct(shape, dtype)


SMEM = pl.BlockSpec(memory_space=pltpu.SMEM)
ANY = pl.BlockSpec(memory_space=pl.ANY)


def dot(left, right):
    return lax.dot_general(left, right, (((1,), (0,)), ((), ())), preferred_element_type=F32)


def dot_nt(left, right):
    return lax.dot_general(left, right, (((1,), (1,)), ((), ())), preferred_element_type=F32)


def dot_tn(left, right):
    return lax.dot_general(left, right, (((0,), (0,)), ((), ())), preferred_element_type=F32)


def iota(shape, dim):
    return lax.broadcasted_iota(I32, shape, dim)


def normalize(rows):
    centred = rows - jnp.mean(rows, -1, keepdims=True)
    inverse = lax.rsqrt(jnp.mean(centred * centred, -1, keepdims=True) + EPSILON)
    return centred * inverse, inverse


def norm_backward(grad, gain, hat, inverse):
    scaled = grad * gain
    return inverse * (
        scaled
        - jnp.mean(scaled, -1, keepdims=True)
        - hat * jnp.mean(scaled * hat, -1, keepdims=True)
    )


def sigmoid(values):
    return 1.0 / (1.0 + jnp.exp(-values))


def slope(values, logistic):
    return logistic * (1.0 + values * (1.0 - logistic))


def chunks(total, size):
    return [pl.ds(start, size) for start in range(0, total, size)]


def gathered(slot_col, blocks, rows):
    slot = slot_col[rows, :]
    total = None
    for k, block in enumerate(blocks):
        capacity = block.shape[0]
        pick = (slot == iota((slot.shape[0], capacity), 1) + k * capacity).astype(F32).astype(BF16)
        part = dot(pick, block[...])
        total = part if total is None else total + part
    return total


def scatter_to(slot_row, values, outs):
    for k, out in enumerate(outs):
        capacity = out.shape[0]
        pick = (slot_row[...] == iota((capacity, slot_row.shape[1]), 0) + k * capacity)
        out[...] = dot(pick.astype(F32).astype(BF16), values).astype(BF16)


def start_kernel(own, frames, col1, row1, col2, row2, sent, slot_col1, slot_row1, slot_col2, slot_row2):
    rows = frames.shape[0]
    capacity = sent[0].shape[0]
    below = (iota((rows, rows), 0) > iota((rows, rows), 1)).astype(F32).astype(BF16)
    above = (iota((rows, rows), 0) < iota((rows, rows), 1)).astype(F32).astype(BF16)
    for col, row, out_col, out_row in (
        (col1, row1, slot_col1, slot_row1),
        (col2, row2, slot_col2, slot_row2),
    ):
        hot = (col[...] == iota((rows, LANES), 1)).astype(F32)
        rank = jnp.sum(dot(below, hot.astype(BF16)) * hot, 1, keepdims=True)
        out_col[...] = (col[...] ^ own[0]) * capacity + rank.astype(I32)
        hot = (row[...] == iota((16, rows), 0)).astype(F32)
        rank = jnp.sum(dot(hot.astype(BF16), above) * hot, 0, keepdims=True)
        out_row[...] = (row[...] ^ own[0]) * capacity + rank.astype(I32)
    scatter_to(slot_row1, frames[...], sent)


def expert_specs(weights, hidden, tile):
    count, rows, width = weights.shape
    half = rows // 2
    in_rows = width // count
    rows = in_rows * (tile // width)
    first = pl.BlockSpec((count, rows, width), lambda j: (0, half // rows + j, 0))
    second = pl.BlockSpec((tile // half, half, width), lambda j: (j, 0, 0))
    return first, second


def tiles_of(w_in, w_out):
    count, rows, width = w_in.shape
    owners, half, _ = w_out.shape
    tiles = owners * half // width
    in_rows, per_tile = rows // tiles, owners // tiles
    for tile in range(tiles):
        first = w_in[:, tile * in_rows : (tile + 1) * in_rows, :].reshape(count * in_rows, width)
        second = w_out[tile * per_tile : (tile + 1) * per_tile].reshape(width, width)
        yield pl.ds(tile * width, width), first, second


def expert_forward_kernel(with_norm, block, gain, w_in, w_out, out, total, inputs):
    step = pl.program_id(0)

    @pl.when(step == 0)
    def _():
        if with_norm:
            hat, _ = normalize(block[...].astype(F32))
            inputs[...] = (hat * gain[...]).astype(BF16)
        else:
            inputs[...] = block[...]
        total[...] = jnp.zeros_like(total)

    for _, first, second in tiles_of(w_in, w_out):
        pre = dot(inputs[...], first)
        hidden = (pre * sigmoid(pre)).astype(BF16)
        total[...] += dot(hidden, second)

    @pl.when(step == pl.num_programs(0) - 1)
    def _():
        out[...] = total[...].astype(BF16)


def expert_forward(block, gain, weights, hidden, with_norm, tile=1024):
    capacity, width = block.shape
    first, second = expert_specs(weights, hidden, tile)
    whole = pl.BlockSpec((capacity, width), lambda j: (0, 0))
    return call(
        functools.partial(expert_forward_kernel, with_norm),
        shaped((capacity, width), BF16),
        block,
        gain,
        weights,
        weights,
        specs=[whole, pl.BlockSpec((1, width), lambda j: (0, 0)), first, second],
        out_specs=whole,
        scratch=[pltpu.VMEM((capacity, width), F32), pltpu.VMEM((capacity, width), BF16)],
        grid=(hidden // tile,),
        vmem=16,
        cost=20,
    )


def expert_backward_kernel(
    with_norm, block, grad, gain, w_in, w_out, out, hidden_out, pre_grad_out, input_out, gain_out, total, hats
):
    step = pl.program_id(0)

    @pl.when(step == 0)
    def _():
        if with_norm:
            hat, _ = normalize(block[...].astype(F32))
            hats[...] = hat
            input_out[...] = (hat * gain[...]).astype(BF16)
        else:
            input_out[...] = block[...]
        total[...] = jnp.zeros_like(total)

    for lanes, first, second in tiles_of(w_in, w_out):
        pre = dot(input_out[...], first)
        logistic = sigmoid(pre)
        hidden_out[:, lanes] = (pre * logistic).astype(BF16)
        hidden_grad = dot_nt(grad[...], second)
        pre_grad = (hidden_grad * slope(pre, logistic)).astype(BF16)
        pre_grad_out[:, lanes] = pre_grad
        total[...] += dot_nt(pre_grad, first)

    @pl.when(step == pl.num_programs(0) - 1)
    def _():
        back = total[...].astype(BF16)
        out[...] = back
        if with_norm:
            gain_out[...] = jnp.sum(back.astype(F32) * hats[...], 0, keepdims=True)
        else:
            gain_out[...] = jnp.zeros_like(gain_out)


def expert_backward(block, grad, gain, weights, hidden, with_norm, tile=1024):
    capacity, width = block.shape
    first, second = expert_specs(weights, hidden, tile)
    whole = pl.BlockSpec((capacity, width), lambda j: (0, 0))
    tiled = pl.BlockSpec((capacity, tile), lambda j: (0, j))
    one = pl.BlockSpec((1, width), lambda j: (0, 0))
    return call(
        functools.partial(expert_backward_kernel, with_norm),
        (
            shaped((capacity, width), BF16),
            shaped((capacity, hidden), BF16),
            shaped((capacity, hidden), BF16),
            shaped((capacity, width), BF16),
            shaped((1, width), F32),
        ),
        block,
        grad,
        gain,
        weights,
        weights,
        specs=[whole, whole, one, first, second],
        out_specs=(whole, tiled, tiled, whole, one),
        scratch=[pltpu.VMEM((capacity, width), F32), pltpu.VMEM((capacity, width), F32)],
        grid=(hidden // tile,),
        vmem=24,
        cost=20,
    )


def weight_grad_kernel(relative, dp_index, inputs, grads, hidden, pre_grads, *refs):
    outs, (first, second) = refs[:-2], refs[-2:]
    step = pl.program_id(0)
    first_sum = second_sum = None
    for block, grad, hid, pre_grad in zip(inputs, grads, hidden, pre_grads):
        part = dot_tn(block[...], pre_grad[...])
        first_sum = part if first_sum is None else first_sum + part
        part = dot_tn(hid[...], grad[...])
        second_sum = part if second_sum is None else second_sum + part
    count = sum(out.shape[0] for out in outs)
    half = outs[0].shape[1] // 2
    in_rows = first_sum.shape[0] // count
    tile = second_sum.shape[0]
    owners = tile // half
    place = pl.ds(pl.multiple_of(half + step * in_rows, in_rows), in_rows)
    if not relative:
        for device in range(count):
            outs[0][device, place, :] = first_sum[device * in_rows : (device + 1) * in_rows].astype(BF16)
        for number in range(owners):
            outs[0][step * owners + number, pl.ds(0, half), :] = second_sum[
                number * half : (number + 1) * half
            ].astype(BF16)
    else:
        first[...] = first_sum.astype(BF16)
        for number in range(count):
            source = pl.multiple_of((dp_index[0] ^ number) * in_rows, in_rows)
            outs[number % 2][number // 2, place, :] = first[pl.ds(source, in_rows), :]
        second[...] = second_sum.astype(BF16)
        for number in range(owners):
            owner = (step * owners + number) ^ dp_index[0]

            @pl.when(owner % 2 == 0)
            def _():
                outs[0][owner // 2, pl.ds(0, half), :] = second[pl.ds(number * half, half), :]

            @pl.when(owner % 2 == 1)
            def _():
                outs[1][owner // 2, pl.ds(0, half), :] = second[pl.ds(number * half, half), :]


def weight_grads(dp_index, inputs, grads, hidden, pre_grads, count, relative, tile=512):
    capacity, width = inputs[0].shape
    units = hidden[0].shape[1]
    whole = pl.BlockSpec((capacity, width), lambda j: (0, 0))
    tiled = pl.BlockSpec((capacity, tile), lambda j: (0, j))
    rows = 2 * units // count
    if relative:
        outs = (shaped((count // 2, rows, width), BF16),) * 2
    else:
        outs = (shaped((count, rows, width), BF16),)
    peers = len(inputs)
    return call(
        functools.partial(weight_grad_kernel, relative),
        outs,
        dp_index,
        list(inputs),
        list(grads),
        list(hidden),
        list(pre_grads),
        specs=[SMEM, [whole] * peers, [whole] * peers, [tiled] * peers, [tiled] * peers],
        out_specs=tuple(pl.BlockSpec(o.shape, lambda j: (0, 0, 0)) for o in outs),
        scratch=[pltpu.VMEM((width, tile), BF16), pltpu.VMEM((tile, width), BF16)],
        grid=(units // tile,),
        vmem=28,
        cost=8,
    )


def dense_grad_kernel(
    experts, stream, ua, dproj, attended, dat, uc, dgin, swish, dco, gate_grad1, gate1, col1, gate_grad2, gate2, col2,
    dp_index, probs, routers, pre, embedded, frames, kept, moved, dz, router_terms, logits, term, turned,
):
    width = ua.shape[1]
    count = 2 * kept.shape[0]
    part_rows = width // count

    def place(left, right, tile):
        turned[...] = left[...].T
        for column in range(right.shape[1] // width):
            term[...] = dot(turned[...], right[:, pl.ds(column * width, width)]).astype(BF16)
            for number in range(count):
                source = pl.multiple_of((dp_index[0] ^ number) * part_rows, part_rows)
                target = moved if number % 2 else kept
                target[number // 2, pl.ds((tile + column) * part_rows, part_rows), :] = term[pl.ds(source, part_rows), :]

    rows = frames.shape[0]
    stream.ready(0)
    stream.ready(1)
    place(ua, dproj, 0)
    place(attended, dat, 3)
    for ref in (kept, moved):
        stream.flush_rows(ref, 0, 4 * part_rows)
    stream.ready(2)
    for part in chunks(rows, 256):
        lane = iota((256, LANES), 1)
        grad = jnp.zeros((256, LANES), F32)
        for number, (gate_grad, gate, col) in enumerate(((gate_grad1, gate1, col1), (gate_grad2, gate2, col2))):
            inside = (lane >= number * experts) & (lane < (number + 1) * experts)
            hot = (lane == col[part, :] + number * experts).astype(F32)
            scale = gate_grad[part, :] * gate[part, :]
            grad = jnp.where(inside, scale * (hot - probs[part, :]), grad)
        logits[part, :] = grad
        demb = dot_nt(grad.astype(BF16), routers[...].astype(BF16))
        held = pre[part, :]
        dz[part, :] = (demb * slope(held, sigmoid(held))).astype(BF16)
    router_terms[...] = dot(logits[...].T.astype(BF16), embedded[...].astype(BF16))
    stream.flush(dz, router_terms)
    place(uc, dgin, 4)
    place(swish, dco, 6)
    place(frames, dz, 7)
    for ref in (kept, moved):
        stream.flush_rows(ref, 4 * part_rows, 4 * part_rows)


def sum_kernel(parts, out):
    total = parts[0][...].astype(F32)
    for part in parts[1:]:
        total = total + part[...].astype(F32)
    out[...] = total.astype(BF16)


def pair_kernel(kept, moved, *outs):
    for number, out in enumerate(outs):
        out[...] = (kept[number].astype(F32) + moved[number].astype(F32)).astype(BF16)


def experts_out_kernel(parts, second, in_out, out_out):
    _, _, in_rows, hidden = in_out.shape
    width = out_out.shape[3]
    half = out_out.shape[2]

    first = parts[0][...].astype(F32)
    for part in parts[1:]:
        first = first + part[...].astype(F32)
    for layer, values in ((0, first), (1, second[...].astype(F32))):
        out_out[layer, 0] = values[:half]
        for tile in range(hidden // width):
            rows = values[half + tile * in_rows : half + (tile + 1) * in_rows]
            in_out[layer, 0, :, tile * width : (tile + 1) * width] = rows


def dense_out_kernel(arrived, *outs):
    start = 0
    for out in outs:
        lanes = pl.ds(start, out.shape[1])
        total = arrived[0, :, lanes].astype(F32)
        for number in range(1, arrived.shape[0]):
            total = total + arrived[number, :, lanes].astype(F32)
        out[...] = total.astype(out.dtype)
        start += out.shape[1]


def embed_kernel(experts, ends, frames, weight, routers, col1, col2, pre_out, embedded_out, probs_out, gate1, gate2, seg_col, seg_row, taps_out, offset_out):
    rows = frames.shape[0]
    for part in chunks(rows, 256):
        pre = dot(frames[part, :], weight[...])
        pre_out[part, :] = pre
        embedded = pre * sigmoid(pre)
        embedded_out[part, :] = embedded
        logits = jnp.dot(embedded, routers[...], precision=HIGHEST, preferred_element_type=F32)
        lane = iota(logits.shape, 1)
        probs = jnp.zeros_like(logits)
        for number, (col, gate) in enumerate(((col1, gate1), (col2, gate2))):
            inside = (lane >= number * experts) & (lane < (number + 1) * experts)
            top = jnp.max(jnp.where(inside, logits, -MASK_FILL), 1, keepdims=True)
            weights = jnp.where(inside, jnp.exp(jnp.where(inside, logits - top, 0.0)), 0.0)
            own = weights / jnp.sum(weights, 1, keepdims=True)
            hot = lane == col[part, :] + number * experts
            gate[part, :] = jnp.sum(jnp.where(hot, own, 0.0), 1, keepdims=True)
            probs = probs + own
        probs_out[part, :] = probs

    def segment_of(place):
        found = jnp.zeros(place.shape, I32)
        for number in range(3):
            found += (place >= ends[number]).astype(I32)
        return found

    segment = segment_of(iota((rows, 1), 0))
    seg_col[...] = segment
    seg_row[...] = segment_of(iota((1, rows), 1))
    place = iota((rows, LANES), 0) + iota((rows, LANES), 1) - 7
    same = (segment_of(place) == segment) & (place >= 0) & (place < rows)
    taps_out[...] = same.astype(F32)
    first = jnp.zeros((rows, 1), I32)
    for number in range(3):
        first = jnp.where(segment > number, ends[number], first)
    offset_out[...] = (iota((rows, 1), 0) - first).astype(F32)


def partner(values):
    half = DH // 2
    lane = iota(values.shape, 1)
    return jnp.where(lane % DH < half, pltpu.roll(values, LANES - half, 1), pltpu.roll(values, half, 1))


def shifts(padded, part):
    size = part.size
    for offset in range(8):
        held = padded[pl.ds(part.start + offset, size + 8), :]
        if offset:
            yield offset - 1, held[:size]
        yield offset + 7, held[8:]


def folded(values):
    return jnp.sum(values.reshape(-1, 8, values.shape[1]), 0)


def front_kernel(
    stream, frames, blocks, slot_col, gate, table, attn_in, attn_out, conv_in, cosine, sine, seg_col, seg_row, taps,
    expert_out, x1_out, x2_out, ua_out, qkv_out, lse_out, attended_out, uc_out, gin_out, depth_out, moments,
    padded, flipped,
):
    rows, width = frames.shape
    gains = lambda n: table[pl.ds(n, 1), :]
    stream.ready(0)
    for part in chunks(rows, 256):
        found = gathered(slot_col, blocks, part)
        expert_out[part, :] = found.astype(BF16)
        x1 = frames[part, :].astype(F32) + 0.5 * gate[part, :] * found
        x1_out[part, :] = x1
        hat, _ = normalize(x1)
        ua_out[part, :] = (hat * gains(1)).astype(BF16)
    stream.flush(expert_out, x1_out, ua_out)
    stream.ready(1)
    for part in chunks(rows, 256):
        ua = ua_out[part, :]
        for piece in range(3 * width // LANES):
            lanes = pl.ds(piece * LANES, LANES)
            if piece % 2 == 0:
                pair = dot(ua, attn_in[:, pl.ds(piece * LANES, 2 * LANES)])
            values = pair[:, :LANES] if piece % 2 == 0 else pair[:, LANES:]
            if piece < 2 * width // LANES:
                values = values * cosine[part, :] + partner(values) * sine[part, :]
            if piece < width // LANES:
                values = values * DH**-0.5
            qkv_out[part, lanes] = values.astype(BF16)

    stream.flush(qkv_out)
    zero = jnp.zeros((), BF16)
    sides = tuple((iota((1, LANES), 1) < DH) == (side == 0) for side in range(2))
    turned = tuple((iota((LANES, 1), 0) < DH) == (side == 0) for side in range(2))
    for pair in range(width // LANES):
        flipped[pl.ds(pair * LANES, LANES), :] = qkv_out[:, pl.ds(2 * width + pair * LANES, LANES)].T

    def attend(part_index, carry):
        part = pl.ds(pl.multiple_of(part_index * 512, 512), 512)
        related = seg_col[...] == seg_row[:, part]
        for pair in range(width // LANES):
            q = qkv_out[part, pl.ds(pair * LANES, LANES)]
            k = qkv_out[:, pl.ds(width + pair * LANES, LANES)]
            v = flipped[pl.ds(pair * LANES, LANES), :]
            result = jnp.zeros((LANES, 512), F32)
            for side in range(2):
                scores = dot_nt(k, jnp.where(sides[side], q, zero))
                scores = jnp.where(related, scores, -MASK_FILL)
                top = jnp.max(scores, 0, keepdims=True)
                weights = jnp.exp(scores - top)
                summed = jnp.sum(weights, 0, keepdims=True)
                probs = (weights * (1.0 / summed)).astype(BF16)
                result += dot(jnp.where(turned[side], v, zero), probs)
                lse_out[pl.ds(2 * pair + side, 1), part] = top + jnp.log(summed)
            attended_out[part, pl.ds(pair * LANES, LANES)] = result.T.astype(BF16)
        return carry

    lax.fori_loop(0, rows // 512, attend, 0)
    stream.flush(attended_out, lse_out)
    stream.ready(2)

    edge = jnp.zeros((8, width), F32)
    padded[pl.ds(0, 8), :] = edge
    padded[pl.ds(rows + 8, 8), :] = edge
    for part in chunks(rows, 256):
        x2 = x1_out[part, :] + dot(attended_out[part, :], attn_out[...])
        x2_out[part, :] = x2
        hat, _ = normalize(x2)
        uc = (hat * gains(2)).astype(BF16)
        uc_out[part, :] = uc
        gin = dot(uc, conv_in[...])
        gin_out[part, :] = gin
        padded[pl.ds(part.start + 8, 256), :] = gin[:, :width] * sigmoid(gin[:, width:])

    stream.flush(x2_out, uc_out, gin_out)
    sums = jnp.zeros((1, width), F32)
    squares = jnp.zeros((1, width), F32)
    for part in chunks(rows, 64):
        depth = jnp.zeros((64, width), F32)
        for tap, shifted in shifts(padded, part):
            depth += table[pl.ds(6 + tap, 1), :] * shifted * taps[part, pl.ds(tap, 1)]
        depth_out[part, :] = depth
        weighted = jnp.where(seg_col[part, :] < 3, depth, 0.0)
        sums += jnp.sum(weighted, 0, keepdims=True)
        squares += jnp.sum(weighted * depth, 0, keepdims=True)
    moments[pl.ds(0, 1), :] = sums
    moments[pl.ds(1, 1), :] = squares
    moments[pl.ds(2, 6), :] = jnp.zeros((6, width), F32)
    stream.flush(depth_out, moments)


def batch_terms(moments, frame_count):
    mean = moments[pl.ds(0, 1), :] / frame_count[0]
    variance = moments[pl.ds(1, 1), :] / frame_count[0] - mean * mean
    return mean, lax.rsqrt(variance + EPSILON)


def middle_kernel(frame_count, depth, terms, x2, table, conv_out, slot_row, swish_out, x3_out, moments, sent, normed):
    rows, width = depth.shape
    moments[...] = total_of(terms)
    mean, scale = batch_terms(moments, frame_count)
    for part in chunks(rows, 256):
        bn = (depth[part, :] - mean) * scale * table[pl.ds(5, 1), :] + table[pl.ds(21, 1), :]
        swish = (bn * sigmoid(bn)).astype(BF16)
        swish_out[part, :] = swish
        x3 = x2[part, :] + dot(swish, conv_out[...])
        x3_out[part, :] = x3
        hat, _ = normalize(x3)
        normed[part, :] = (hat * table[pl.ds(3, 1), :]).astype(BF16)
    scatter_to(slot_row, normed[...], sent)


def turn_kernel(
    x3, blocks, slot_col, slot_row, gate, table, cotangent, seg_col,
    block_out, dx4_out, gate_grad, gain_out, sent, grads,
):
    rows, width = x3.shape
    gain = table[pl.ds(4, 1), :]
    gain_sum = jnp.zeros((1, width), F32)
    for part in chunks(rows, 256):
        found = gathered(slot_col, blocks, part)
        half = 0.5 * gate[part, :]
        x4 = x3[part, :] + half * found
        hat, inverse = normalize(x4)
        valid = seg_col[part, :] < 3
        block_out[part, :] = jnp.where(valid, hat * gain, 0.0).astype(BF16)
        grad = jnp.where(valid, cotangent[part, :].astype(F32), 0.0)
        gain_sum += jnp.sum(grad * hat, 0, keepdims=True)
        dx4 = norm_backward(grad, gain, hat, inverse)
        dx4_out[part, :] = dx4
        gate_grad[part, :] = 0.5 * jnp.sum(found * dx4, 1, keepdims=True)
        grads[part, :] = (half * dx4).astype(BF16)
    gain_out[...] = gain_sum
    scatter_to(slot_row, grads[...], sent)


def conv_back_kernel(
    frame_count, dx4, blocks, slot_col, x3, table, conv_out, depth, moments,
    dx3_out, dco_out, dh_out, sums,
):
    rows, width = x3.shape
    mean, scale = batch_terms(moments, frame_count)
    total = jnp.zeros((1, width), F32)
    moment = jnp.zeros((1, width), F32)
    shift = jnp.zeros((1, width), F32)
    gain5 = jnp.zeros((1, width), F32)
    gain3 = jnp.zeros((1, width), F32)
    for part in chunks(rows, 256):
        grad = gathered(slot_col, blocks, part)
        hat, inverse = normalize(x3[part, :])
        gain3 += jnp.sum(grad * hat, 0, keepdims=True)
        dx3 = dx4[part, :] + norm_backward(grad, table[pl.ds(3, 1), :], hat, inverse)
        dx3_out[part, :] = dx3
        dco = dx3.astype(BF16)
        dco_out[part, :] = dco
        centred = depth[part, :] - mean
        hat = centred * scale
        bn = hat * table[pl.ds(5, 1), :] + table[pl.ds(21, 1), :]
        dbn = dot_nt(dco, conv_out[...]) * slope(bn, sigmoid(bn))
        shift += jnp.sum(dbn, 0, keepdims=True)
        gain5 += jnp.sum(dbn * hat, 0, keepdims=True)
        dh = dbn * table[pl.ds(5, 1), :]
        dh_out[part, :] = dh
        total += jnp.sum(dh, 0, keepdims=True)
        moment += jnp.sum(dh * centred, 0, keepdims=True)
    for number, row in enumerate((total, moment, shift, gain5, gain3)):
        sums[pl.ds(number, 1), :] = row
    sums[pl.ds(5, 3), :] = jnp.zeros((3, width), F32)


def back_kernel(
    stream, frame_count, dh, depth, moments, sum_terms, dx3, gin, x2, x1, table, conv_in, attn_out, attn_in, qkv, attended, lse,
    cosine, sine, seg_col, seg_row, taps, expert, gate, slot_row,
    dgin_out, dat_out, dproj_out, dx1_out, gate_grad, terms, sent,
    padded, glu, grad_rows, dk, dv, rows_sent, flipped,
):
    rows, width = dh.shape
    mean, scale = batch_terms(moments, frame_count)
    sums = total_of(sum_terms)
    total, moment = sums[0:1], sums[1:2]
    var_grad = -0.5 * moment * scale * scale * scale
    mean_grad = -scale * total - 2.0 * mean * var_grad
    edge = jnp.zeros((8, width), F32)
    for ref in (padded, glu):
        ref[pl.ds(0, 8), :] = edge
        ref[pl.ds(rows + 8, 8), :] = edge
    stream.ready(0)
    for part in chunks(rows, 64):
        held = depth[part, :]
        grad = (mean_grad + 2.0 * held * var_grad) * (1.0 / frame_count[0])
        padded[pl.ds(part.start + 8, 64), :] = dh[part, :] * scale + jnp.where(seg_col[part, :] < 3, grad, 0.0)
    stream.ready(1)
    for part in chunks(rows, 64):
        glu[pl.ds(part.start + 8, 64), :] = gin[part, :width] * sigmoid(gin[part, width:])
    kernel_sums = [jnp.zeros((8, width), F32) for _ in range(15)]
    gain2 = jnp.zeros((1, width), F32)
    for part in chunks(rows, 64):
        dglu = jnp.zeros((64, width), F32)
        own = padded[pl.ds(part.start + 8, 64), :]
        for (tap, grad), (_, value) in zip(shifts(padded, part), shifts(glu, part)):
            mask = taps[part, pl.ds(tap, 1)]
            dglu += table[pl.ds(20 - tap, 1), :] * grad * mask
            kernel_sums[tap] += folded(own * value * mask)
        logistic = sigmoid(gin[part, width:])
        dgin_out[part, :width] = (dglu * logistic).astype(BF16)
        dgin_out[part, width:] = (dglu * gin[part, :width] * logistic * (1.0 - logistic)).astype(BF16)
    for tap in range(15):
        terms[pl.ds(6 + tap, 1), :] = jnp.sum(kernel_sums[tap], 0, keepdims=True)
    stream.flush(dgin_out)
    stream.ready(2)
    for part in chunks(rows, 256):
        grad = dot_nt(dgin_out[part, :], conv_in[...])
        hat, inverse = normalize(x2[part, :])
        gain2 += jnp.sum(grad * hat, 0, keepdims=True)
        dx2 = dx3[part, :] + norm_backward(grad, table[pl.ds(2, 1), :], hat, inverse)
        dx1_out[part, :] = dx2
        dat = dx2.astype(BF16)
        dat_out[part, :] = dat
        grad_rows[part, :] = dot_nt(dat, attn_out[...]).astype(BF16)
    terms[pl.ds(2, 1), :] = gain2

    stream.flush(dat_out)
    stream.ready(3)
    zero = jnp.zeros((), BF16)
    sides = tuple((iota((1, LANES), 1) < DH) == (side == 0) for side in range(2))
    turned = tuple((iota((LANES, 1), 0) < DH) == (side == 0) for side in range(2))
    for pair in range(width // LANES):
        flipped[pl.ds(pair * LANES, LANES), :] = qkv[:, pl.ds(width + pair * LANES, LANES)].T

    for pair in range(width // LANES):
        own = pl.ds(pair * LANES, LANES)
        q, da = qkv[:, own], grad_rows[:, own]
        products = (attended[:, own].astype(F32) * da.astype(F32)).T
        dq = jnp.zeros((LANES, rows), F32)
        for start in range(0, rows, 512):
            keys = pl.ds(start, 512)
            related = seg_col[keys, :] == seg_row[...]
            k = qkv[keys, pl.ds(width + pair * LANES, LANES)]
            v = qkv[keys, pl.ds(2 * width + pair * LANES, LANES)]
            dk_sum = jnp.zeros((512, LANES), F32)
            dv_sum = jnp.zeros((512, LANES), F32)
            for side in range(2):
                inner = jnp.sum(products[side * DH : (side + 1) * DH], 0, keepdims=True)
                q_side = jnp.where(sides[side], q, zero)
                da_side = jnp.where(sides[side], da, zero)
                scores = dot_nt(k, q_side) - lse[pl.ds(2 * pair + side, 1), :]
                probs = jnp.exp(jnp.where(related, scores, -MASK_FILL))
                dscores = (probs * (dot_nt(v, da_side) - inner)).astype(BF16)
                dq += dot(jnp.where(turned[side], flipped[own, keys], zero), dscores)
                dk_sum += dot(dscores, q_side)
                dv_sum += dot(probs.astype(BF16), da_side)
            dk[keys, own] = dk_sum
            dv[keys, own] = dv_sum
        dq = dq.T * DH**-0.5
        dproj_out[:, own] = (dq * cosine[...] - partner(dq) * sine[...]).astype(BF16)

    stream.ready(4)
    gain1 = jnp.zeros((1, width), F32)
    for part in chunks(rows, 256):
        for pair in range(width // LANES):
            own = pl.ds(pair * LANES, LANES)
            held = dk[part, own]
            dproj_out[part, pl.ds(width + pair * LANES, LANES)] = (
                held * cosine[part, :] - partner(held) * sine[part, :]
            ).astype(BF16)
            dproj_out[part, pl.ds(2 * width + pair * LANES, LANES)] = dv[part, own].astype(BF16)
        grad = dot_nt(dproj_out[part, :], attn_in[...])
        hat, inverse = normalize(x1[part, :])
        gain1 += jnp.sum(grad * hat, 0, keepdims=True)
        dx1 = dx1_out[part, :] + norm_backward(grad, table[pl.ds(1, 1), :], hat, inverse)
        dx1_out[part, :] = dx1
        gate_grad[part, :] = 0.5 * jnp.sum(expert[part, :].astype(F32) * dx1, 1, keepdims=True)
        rows_sent[part, :] = (0.5 * gate[part, :] * dx1).astype(BF16)
    terms[pl.ds(1, 1), :] = gain1
    stream.flush(dproj_out, dx1_out, gate_grad, terms)
    scatter_to(slot_row, rows_sent[...], sent)
    stream.flush(*sent)


def final_kernel(frames, blocks, slot_col, table, dx1, dz, embed_weight, _, out):
    for part in chunks(frames.shape[0], 128):
        grad = gathered(slot_col, blocks, part)
        hat, inverse = normalize(frames[part, :].astype(F32))
        dx0 = dx1[part, :] + norm_backward(grad, table[pl.ds(0, 1), :], hat, inverse)
        out[part, :] = dx0 + dot_nt(dz[part, :], embed_weight[...])


def after(value, *others):
    return lax.optimization_barrier((value,) + others)[0]


def shards(
    frames,
    lengths,
    choice_first,
    choice_second,
    embed_weight,
    routers,
    norm_gains,
    attn_in,
    attn_out,
    conv_in,
    conv_kernel,
    bn_shift,
    conv_out,
    expert_in,
    expert_out,
    cotangent,
):
    rows, width = frames.shape
    layers, slice_width, experts = routers.shape
    taps = conv_kernel.shape[0]
    gains = norm_gains.shape[0]
    peers = lax.axis_size("expert")
    dp_count = lax.axis_size("dp")
    dp_bits = bit_count(("dp",))
    capacity = 2 * rows // experts
    hidden = expert_in.shape[3]
    device = lax.axis_index(AXES)
    block = shaped((capacity, width), BF16)
    wide = shaped((rows, width), F32)
    low = shaped((rows, width), BF16)
    column = shaped((rows, 1), F32)

    dp_index = lax.axis_index("dp")[None]

    def shard_of(layer):
        first = expert_in[layer, 0]
        tiles = [first[:, start : start + width] for start in range(0, hidden, width)]
        return jnp.concatenate([expert_out[layer, 0]] + tiles, 0)

    first_weights = lax.all_gather(shard_of(0), "dp", axis=0)
    sent, slot_col1, slot_row1, slot_col2, slot_row2 = call(
        start_kernel,
        ([block] * peers, shaped((rows, 1), I32), shaped((1, rows), I32), shaped((rows, 1), I32), shaped((1, rows), I32)),
        lax.axis_index("expert")[None],
        frames,
        choice_first,
        choice_first.reshape(1, rows),
        choice_second,
        choice_second.reshape(1, rows),
        specs=[SMEM] + [None] * 5,
    )
    first_blocks = swap_blocks(sent)

    small_width = gains + taps + 1 + layers * experts
    small = jnp.concatenate(
        [
            norm_gains.T,
            conv_kernel.T,
            bn_shift[:, None],
            jnp.moveaxis(routers, 1, 0).reshape(slice_width, -1),
            jnp.zeros((slice_width, -small_width % LANES), BF16),
        ],
        1,
    )
    small = after(small, sent[0])
    small_all = gather_everywhere(small).reshape(width, LANES).astype(F32)
    table = small_all[:, : gains + taps + 3].T
    router_table = jnp.pad(
        small_all[:, gains + taps + 1 : small_width], ((0, 0), (0, LANES - layers * experts))
    )
    dense = jnp.concatenate([attn_in, attn_out, conv_in, conv_out], 1)
    dense = lax.all_to_all(
        jnp.broadcast_to(dense[None], (peers,) + dense.shape), "expert", split_axis=0, concat_axis=0, tiled=True
    )
    dense = lax.all_gather(
        dense.reshape(peers * slice_width, 7 * width), "dp", axis=0, tiled=True
    )
    second_weights = lax.all_gather(shard_of(1), "dp", axis=0)

    own_lengths = lax.dynamic_index_in_dim(lengths, device, 0, keepdims=False)
    frame_count = jnp.sum(lengths[:, :-1]).astype(F32)[None]
    (embed_pre, embedded, probs, gate1, gate2, seg_col, seg_row, tap_masks, offsets) = call(
        functools.partial(embed_kernel, experts),
        [
            wide,
            wide,
            shaped((rows, LANES), F32),
            column,
            column,
            shaped((rows, 1), I32),
            shaped((1, rows), I32),
            shaped((rows, LANES), F32),
            column,
        ],
        jnp.cumsum(own_lengths, dtype=I32)[:-1],
        frames,
        embed_weight,
        router_table,
        choice_first,
        choice_second,
        specs=[SMEM] + [None] * 5,
    )
    half = DH // 2
    frequency = 10000.0 ** (-jnp.arange(half, dtype=F32) / half)
    angles = offsets * jnp.tile(frequency, LANES // half)[None, :]
    sign = jnp.asarray(np.where(np.arange(LANES) % DH < half, -1.0, 1.0), F32)
    cosine, sine = jnp.cos(angles), jnp.sin(angles) * sign[None, :]

    def gain(number):
        return table[number : number + 1]

    first_results = swap_blocks(
        [expert_forward(block, gain(0), first_weights, hidden, True) for block in first_blocks]
    )

    def dense_spec(columns, start):
        return pl.BlockSpec((width, columns), lambda i: (0, start // columns))

    attn_in_spec = dense_spec(3 * width, 0)
    attn_out_spec = dense_spec(width, 3 * width)
    conv_in_spec = dense_spec(2 * width, 4 * width)
    conv_out_spec = dense_spec(width, 6 * width)
    sums_shape = shaped((8, width), F32)
    padded = pltpu.VMEM((rows + 16, width), F32)

    first_expert, x1, x2, ua, qkv, lse, attended, uc, gin, depth, moments = call(
        front_kernel,
        [
            low,
            wide,
            wide,
            low,
            shaped((rows, 3 * width), BF16),
            shaped((8, rows), F32),
            low,
            low,
            shaped((rows, 2 * width), F32),
            wide,
            sums_shape,
        ],
        frames,
        first_results,
        slot_col1,
        gate1,
        table,
        Columns(dense, 0, 3 * width),
        Columns(dense, 3 * width, width),
        Columns(dense, 4 * width, 2 * width),
        cosine,
        sine,
        seg_col,
        seg_row,
        tap_masks,
        stages=[0, 0, None, None, None, 1, 2, 2, 1, 1, None, None, 2],
        cost=20,
        scratch=[padded, pltpu.VMEM((width, rows), BF16)],
    )
    moment_terms = terms_everywhere(moments)
    swish, x3, moments, sent = call(
        middle_kernel,
        (low, wide, sums_shape, [block] * peers),
        frame_count,
        depth,
        moment_terms,
        x2,
        table,
        dense,
        slot_row2,
        specs=[SMEM] + [None] * 4 + [conv_out_spec, None],
        scratch=[pltpu.VMEM((rows, width), BF16)],
    )

    second_blocks = swap_blocks(sent)
    second_results = swap_blocks(
        [expert_forward(block, gain(3), second_weights, hidden, False) for block in second_blocks]
    )
    block_out, dx4, gate_grad2, gain4, sent = call(
        turn_kernel,
        (low, wide, column, shaped((1, width), F32), [block] * peers),
        x3,
        second_results,
        slot_col2,
        slot_row2,
        gate2,
        table,
        cotangent,
        seg_col,
        scratch=[pltpu.VMEM((rows, width), BF16)],
    )
    second_grads = swap_blocks(sent)
    backs = [
        expert_backward(block, grad, gain(3), second_weights, hidden, False)
        for block, grad in zip(second_blocks, second_grads)
    ]
    back, hid, pre_grads, inputs, _ = zip(*backs)
    second_back = swap_blocks(back)
    (second_grad,) = weight_grads(
        dp_index, inputs, second_grads, hid, pre_grads, dp_count, False
    )
    second_back[1] = after(second_back[1], second_grad)
    second_own = lax.psum_scatter(second_grad, "dp", scatter_dimension=0, tiled=True)[0]

    dx3, dco, dh, sums = call(
        conv_back_kernel,
        [wide, low, wide, sums_shape],
        frame_count,
        dx4,
        second_back,
        slot_col2,
        x3,
        table,
        dense,
        depth,
        moments,
        specs=[SMEM] + [None] * 5 + [conv_out_spec] + [None] * 2,
    )
    all_sums = terms_everywhere(sums)
    dgin, dat, dproj, dx1, gate_grad1, terms, sent = call(
        back_kernel,
        (
            shaped((rows, 2 * width), BF16),
            low,
            shaped((rows, 3 * width), BF16),
            wide,
            column,
            shaped((24, width), F32),
            [block] * peers,
        ),
        frame_count,
        dh,
        depth,
        moments,
        all_sums,
        dx3,
        gin,
        x2,
        x1,
        table,
        Columns(dense, 4 * width, 2 * width),
        Columns(dense, 3 * width, width),
        Columns(dense, 0, 3 * width),
        qkv,
        attended,
        lse,
        cosine,
        sine,
        seg_col,
        seg_row,
        tap_masks,
        first_expert,
        gate1,
        slot_row1,
        specs=[SMEM] + [None] * 23,
        stages=[None, 0, 0, None, None, 2, 1, 2, 4, None, 2, 2, 4, 3, 3, 3, 3, 3, None, None, 1, 4, None, None],
        cost=30,
        scratch=[padded, padded, pltpu.VMEM((rows, width), BF16), pltpu.VMEM((rows, width), F32), pltpu.VMEM((rows, width), F32), pltpu.VMEM((rows, width), BF16), pltpu.VMEM((width, rows), BF16)],
    )
    first_grads = swap_blocks(sent)

    def dp_exchange(values, mask):
        return lax.ppermute(values, "dp", [(i, i ^ mask) for i in range(dp_count)])

    dense_part = shaped((dp_count // 2, 8 * width // dp_count, width), BF16)
    kept, moved, dz, router_terms = call(
        functools.partial(dense_grad_kernel, experts),
        (dense_part, dense_part, low, shaped((LANES, width), F32)),
        ua,
        dproj,
        attended,
        dat,
        uc,
        dgin,
        swish,
        dco,
        gate_grad1,
        gate1,
        choice_first,
        gate_grad2,
        gate2,
        choice_second,
        dp_index,
        probs,
        router_table,
        embed_pre,
        embedded,
        frames,
        specs=[None] * 14 + [SMEM] + [None] * 5,
        stages=[0, 0, 1, 1, 2, 2, 2, 2] + [None] * 8 + [None, 2, 2, 2],
        cost=1,
        scratch=[pltpu.VMEM((rows, LANES), F32), pltpu.VMEM((width, width), BF16), pltpu.VMEM((width, rows), BF16)],
    )
    pairs = call(
        pair_kernel,
        [shaped(kept.shape[1:], BF16)] * (dp_count // 2),
        kept,
        dp_exchange(moved, 1),
        vmem=16,
        cost=10,
    )
    dense_own = call(
        sum_kernel,
        shaped(pairs[0].shape, BF16),
        [dp_exchange(pair, mask) if mask else pair for pair, mask in zip(pairs, chip_masks())],
        vmem=8,
        cost=60,
    )
    dense_own = dense_own.reshape(8, peers, slice_width, width).transpose(1, 2, 0, 3)
    backs = [
        expert_backward(block, grad, gain(0), first_weights, hidden, True)
        for block, grad in zip(first_blocks, first_grads)
    ]
    back, hid, pre_grads, inputs, gain0 = zip(*backs)
    gain0 = sum(gain0)
    first_back = swap_blocks(back)
    kept, moved = weight_grads(dp_index, inputs, first_grads, hid, pre_grads, dp_count, True)
    moved = after(moved, *first_back[1:])

    pairs = call(
        pair_kernel,
        [shaped(kept.shape[1:], BF16)] * (dp_count // 2),
        kept,
        dp_exchange(moved, 1),
        vmem=16,
        cost=20,
    )
    dense_own = after(dense_own, *pairs)
    dense_own = lax.all_to_all(
        dense_own.reshape(peers, slice_width, 8 * width), "expert", split_axis=0, concat_axis=0, tiled=True
    )
    first_parts = [
        dp_exchange(pair, mask) if mask else pair for pair, mask in zip(pairs, chip_masks())
    ]
    owned = [shaped((slice_width, count * width), F32) for count in (3, 1, 2, 1)]
    *dense_own, embed_own = call(
        dense_out_kernel,
        (*owned, shaped((slice_width, width), BF16)),
        dense_own,
        vmem=8,
        cost=10,
    )
    in_grad, out_grad = call(
        experts_out_kernel,
        (shaped((layers, 1, width // dp_count, hidden), F32), shaped((layers, 1, hidden // dp_count, width), F32)),
        first_parts,
        second_own,
        vmem=24,
        cost=10,
    )

    small_terms = jnp.concatenate(
        [
            gain0,
            terms[1:3],
            sums[4:5],
            gain4,
            sums[3:4],
            terms[6 : 6 + taps],
            sums[2:3],
            router_terms[: layers * experts],
        ],
        0,
    )
    small_terms = small_terms.T
    high = lax.reduce_precision(small_terms, 8, 7)
    split = jnp.concatenate([high, small_terms - high], 1).astype(BF16)
    split = jnp.pad(split, ((0, 0), (0, LANES - 2 * small_width))).reshape(-1, slice_width, LANES)
    mixed = jnp.concatenate([jnp.broadcast_to(embed_own[None], (split.shape[0],) + embed_own.shape), split], 2)
    mixed = lax.all_to_all(mixed, AXES, split_axis=0, concat_axis=0, tiled=True)
    embed_total = mixed[:, :, :width].reshape(width, width).astype(F32)
    small_sums = jnp.sum(mixed[:, :, width:].astype(F32), 0)
    small_sums = (small_sums[:, :small_width] + small_sums[:, small_width : 2 * small_width]).T

    frames_grad = call(
        final_kernel,
        wide,
        frames,
        first_back,
        slot_col1,
        table,
        dx1,
        dz,
        embed_weight,
        second_own,
        specs=[None] * 7 + [ANY],
        cost=40,
    )
    return (
        block_out,
        frames_grad,
        embed_total,
        jnp.moveaxis(
            small_sums[gains + taps + 1 : small_width].reshape(layers, experts, slice_width), 1, 2
        ),
        small_sums[:gains],
        *dense_own[:3],
        small_sums[gains : gains + taps],
        small_sums[gains + taps],
        dense_own[3],
        in_grad,
        out_grad,
    )


def solution(mesh):
    in_specs = (
        P(("dp", "expert"), None),
        P(),
        P(("dp", "expert"), None),
        P(("dp", "expert"), None),
        P(),
        P(None, ("dp", "expert"), None),
        P(None, ("dp", "expert")),
        P(("dp", "expert"), None),
        P(("dp", "expert"), None),
        P(("dp", "expert"), None),
        P(None, ("dp", "expert")),
        P(("dp", "expert")),
        P(("dp", "expert"), None),
        P(None, "expert", "dp", None),
        P(None, "expert", "dp", None),
        P(("dp", "expert"), None),
    )
    out_specs = (
        P(("dp", "expert"), None),
        P(("dp", "expert"), None),
        P(),
        P(None, ("dp", "expert"), None),
        P(None, ("dp", "expert")),
        P(("dp", "expert"), None),
        P(("dp", "expert"), None),
        P(("dp", "expert"), None),
        P(None, ("dp", "expert")),
        P(("dp", "expert")),
        P(("dp", "expert"), None),
        P(None, "expert", "dp", None),
        P(None, "expert", "dp", None),
    )
    return jax.shard_map(shards, mesh=mesh, in_specs=in_specs, out_specs=out_specs, check_vma=False)
```
